256 devices in a mesh: seq: 32 (over x, y, core), tp: 8 (over z).
Axes of the slice: x: 4, y: 4, z: 8, core: 2. Of those that a mesh axis runs over, the one named last changes fastest.
Arguments:
- teacher_query: bfloat16 [8192, 8192], P('seq', 'tp'), may hold values from -30 to 30
- teacher_key: bfloat16 [8192, 1024], P('seq', 'tp'), may hold values from -30 to 30
- teacher_value: bfloat16 [8192, 1024], P('seq', 'tp'), may hold values from -192 to 192
- t_segment: int32 [8192], P('seq'), may hold values from 0 to 2, never falling along the last dimension, each value on 1 to 6144 neighbouring positions
- s_hidden: bfloat16 [8192, 3584], P('seq'), may hold values from -80 to 80
- norm_gain: float32 [3584], replicated, may hold values from 0.5 to 1.5
- proj_weight: bfloat16 [3584, 8192], P('seq', 'tp'), may hold values from -0.09375 to 0.09375
- span_start: int32 [8192], P('seq'), may hold values from 0 to 8186, as said below
- span_count: int32 [8192], P('seq'), may hold values from 1 to 6
Outputs:
- grad_proj: float32 [3584, 8192], P('seq', 'tp')
- grad_hidden: float32 [8192, 3584], P('seq', 'tp')
The draws below stay inside these ranges and needn't reach their ends.
Inputs may be any that keep to these rules, and one draw needn't show every extreme that they name: For student token j, span_start[j] lies within 66 of j.
All inputs are finite; a program needn't handle non-finite values.
Results may differ from the reference program's by a relative error of at most 0.02.
Values may be sent and summed in bfloat16 or wider, within the bound.
A program may use at most 64 MiB of HBM per device.

```python
import math
import jax
import jax.numpy as jnp
import numpy as np
from jax import lax

D_S = 3584
QUERY_HEADS = 64
KEY_VALUE_HEADS = 8
HEAD_SIZE = 128
TEACHER_WIDTH = 8192
KV_W = 1024
TT_DEV = 256
TS_DEV = 256
SPAN = 6
DOCS = 3
TEACHER_TOKENS = 8192
TS = 8192
N_SEQ = 32


def key_base(key):
    return jnp.clip(jax.random.normal(jax.random.fold_in(key, 5), (TEACHER_TOKENS, KV_W), jnp.float32), -6.0, 6.0)


def draw_teacher_key(key, part):
    start_index = key_base(key)
    return start_index.astype(jnp.bfloat16)


def draw_teacher_query(key, part):
    key = jax.random.fold_in(key, 22)
    drawn = jnp.clip(jax.random.normal(key, (TEACHER_TOKENS, TEACHER_WIDTH), jnp.float32), -6.0, 6.0)
    return drawn.astype(jnp.bfloat16)


def draw_s_hidden(key, part):
    key = jax.random.fold_in(key, 31)
    noise = jnp.clip(jax.random.normal(jax.random.fold_in(key, 1), (TS, D_S), jnp.float32), -6.0, 6.0)
    low = jnp.log(0.3)
    high = jnp.log(3.0)
    row_scale = jnp.exp(jax.random.uniform(jax.random.fold_in(key, 2), (TS, 1), jnp.float32, low, high))
    col_scale = jnp.exp(jax.random.uniform(jax.random.fold_in(key, 3), (1, D_S), jnp.float32, low, high))
    return (noise * row_scale * col_scale).astype(jnp.bfloat16)


def span_pair(key):
    key = jax.random.fold_in(key, 41)
    tokens = jnp.arange(TS, dtype=jnp.int32)
    center = tokens * TEACHER_TOKENS // TS
    blocks = TS // TS_DEV
    reach = TT_DEV // 4
    wobble = jax.random.randint(jax.random.fold_in(key, 1), (blocks,), -reach, reach + 1)
    jitter = jax.random.randint(jax.random.fold_in(key, 2), (TS,), -2, 3)
    starts = jnp.clip(center + wobble[tokens // TS_DEV] + jitter, 0, TEACHER_TOKENS - SPAN)
    starts = jnp.where(tokens == 0, 0, jnp.where(tokens == TS - 1, TEACHER_TOKENS - SPAN, starts))
    counts = jax.random.randint(jax.random.fold_in(key, 3), (TS,), 1, SPAN + 1)
    counts = jnp.where(tokens == 0, SPAN, counts)
    return (starts.astype(jnp.int32), counts.astype(jnp.int32))


def draw_span_start(key, part):
    starts, counts = span_pair(key)
    return starts


def draw_span_count(key, part):
    starts, counts = span_pair(key)
    return counts


def shard_levels(stream_key, dims, pieces, least, top_value):
    def one(axis_at, blocks):
        heights = jax.random.uniform(jax.random.fold_in(jax.random.fold_in(stream_key, 6), axis_at), (blocks,), jnp.float32, least / len(pieces), top_value / len(pieces))
        return jnp.repeat(jnp.exp(heights), dims[axis_at] // blocks).reshape((-1,) + (1,) * (len(dims) - axis_at - 1))

    factor_of = one(*pieces[0])
    for cut in pieces[1:]:
        factor_of = factor_of * one(*cut)
    return factor_of


def profile(amount, total, bound, skew):
    weights = [(1 << 20) // math.isqrt(rank ** skew) + 1 for rank in range(2, amount + 1)]
    surplus, holding = total - bound - (amount - 1), [1] * (amount - 1)
    while surplus > 0:
        free = [i for i in range(amount - 1) if holding[i] < bound]
        whole, remaining = sum([weights[i] for i in free]), surplus
        for i in free:
            addition = min(bound - holding[i], max(1, remaining * weights[i] // whole), surplus)
            holding[i] = holding[i] + addition
            surplus = surplus - addition
    return np.array([bound] + holding)


def uneven(own_key, amount, total, limit, skew):
    if amount == 2:
        one = jax.random.randint(own_key, (), max(1, total - limit), min(limit, total - 1) + 1)
        return jnp.stack([one, total - one])
    tallies = jnp.asarray(profile(amount, total, limit, skew), jnp.int32)
    couples = (amount - 1) // 2
    donor, sink = tallies[1:1 + 2 * couples:2], tallies[2:2 + 2 * couples:2]
    room = jnp.minimum(donor - 1, limit - sink)
    moved = jax.random.randint(jax.random.fold_in(own_key, 1), (couples,), 0, 1 << 20) % (room + 1)
    tallies = tallies.at[1:1 + 2 * couples:2].set(donor - moved).at[2:2 + 2 * couples:2].set(sink + moved)
    return tallies[jax.random.permutation(jax.random.fold_in(own_key, 2), amount)]


def centred(stream_key, dims, scale, bound, split=(), held_as=jnp.bfloat16):
    values = jax.random.normal(stream_key, dims, jnp.float32) * scale
    if len(split) > 0:
        values = shard_levels(stream_key, dims, split, -0.22, 0.18) * values
    return jnp.clip(values, min=-bound, max=bound).astype(held_as)


def setup_inputs(seed: int = 0) -> dict:
    arg_keys = jax.random.split(jax.random.key(seed), 10)
    teacher_query = draw_teacher_query(jax.random.fold_in(arg_keys[9], 71), 0)
    teacher_key = draw_teacher_key(jax.random.fold_in(arg_keys[9], 71), 0)
    teacher_value = centred(arg_keys[2], (TEACHER_TOKENS, KV_W), 32.0, 192.0, ((0, 32), (1, 8)))
    t_segment = jnp.searchsorted(jnp.cumsum(uneven(arg_keys[3], DOCS, TEACHER_TOKENS, TEACHER_TOKENS * 3 // 4, 0)), jnp.arange(TEACHER_TOKENS), side="right").astype(jnp.int32)
    s_hidden = draw_s_hidden(jax.random.fold_in(arg_keys[9], 71), 0)
    norm_gain = jnp.clip(1.0 + 0.1 * jax.random.normal(arg_keys[5], (D_S,), jnp.float32), 0.5, 1.5)
    proj_weight = centred(arg_keys[6], (D_S, TEACHER_WIDTH), D_S ** -0.5, 0.09375, ((0, 32), (1, 8)))
    span_start = draw_span_start(jax.random.fold_in(arg_keys[9], 71), 0)
    span_count = draw_span_count(jax.random.fold_in(arg_keys[9], 71), 0)
    return {"teacher_query": teacher_query, "teacher_key": teacher_key, "teacher_value": teacher_value, "t_segment": t_segment, "s_hidden": s_hidden, "norm_gain": norm_gain, "proj_weight": proj_weight, "span_start": span_start, "span_count": span_count}


def teacher_attention(teacher_query, teacher_key, teacher_value, t_segment):
    head_groups = QUERY_HEADS // KEY_VALUE_HEADS
    current_block = math.gcd(TEACHER_TOKENS, 128)
    query_tiles = teacher_query.reshape(TEACHER_TOKENS // current_block, current_block, KEY_VALUE_HEADS, head_groups, HEAD_SIZE)
    every_key = teacher_key.reshape(TEACHER_TOKENS, KEY_VALUE_HEADS, HEAD_SIZE).astype(jnp.float32)
    every_value = teacher_value.reshape(TEACHER_TOKENS, KEY_VALUE_HEADS, HEAD_SIZE).astype(jnp.float32)
    positions = jnp.arange(TEACHER_TOKENS, dtype=jnp.int32)
    scale = 1.0 / math.sqrt(HEAD_SIZE)

    def one_block(packed):
        query_block, query_pos, query_doc = packed
        scores = jnp.einsum('qhgd,khd->hgqk', query_block.astype(jnp.float32), every_key) * scale
        allowed = (query_doc[:, None] == t_segment[None, :]) & (positions[None, :] <= query_pos[:, None])
        scores = jnp.where(allowed, scores, -1e+30)
        highest = lax.optimization_barrier(jnp.max(scores, axis=-1, keepdims=True))
        weights = jnp.where(allowed, jnp.exp(scores - highest), 0.0)
        totals = lax.optimization_barrier(jnp.sum(weights, axis=-1))
        rounded = lax.optimization_barrier(weights.astype(jnp.bfloat16)).astype(jnp.float32)
        numer = jnp.einsum('hgqk,khd->qhgd', rounded, every_value)
        return (numer / jnp.transpose(totals, (2, 0, 1))[..., None]).astype(jnp.bfloat16)
    outputs = lax.map(one_block, (query_tiles, positions.reshape(-1, current_block), t_segment.reshape(-1, current_block)))
    return outputs.reshape(TEACHER_TOKENS, TEACHER_WIDTH)

def reference(teacher_query, teacher_key, teacher_value, t_segment, s_hidden, norm_gain, proj_weight, span_start, span_count):
    teacher_out = teacher_attention(teacher_query, teacher_key, teacher_value, t_segment)
    summed = jnp.zeros((TS, TEACHER_WIDTH), jnp.float32)
    for offset in range(SPAN):
        index = jnp.minimum(span_start + offset, TEACHER_TOKENS - 1).astype(jnp.int32)
        rows = jnp.take(teacher_out, index, axis=0).astype(jnp.float32)
        summed = summed + jnp.where((offset < span_count)[:, None], rows, 0.0)
    target = summed / span_count.astype(jnp.float32)[:, None]
    hidden = s_hidden.astype(jnp.float32)
    scale = lax.rsqrt(lax.optimization_barrier(jnp.mean(hidden * hidden, axis=1, keepdims=True)) + 1e-06)
    normed = (hidden * scale * norm_gain).astype(jnp.bfloat16)
    prediction = jnp.dot(normed, proj_weight, preferred_element_type=jnp.float32)
    residual_grad = (prediction - target).astype(jnp.bfloat16)
    normed_groups = normed.reshape(N_SEQ, TS_DEV, D_S)
    grad_groups = residual_grad.reshape(N_SEQ, TS_DEV, TEACHER_WIDTH)

    def add_group(total, pair):
        left, right = pair
        part = jnp.dot(left.T, right, preferred_element_type=jnp.float32)
        part = lax.optimization_barrier(part.astype(jnp.bfloat16)).astype(jnp.float32)
        return (total + part, None)
    grad_proj, unused = lax.scan(add_group, jnp.zeros((D_S, TEACHER_WIDTH), jnp.float32), (normed_groups, grad_groups))
    normed_grad = jnp.dot(residual_grad, proj_weight.T, preferred_element_type=jnp.float32)
    scaled = normed_grad * norm_gain
    inner = lax.optimization_barrier(jnp.mean(scaled * hidden, axis=1, keepdims=True))
    grad_hidden = scale * scaled - hidden * scale ** 3 * inner
    return (grad_proj, grad_hidden)
```

```python
import math

import jax
import jax.numpy as jnp
from jax import lax
from jax.experimental import pallas as pl
from jax.experimental.pallas import tpu as pltpu
from jax.sharding import PartitionSpec as P

MESH = pl.DeviceIdType.MESH
F32, BF16 = jnp.float32, jnp.bfloat16
HEAD = 128
T = 256
WIDE = 3584
FEAT = 1024
BIG = float(2**20)
EXP_SCALE = math.log2(math.e) / math.sqrt(HEAD)
REACH = 12
HALO = 80
EVENTS = 176

NT = (((1,), (1,)), ((), ()))


def dot(a, b):
    return jnp.dot(a, b, preferred_element_type=F32)


def dot_nt(a, b):
    return lax.dot_general(a, b, NT, preferred_element_type=F32)


def kernel(
    q_ref, k_ref, v_ref, seg_ref, sh_ref, gain_ref, w_ref, start_ref, count_ref,
    gp_ref, gh_ref,
    kbuf, vbuf, kt_ref, wbuf, qa, m_ref, acc_ref, to_ref,
    normed, nt_ref, nsib, ht_ref, gt_ref, sc_ref, sct_ref, p_ref, r_ref, rsib,
    in_own, in_all, ngb, zrp, zrm,
    ga, gb, ra0p, ra0m, ra1p, ra1m, rb0p, rb0m, rb1p, rb1m,
    ha, hb, sa0p, sa0m, sa1p, sa1m, sb0p, sb0m, sb1p, sb1m,
    send_sems, recv_sems,
):
    i = lax.axis_index("seq")
    z = lax.axis_index("tp")
    c = lax.rem(i, 2)
    t = lax.div(i, 2)
    y = lax.rem(t, 4)
    x = lax.div(t, 4)
    oc = 1 - c

    def mod4(v):
        return lax.rem(v + 8, 4)

    def seq_dev(xx, yy, cc):
        return {"seq": (xx * 4 + yy) * 2 + cc}

    dev_x = {1: seq_dev(mod4(x + 1), y, c), -1: seq_dev(mod4(x - 1), y, c)}
    dev_y = {1: seq_dev(x, mod4(y + 1), c), -1: seq_dev(x, mod4(y - 1), c)}
    dev_z = {d: {"tp": lax.rem(z + d + 8, 8)} for d in (1, -1)}
    sib = seq_dev(x, y, oc)

    barrier = pltpu.get_barrier_semaphore()
    partners = [dev_x[1], dev_x[-1], dev_y[1], dev_y[-1], sib, {"seq": lax.rem(i + 2 * c + 31, 32)}]
    partners += [{"tp": lax.rem(z + d, 8)} for d in range(1, 8)]
    for device in partners:
        pl.semaphore_signal(barrier, inc=1, device_id=device, device_id_type=MESH)

    counter = [0]
    sent = []

    class Send:
        def __init__(self, src, dst, device, arrive=None):
            n = counter[0]
            counter[0] += 1
            self.parts = (n, device)
            self.copy = self.make(src, dst)
            self.copy.start()
            sent.append(self.copy)
            self.arrive = dst if arrive is None else arrive

        def make(self, src, dst):
            n, device = self.parts
            return pltpu.make_async_remote_copy(
                src_ref=src, dst_ref=dst, send_sem=send_sems.at[n], recv_sem=recv_sems.at[n],
                device_id=device, device_id_type=MESH,
            )

        def wait(self):
            self.make(self.arrive, self.arrive).wait_recv()

    def drain():
        for copy in sent:
            copy.wait_send()
        sent.clear()

    class Gather:
        def __init__(self, view, column, x_first):
            self.view, self.column_view, self.x_first = view, column, x_first
            self.dev_a, self.dev_b = (dev_x, dev_y) if x_first else (dev_y, dev_x)
            self.p2, self.f2, self.sibs = {}, {}, []

        def at(self, da, db, part=None):
            dx, dy = (da, db) if self.x_first else (db, da)
            return self.view(mod4(x + dx), mod4(y + dy), part)

        def to_a(self, sign, da, part=None):
            ref = self.at(da, 0, part)
            return Send(ref, ref, self.dev_a[sign], self.at(da - sign, 0, part))

        def to_b(self, sign, da, db, part=None):
            ref = self.at(da, db, part)
            return Send(ref, ref, self.dev_b[sign], self.at(da, db - sign, part))

        def to_sib(self, db):
            b = mod4((y if self.x_first else x) + db)
            ref = self.column_view(b, c)
            self.sibs.append(Send(ref, ref, sib, self.column_view(b, oc)))

        def stage0(self):
            self.p1 = {s: self.to_a(s, 0) for s in (1, -1)}
            for s in (1, -1):
                self.p2[s, 0] = self.to_b(s, 0, 0)

        def stage1(self):
            self.f1 = {}
            for s, part in ((1, 0), (-1, 1)):
                self.p1[s].wait()
                self.f1[s] = self.to_a(s, -s, part)
                for sb in (1, -1):
                    self.p2[sb, -s] = self.to_b(sb, -s, 0)
            self.forward(0)

        def forward(self, da):
            for s, part in ((1, 0), (-1, 1)):
                self.p2[s, da].wait()
                self.f2[s, da] = self.to_b(s, da, -s, part)

        def stage2(self):
            for s in (1, -1):
                self.f1[s].wait()
            for sb in (1, -1):
                self.p2[sb, 2] = self.to_b(sb, 2, 0)
            self.forward(-1)
            self.forward(1)
            self.to_sib(0)

        def stage3(self):
            self.forward(2)
            self.to_sib(-1)
            self.to_sib(1)

        def stage4(self):
            for key in self.f2:
                self.f2[key].wait()
            self.to_sib(2)

        def stage5(self, first=0):
            for s in self.sibs[first:]:
                s.wait()

    def k_view(xx, yy, part):
        return kbuf.at[xx, yy, c] if part is None else kbuf.at[xx, yy, c, pl.ds((0, 128)[part], (128, 144)[part])]

    def v_view(xx, yy, part):
        return vbuf.at[xx, yy, c] if part is None else vbuf.at[xx, yy, c, pl.ds(128 * part, 128)]

    def w_view(first):
        def view(xx, yy, part):
            if part is None:
                return wbuf.at[xx, yy, c, :, pl.ds(first, 512)]
            return wbuf.at[xx, yy, c, :, pl.ds(first + 256 * part, 256)]

        return view

    gather_k = Gather(k_view, lambda b, cc: kbuf.at[:, b, cc], True)
    gather_v = Gather(v_view, lambda b, cc: vbuf.at[b, :, cc], False)
    gather_w0 = Gather(w_view(0), lambda b, cc: wbuf.at[:, b, cc, :, pl.ds(0, 512)], True)
    gather_w1 = Gather(w_view(512), lambda b, cc: wbuf.at[b, :, cc, :, pl.ds(512, 512)], False)

    seg = seg_ref[...]
    below1 = jnp.sum((seg < 1).astype(F32), axis=1, keepdims=True)
    below2 = jnp.sum((seg < 2).astype(F32), axis=1, keepdims=True)
    strip_row = lax.broadcasted_iota(jnp.int32, (16, 128), 0)
    kbuf[x, y, c, 0:T, :] = k_ref[...]
    kbuf[x, y, c, T : T + 16, :] = jnp.where(strip_row < 8, below1, below2).astype(BF16)
    vbuf[x, y, c] = v_ref[...]
    wbuf[x, y, c] = w_ref[...]

    pl.semaphore_wait(barrier, len(partners))

    gather_k.stage0()
    gather_v.stage0()

    squares = jnp.zeros((T, 128), F32)
    for piece in range(WIDE // 128):
        h = sh_ref[:, piece * 128 : (piece + 1) * 128].astype(F32)
        squares = squares + h * h
    mean = jnp.sum(squares, axis=1, keepdims=True) * (1.0 / WIDE)
    scale = lax.rsqrt(mean + 1e-6)
    scale_wide = jnp.broadcast_to(scale, (T, 128))
    sc_ref[...] = scale_wide
    sct_ref[...] = jnp.transpose(scale_wide)[0:8, :]

    def norm_piece(piece, carry):
        cols = pl.ds(pl.multiple_of(piece * 896, 128), 896)
        h = sh_ref[:, cols]
        gain = jnp.concatenate([gain_ref[pl.ds(piece * 7 + n, 1), :] for n in range(7)], axis=1)
        value = (h.astype(F32) * sc_ref[:, 0:1] * gain).astype(BF16)
        normed[:, cols] = value
        nt_ref[piece] = jnp.transpose(value).reshape(4, 2, 112, T)

        @pl.when(piece == lax.div(z, 2))
        def _():
            ht_ref[...] = jnp.transpose(h)
            gt_ref[...] = jnp.transpose(jnp.broadcast_to(gain, (128, 896)))

        return carry

    lax.fori_loop(0, 4, norm_piece, 0)

    send_nt = Send(nt_ref.at[:, :, oc], nsib, sib)
    gather_k.stage1()
    gather_v.stage1()

    rows = lax.broadcasted_iota(jnp.int32, (T, 128), 0).astype(F32)
    lanes = lax.broadcasted_iota(jnp.int32, (T, 128), 1).astype(F32)

    def doc_of(n1, n2):
        return jnp.where(rows >= n1, 1.0, 0.0) + jnp.where(rows >= n2, 1.0, 0.0)

    one_hot = jnp.where(doc_of(below1, below2) == lanes, 1.0, 0.0).astype(BF16)
    for h in range(8):
        qa[h, :, 0:HEAD] = q_ref[:, h * HEAD : (h + 1) * HEAD]
        qa[h, :, HEAD : 2 * HEAD] = one_hot

    doc_id = lax.broadcasted_iota(jnp.int32, (HEAD, T), 0).astype(F32)
    key_id = lax.broadcasted_iota(jnp.int32, (HEAD, T), 1).astype(F32)

    def build_keys(tt):
        xx, yy = lax.div(tt, 4), lax.rem(tt, 4)
        for cc in range(2):
            at = slice(cc * T, (cc + 1) * T)
            strip = kbuf[xx, yy, cc, T : T + 16, :].astype(F32)
            doc = jnp.where(key_id >= strip[0:1, 0:1], 1.0, 0.0) + jnp.where(key_id >= strip[8:9, 0:1], 1.0, 0.0)
            kt_ref[tt, 0:HEAD, at] = jnp.transpose(kbuf[xx, yy, cc, 0:T, :])
            kt_ref[tt, HEAD : 2 * HEAD, at] = jnp.where(doc == doc_id, 0.0, -BIG).astype(BF16)

    ones = jnp.ones((2 * T, HEAD), BF16)

    def wide(v, n):
        return jnp.concatenate([v] * n, axis=1)

    def attend_chip(tt, own):
        xx, yy = lax.div(tt, 4), lax.rem(tt, 4)
        keys = kt_ref[tt]
        values = jnp.concatenate([jnp.concatenate([vbuf[xx, yy, 0], vbuf[xx, yy, 1]], axis=0), ones], axis=1)
        scores = {0: dot(qa[0], keys)}
        for h in range(8):
            if h < 7:
                scores[h + 1] = dot(qa[h + 1], keys)
            s = scores.pop(h)
            if own:
                row = lax.broadcasted_iota(jnp.int32, (T, 2 * T), 0)
                col = lax.broadcasted_iota(jnp.int32, (T, 2 * T), 1)
                s = jnp.where(col <= row + c * T, s, -2.0 * BIG)
                m = jnp.broadcast_to(jnp.max(s, axis=1, keepdims=True), (T, 128))
            else:
                m_old = m_ref[h]
                m = jnp.maximum(m_old, jnp.max(s, axis=1, keepdims=True))
            p = jnp.exp2(((s - wide(m, 4)) * EXP_SCALE).astype(BF16))
            m_ref[h] = m
            update = dot(p, values)
            if own:
                acc_ref[h] = update
            else:
                alpha = jnp.exp2((m_old - m) * EXP_SCALE)
                acc_ref[h] = acc_ref[h] * wide(alpha, 2) + update

    chips = jnp.minimum(t, REACH)

    def attend(quarter):
        def chip(tt, carry):
            attend_chip(tt, False)
            return carry

        low = t - chips + lax.div(chips * quarter, 4)
        high = t - chips + lax.div(chips * (quarter + 1), 4)
        lax.fori_loop(low, high, chip, 0)

    def finish():
        for h in range(8):
            acc = acc_ref[h]
            out = (acc[:, 0:HEAD] / acc[:, HEAD : 2 * HEAD]).astype(BF16)
            to_ref[128 : 128 + T, h * HEAD : (h + 1) * HEAD] = out
        last = Send(
            to_ref.at[pl.ds(128 + T - HALO, HALO)], to_ref.at[pl.ds(128 - HALO, HALO)],
            {"seq": lax.rem(i + 1, 32)},
        )
        first = Send(
            to_ref.at[pl.ds(128, HALO)], to_ref.at[pl.ds(128 + T, HALO)],
            {"seq": lax.rem(i + 31, 32)},
        )
        return [last, first]

    gather_k.stage2()
    gather_v.stage2()
    gather_k.stage3()
    gather_v.stage3()
    gather_w0.stage0()
    gather_w1.stage0()
    gather_k.sibs[0].wait()
    gather_v.sibs[0].wait()
    build_keys(t)
    attend_chip(t, True)

    def column(ref):
        return jnp.transpose(jnp.broadcast_to(ref[...].astype(F32), (128, T)))

    to_ref[0 : 128 - HALO, :] = jnp.zeros((128 - HALO, FEAT), BF16)
    to_ref[128 + T + HALO : 512, :] = jnp.zeros((128 - HALO, FEAT), BF16)
    span_start = column(start_ref)
    span_count = column(count_ref)
    inverse_count = 1.0 / span_count
    first_row = (i * T - 128).astype(F32)
    row_id = lax.broadcasted_iota(jnp.int32, (T, 512), 1).astype(F32) + first_row
    begin, end = wide(span_start, 4), wide(span_start + span_count, 4)
    select = jnp.where((row_id >= begin) & (row_id < end), 1.0, 0.0).astype(BF16)

    gather_k.stage4()
    gather_v.stage4()
    gather_k.stage5(1)
    gather_v.stage5(1)

    def keys_chip(tt, carry):
        build_keys(tt)
        return carry

    lax.fori_loop(t - chips, t, keys_chip, 0)

    attend(0)
    gather_w0.stage1()
    gather_w1.stage1()
    attend(1)
    gather_w0.stage2()
    gather_w1.stage2()
    attend(2)
    gather_w0.stage3()
    gather_w1.stage3()
    attend(3)
    halos = finish()
    gather_w0.stage4()
    gather_w1.stage4()
    gather_w0.stage5()
    gather_w1.stage5()

    def predict(piece, carry):
        cols = pl.ds(pl.multiple_of(piece * 256, 256), 256)
        total = jnp.zeros((T, 256), F32)
        for xx in range(4):
            total = total + dot(normed[:, xx * 896 : (xx + 1) * 896], wbuf[xx, :, :, :, cols].reshape(896, 256))
        p_ref[:, cols] = total
        return carry

    lax.fori_loop(0, 4, predict, 0)
    for s in halos:
        s.wait()

    inner = jnp.zeros((T, 128), F32)
    for piece in range(4):
        cols = slice(piece * 256, (piece + 1) * 256)
        target = dot(select, to_ref[:, cols]) * wide(inverse_count, 2)
        prediction = p_ref[:, cols]
        residual = (prediction - target).astype(BF16)
        r_ref[:, cols] = residual
        product = residual.astype(F32) * prediction
        inner = inner + product[:, 0:128] + product[:, 128:256]
    send_r = Send(r_ref, rsib, sib)
    inner = jnp.broadcast_to(jnp.sum(inner, axis=1, keepdims=True), (T, 128))
    in_own[...] = jnp.transpose(inner)[0:8, :]
    inners = [Send(in_own, in_all.at[d], {"tp": lax.rem(z + d, 8)}) for d in range(1, 8)]

    def normed_grad(d):
        zz = lax.rem(z + d, 8)
        w = wbuf[lax.div(zz, 2), pl.ds(lax.rem(zz, 2) * 2, 2)].reshape(448, FEAT)
        ngb[d] = dot_nt(w, r_ref[...]).astype(BF16)

    lo, hi = pl.ds(0, 224), pl.ds(224, 224)

    def z_send(step, sign, rows_):
        d = (4 - step if sign == 1 else 4 + step)
        box = zrp if sign == 1 else zrm
        return Send(ngb.at[d, rows_], box.at[step, rows_], dev_z[sign])

    def z_add(step, sign, rows_):
        d = (3 - step if sign == 1 else 5 + step)
        box = zrp if sign == 1 else zrm
        ngb[d, rows_] = (ngb[d, rows_].astype(F32) + box[step, rows_].astype(F32)).astype(BF16)

    normed_grad(4)
    z0p, z0m = z_send(0, 1, lo), z_send(0, -1, hi)

    send_nt.wait()
    send_r.wait()

    def grad_a(d):
        yy = mod4(y + d)
        left = nt_ref[:, yy, c].reshape(448, T)
        left_sib = nsib[:, yy].reshape(448, T)
        block = dot(left, r_ref[:, 0:512]) + dot(left_sib, rsib[:, 0:512])
        ga[d] = block.astype(BF16).reshape(4, 112, 512)

    def grad_b(d):
        xx = mod4(x + d)
        left = nt_ref[xx, :, c].reshape(448, T)
        left_sib = nsib[xx].reshape(448, T)
        block = dot(left, r_ref[:, 512:1024]) + dot(left_sib, rsib[:, 512:1024])
        gb[d] = block.astype(BF16).reshape(4, 112, 512)

    two, four = pl.ds(0, 2), pl.ds(2, 2)

    class Scatter:
        def __init__(self, g, r0p, r0m, r1p, r1m, h, s0p, s0m, s1p, s1m, dev_a, dev_b, b):
            self.g, self.r0, self.r1, self.h = g, {1: r0p, -1: r0m}, {1: r1p, -1: r1m}, h
            self.s0, self.s1 = {1: s0p, -1: s0m}, {1: s1p, -1: s1m}
            self.dev_a, self.dev_b, self.b = dev_a, dev_b, b
            self.part = {1: two, -1: four}
            self.cols = {1: pl.ds(0, 256), -1: pl.ds(256, 256)}

        def first(self):
            self.e0 = {s: Send(self.g.at[2, self.part[s]], self.r0[s], self.dev_a[s]) for s in (1, -1)}

        def second(self):
            self.e1 = {}
            for s, d in ((1, 1), (-1, 3)):
                part = self.part[-s]
                self.e1[s] = [Send(self.g.at[d, part], self.r1[s].at[part], self.dev_a[s])]

        def third(self):
            for s, d in ((1, 1), (-1, 3)):
                part = self.part[s]
                self.e0[s].wait()
                self.g[d, part] = (self.g[d, part].astype(F32) + self.r0[s][...].astype(F32)).astype(BF16)
                self.e1[s].append(Send(self.g.at[d, part], self.r1[s].at[part], self.dev_a[s]))

        def fourth(self):
            for s in (1, -1):
                for e in self.e1[s]:
                    e.wait()
            self.h[...] = (
                self.g[0].astype(F32) + self.r1[1][...].astype(F32) + self.r1[-1][...].astype(F32)
            ).astype(BF16)
            far = mod4(self.b + 2)
            self.f0, self.f1 = {}, {}
            for s in (1, -1):
                self.f0[s] = Send(self.h.at[far, :, self.cols[s]], self.s0[s], self.dev_b[s])
            for s in (1, -1):
                cols = self.cols[-s]
                self.f1[s] = [Send(self.h.at[mod4(self.b + s), :, cols], self.s1[s].at[:, cols], self.dev_b[s])]

        def fifth(self):
            for s in (1, -1):
                cols, near = self.cols[s], mod4(self.b + s)
                self.f0[s].wait()
                self.h[near, :, cols] = (
                    self.h[near, :, cols].astype(F32) + self.s0[s][...].astype(F32)
                ).astype(BF16)
                self.f1[s].append(Send(self.h.at[near, :, cols], self.s1[s].at[:, cols], self.dev_b[s]))

        def result(self):
            for s in (1, -1):
                for e in self.f1[s]:
                    e.wait()
            return self.h[self.b].astype(F32) + self.s1[1][...].astype(F32) + self.s1[-1][...].astype(F32)

    scatter_a = Scatter(ga, ra0p, ra0m, ra1p, ra1m, ha, sa0p, sa0m, sa1p, sa1m, dev_y, dev_x, x)
    scatter_b = Scatter(gb, rb0p, rb0m, rb1p, rb1m, hb, sb0p, sb0m, sb1p, sb1m, dev_x, dev_y, y)

    grad_a(2)
    grad_b(2)
    scatter_a.first()
    scatter_b.first()
    grad_a(1)
    grad_a(3)
    scatter_a.second()
    grad_b(1)
    grad_b(3)
    scatter_b.second()
    normed_grad(3)
    z1p = [z_send(1, 1, hi)]
    normed_grad(5)
    z1m = [z_send(1, -1, lo)]
    z0p.wait()
    z_add(0, 1, lo)
    z1p.append(z_send(1, 1, lo))
    z0m.wait()
    z_add(0, -1, hi)
    z1m.append(z_send(1, -1, hi))
    normed_grad(2)
    normed_grad(6)
    scatter_a.third()
    scatter_b.third()

    def z_pass(step, plus, minus):
        out_p, out_m = [], []
        for n in range(2):
            rows_p, rows_m = (hi, lo)[n], (lo, hi)[n]
            plus[n].wait()
            z_add(step, 1, rows_p)
            out_p.append(z_send(step + 1, 1, rows_p))
            minus[n].wait()
            z_add(step, -1, rows_m)
            out_m.append(z_send(step + 1, -1, rows_m))
        return out_p, out_m

    z2p, z2m = z_pass(1, z1p, z1m)
    normed_grad(1)
    normed_grad(7)
    normed_grad(0)
    grad_a(0)
    grad_b(0)
    z3p, z3m = z_pass(2, z2p, z2m)
    scatter_a.fourth()
    scatter_b.fourth()
    scatter_a.fifth()
    scatter_b.fifth()

    total_inner = in_own[0:1, :]
    for d, e in enumerate(inners):
        e.wait()
        total_inner = total_inner + in_all[d + 1, 0:1, :]
    scale_row = sct_ref[0:1, :]
    factor = total_inner * scale_row * scale_row * (1.0 / WIDE)
    for e in z3p + z3m:
        e.wait()
    mine = pl.ds(lax.rem(z, 2) * 448, 448)
    ng = ngb[0].astype(F32) + zrp[3].astype(F32) + zrm[3].astype(F32)
    u = ng * wide(gt_ref[mine, :], 2)
    gh_ref[...] = u * scale_row - ht_ref[mine, :].astype(F32) * factor

    gp_ref[:, 0:512] = scatter_a.result()
    gp_ref[:, 512:1024] = scatter_b.result()
    drain()


def deliver(gp_in, gh_in, gp_out, gh_out, sems):
    copies = [pltpu.make_async_copy(gp_in, gp_out, sems.at[0]), pltpu.make_async_copy(gh_in, gh_out, sems.at[1])]
    for copy in copies:
        copy.start()
    for copy in copies:
        copy.wait()


def vm(shape, dtype=BF16):
    return pltpu.VMEM(shape, dtype)


def body(teacher_query, teacher_key, teacher_value, t_segment, s_hidden, norm_gain, proj_weight, span_start, span_count):
    spec = pl.BlockSpec(memory_space=pltpu.VMEM)
    scratch = [
        vm((4, 4, 2, T + 16, 128)),
        vm((4, 4, 2, T, 128)),
        vm((16, 2 * HEAD, 2 * T)),
        vm((4, 4, 2, 112, FEAT)),
        vm((8, T, 2 * HEAD)),
        vm((8, T, 128), F32),
        vm((8, T, 2 * HEAD), F32),
        vm((512, FEAT)),
        vm((T, WIDE)),
        vm((4, 4, 2, 112, T)),
        vm((4, 4, 112, T)),
        vm((896, T)),
        vm((896, 128), F32),
        vm((T, 128), F32),
        vm((8, T), F32),
        vm((T, FEAT), F32),
        vm((T, FEAT)),
        vm((T, FEAT)),
        vm((8, T), F32),
        vm((8, 8, T), F32),
        vm((8, 448, T)),
        vm((4, 448, T)),
        vm((4, 448, T)),
        vm((4, 4, 112, 512)),
        vm((4, 4, 112, 512)),
    ]
    scratch += [vm((2, 112, 512)), vm((2, 112, 512)), vm((4, 112, 512)), vm((4, 112, 512))] * 2
    scratch += [vm((4, 112, 512))] * 2
    scratch += [vm((112, 256)), vm((112, 256)), vm((112, 512)), vm((112, 512))] * 2
    scratch += [pltpu.SemaphoreType.DMA((EVENTS,)), pltpu.SemaphoreType.DMA((EVENTS,))]
    grad_proj, grad_hidden = pl.pallas_call(
        kernel,
        out_shape=(jax.ShapeDtypeStruct((112, FEAT), F32), jax.ShapeDtypeStruct((448, T), F32)),
        in_specs=[spec] * 9,
        out_specs=(spec, spec),
        scratch_shapes=scratch,
        compiler_params=pltpu.CompilerParams(
            collective_id=0, has_side_effects=True, vmem_limit_bytes=60 * 2**20
        ),
    )(
        teacher_query, teacher_key, teacher_value, t_segment.reshape(1, T), s_hidden,
        norm_gain.reshape(28, 128), proj_weight, span_start.reshape(1, T), span_count.reshape(1, T),
    )
    anywhere = pl.BlockSpec(memory_space=pl.ANY)
    grad_proj, grad_hidden = pl.pallas_call(
        deliver,
        out_shape=(jax.ShapeDtypeStruct((112, FEAT), F32), jax.ShapeDtypeStruct((448, T), F32)),
        in_specs=[anywhere] * 2,
        out_specs=(anywhere, anywhere),
        scratch_shapes=[pltpu.SemaphoreType.DMA((2,))],
        compiler_params=pltpu.CompilerParams(vmem_limit_bytes=60 * 2**20),
    )(grad_proj, grad_hidden)
    return grad_proj, grad_hidden.T


def solution(mesh):
    return jax.shard_map(
        body,
        mesh=mesh,
        in_specs=(
            P("seq", "tp"),
            P("seq", "tp"),
            P("seq", "tp"),
            P("seq"),
            P("seq", None),
            P(),
            P("seq", "tp"),
            P("seq"),
            P("seq"),
        ),
        out_specs=(P("seq", "tp"), P("seq", "tp")),
        check_vma=False,
    )
```

```python
import math

import jax
import jax.numpy as jnp
from jax import lax
from jax.experimental import pallas as pl
from jax.experimental.pallas import tpu as pltpu
from jax.sharding import PartitionSpec as P

MESH = pl.DeviceIdType.MESH
F32, BF16 = jnp.float32, jnp.bfloat16
HEAD = 128
T = 256
WIDE = 3584
FEAT = 1024
BIG = float(2**20)
EXP_SCALE = math.log2(math.e) / math.sqrt(HEAD)
REACH = 12
HALO = 80
EVENTS = 176

NT = (((1,), (1,)), ((), ()))


def dot(a, b):
    return jnp.dot(a, b, preferred_element_type=F32)


def dot_nt(a, b):
    return lax.dot_general(a, b, NT, preferred_element_type=F32)


def kernel(
    q_ref, k_ref, v_ref, seg_ref, sh_ref, gain_ref, w_ref, start_ref, count_ref,
    gp_ref, gh_ref,
    kvbuf, kt_ref, wbuf, qa, m_ref, acc_ref, s_ref, pa_ref, pb_ref, to_ref,
    normed, nt_ref, nsib, ht_ref, gt_ref, sc_ref, sct_ref, p_ref, r_ref, rsib,
    in_own, in_all, ngb, zrp, zrm,
    ga, gb, ra0p, ra0m, ra1p, ra1m, rb0p, rb0m, rb1p, rb1m,
    ha, hb, sa0p, sa0m, sa1p, sa1m, sb0p, sb0m, sb1p, sb1m,
    send_sems, recv_sems,
):
    i = lax.axis_index("seq")
    z = lax.axis_index("tp")
    c = lax.rem(i, 2)
    t = lax.div(i, 2)
    y = lax.rem(t, 4)
    x = lax.div(t, 4)
    oc = 1 - c

    def mod4(v):
        return lax.rem(v + 8, 4)

    def seq_dev(xx, yy, cc):
        return {"seq": (xx * 4 + yy) * 2 + cc}

    dev_x = {1: seq_dev(mod4(x + 1), y, c), -1: seq_dev(mod4(x - 1), y, c)}
    dev_y = {1: seq_dev(x, mod4(y + 1), c), -1: seq_dev(x, mod4(y - 1), c)}
    dev_z = {d: {"tp": lax.rem(z + d + 8, 8)} for d in (1, -1)}
    sib = seq_dev(x, y, oc)

    barrier = pltpu.get_barrier_semaphore()
    partners = [dev_x[1], dev_x[-1], dev_y[1], dev_y[-1], sib, {"seq": lax.rem(i + 2 * c + 31, 32)}]
    partners += [{"tp": lax.rem(z + d, 8)} for d in range(1, 8)]
    for device in partners:
        pl.semaphore_signal(barrier, inc=1, device_id=device, device_id_type=MESH)

    counter = [0]
    sent = []

    class Send:
        def __init__(self, src, dst, device, arrive=None):
            n = counter[0]
            counter[0] += 1
            self.parts = (n, device)
            self.copy = self.make(src, dst)
            self.copy.start()
            sent.append(self.copy)
            self.arrive = dst if arrive is None else arrive

        def make(self, src, dst):
            n, device = self.parts
            return pltpu.make_async_remote_copy(
                src_ref=src, dst_ref=dst, send_sem=send_sems.at[n], recv_sem=recv_sems.at[n],
                device_id=device, device_id_type=MESH,
            )

        def wait(self):
            self.make(self.arrive, self.arrive).wait_recv()

    def drain():
        for copy in sent:
            copy.wait_send()
        sent.clear()

    class Gather:
        def __init__(self, view, column, a, b, sib_b, dev_a, dev_b):
            self.view, self.column = view, column
            self.a, self.b, self.sib_b, self.dev_a, self.dev_b = a, b, sib_b, dev_a, dev_b
            self.p2, self.f2, self.sibs = {}, {}, []

        def at(self, da, db, part=None):
            return self.view(mod4(self.a + da), mod4(self.b + db), part)

        def to_a(self, sign, da, part=None):
            ref = self.at(da, 0, part)
            return Send(ref, ref, self.dev_a[sign], self.at(da - sign, 0, part))

        def to_b(self, sign, da, db, part=None):
            ref = self.at(da, db, part)
            return Send(ref, ref, self.dev_b[sign], self.at(da, db - sign, part))

        def to_sib(self, db):
            ref = self.column(mod4(self.b + db), c)
            self.sibs.append(Send(ref, ref, sib, self.column(mod4(self.sib_b + db), oc)))

        def stage0(self):
            self.p1 = {s: self.to_a(s, 0) for s in (1, -1)}
            for s in (1, -1):
                self.p2[s, 0] = self.to_b(s, 0, 0)

        def stage1(self):
            self.f1 = {}
            for s, part in ((1, 0), (-1, 1)):
                self.p1[s].wait()
                self.f1[s] = self.to_a(s, -s, part)
                for sb in (1, -1):
                    self.p2[sb, -s] = self.to_b(sb, -s, 0)
            self.forward(0)

        def forward(self, da):
            for s, part in ((1, 0), (-1, 1)):
                self.p2[s, da].wait()
                self.f2[s, da] = self.to_b(s, da, -s, part)

        def stage2(self):
            for s in (1, -1):
                self.f1[s].wait()
            for sb in (1, -1):
                self.p2[sb, 2] = self.to_b(sb, 2, 0)
            self.forward(-1)
            self.forward(1)
            self.to_sib(0)

        def stage3(self):
            self.forward(2)
            self.to_sib(-1)
            self.to_sib(1)

        def stage4(self):
            for key in self.f2:
                self.f2[key].wait()
            self.to_sib(2)

        def stage5(self, first=0):
            for s in self.sibs[first:]:
                s.wait()

    def kv_view(aa, bb, part):
        if part is None:
            return kvbuf.at[c, aa, bb]
        return kvbuf.at[c, aa, bb, pl.ds((0, 128)[part], (128, 144)[part])]

    def w_view(first, x_first):
        def view(aa, bb, part):
            xx, yy = (aa, bb) if x_first else (bb, aa)
            if part is None:
                return wbuf.at[xx, yy, c, :, pl.ds(first, 512)]
            return wbuf.at[xx, yy, c, :, pl.ds(first + 256 * part, 256)]

        return view

    kv_a, kv_b = oc * x + c * y, oc * y + c * x
    step_a = {d: seq_dev(mod4(x + d * oc), mod4(y + d * c), c) for d in (1, -1)}
    step_b = {d: seq_dev(mod4(x + d * c), mod4(y + d * oc), c) for d in (1, -1)}
    gather_kv = Gather(kv_view, lambda bb, cc: kvbuf.at[cc, :, bb], kv_a, kv_b, kv_a, step_a, step_b)
    gather_w0 = Gather(w_view(0, True), lambda bb, cc: wbuf.at[:, bb, cc, :, pl.ds(0, 512)], x, y, y, dev_x, dev_y)
    gather_w1 = Gather(w_view(512, False), lambda bb, cc: wbuf.at[bb, :, cc, :, pl.ds(512, 512)], y, x, x, dev_y, dev_x)

    seg = seg_ref[...]
    below1 = jnp.sum((seg < 1).astype(F32), axis=1, keepdims=True)
    below2 = jnp.sum((seg < 2).astype(F32), axis=1, keepdims=True)
    strip_row = lax.broadcasted_iota(jnp.int32, (16, 128), 0)
    kvbuf[c, kv_a, kv_b, 0:T, 0:HEAD] = k_ref[...]
    kvbuf[c, kv_a, kv_b, 0:T, HEAD : 2 * HEAD] = v_ref[...]
    strip = jnp.where(strip_row < 8, below1, below2).astype(BF16)
    kvbuf[c, kv_a, kv_b, T : T + 16, :] = jnp.concatenate([strip, strip], axis=1)
    wbuf[x, y, c] = w_ref[...]

    pl.semaphore_wait(barrier, len(partners))

    gather_kv.stage0()

    squares = jnp.zeros((T, 128), F32)
    for piece in range(WIDE // 128):
        h = sh_ref[:, piece * 128 : (piece + 1) * 128].astype(F32)
        squares = squares + h * h
    mean = jnp.sum(squares, axis=1, keepdims=True) * (1.0 / WIDE)
    scale = lax.rsqrt(mean + 1e-6)
    scale_wide = jnp.broadcast_to(scale, (T, 128))
    sc_ref[...] = scale_wide
    sct_ref[...] = jnp.transpose(scale_wide)[0:8, :]

    def norm_piece(piece, carry):
        cols = pl.ds(pl.multiple_of(piece * 896, 128), 896)
        h = sh_ref[:, cols]
        gain = jnp.concatenate([gain_ref[pl.ds(piece * 7 + n, 1), :] for n in range(7)], axis=1)
        value = (h.astype(F32) * sc_ref[:, 0:1] * gain).astype(BF16)
        normed[:, cols] = value
        nt_ref[piece] = jnp.transpose(value).reshape(4, 2, 112, T)

        @pl.when(piece == lax.div(z, 2))
        def _():
            ht_ref[...] = jnp.transpose(h)
            gt_ref[...] = jnp.transpose(jnp.broadcast_to(gain, (128, 896)))

        return carry

    lax.fori_loop(0, 1, norm_piece, 0)
    gather_kv.stage1()
    lax.fori_loop(1, 3, norm_piece, 0)
    gather_kv.stage2()
    lax.fori_loop(3, 4, norm_piece, 0)
    send_nt = Send(nt_ref.at[:, :, oc], nsib, sib)

    rows = lax.broadcasted_iota(jnp.int32, (T, 128), 0).astype(F32)
    lanes = lax.broadcasted_iota(jnp.int32, (T, 128), 1).astype(F32)

    def doc_of(n1, n2):
        return jnp.where(rows >= n1, 1.0, 0.0) + jnp.where(rows >= n2, 1.0, 0.0)

    one_hot = jnp.where(doc_of(below1, below2) == lanes, 1.0, 0.0).astype(BF16)
    for h in range(8):
        at = pl.ds((h % 4) * T, T)
        qa[h // 4, at, 0:HEAD] = q_ref[:, h * HEAD : (h + 1) * HEAD]
        qa[h // 4, at, HEAD : 2 * HEAD] = one_hot

    doc_id = lax.broadcasted_iota(jnp.int32, (HEAD, T), 0).astype(F32)
    key_id = lax.broadcasted_iota(jnp.int32, (HEAD, T), 1).astype(F32)

    def blocks(tt):
        xx, yy = lax.div(tt, 4), lax.rem(tt, 4)
        return kvbuf.at[0, xx, yy], kvbuf.at[1, yy, xx]

    def build_keys(tt):
        for cc, block in enumerate(blocks(tt)):
            at = slice(cc * T, (cc + 1) * T)
            strip = block[T : T + 16, 0:HEAD].astype(F32)
            doc = jnp.where(key_id >= strip[0:1, 0:1], 1.0, 0.0) + jnp.where(key_id >= strip[8:9, 0:1], 1.0, 0.0)
            kt_ref[tt, 0:HEAD, at] = jnp.transpose(block[0:T, 0:HEAD])
            kt_ref[tt, HEAD : 2 * HEAD, at] = jnp.where(doc == doc_id, 0.0, -BIG).astype(BF16)

    ones = jnp.ones((2 * T, HEAD), BF16)

    def wide(v, n):
        return jnp.concatenate([v] * n, axis=1)

    def values_of(tt):
        v = jnp.concatenate([block[0:T, HEAD : 2 * HEAD] for block in blocks(tt)], axis=0)
        return jnp.concatenate([v, ones], axis=1)

    def soften(group, scores, weights, own):
        factors = []
        for piece in range(8):
            at = slice(piece * 128, (piece + 1) * 128)
            s = scores[at, :]
            if own:
                row = lax.broadcasted_iota(jnp.int32, (128, 2 * T), 0) + (piece % 2) * 128
                col = lax.broadcasted_iota(jnp.int32, (128, 2 * T), 1)
                s = jnp.where(col <= row + c * T, s, -2.0 * BIG)
                m = jnp.broadcast_to(jnp.max(s, axis=1, keepdims=True), (128, 128))
            else:
                m_old = m_ref[group, at, :]
                m = jnp.maximum(m_old, jnp.max(s, axis=1, keepdims=True))
                factors.append(jnp.exp2((m_old - m) * EXP_SCALE))
            weights[at, :] = jnp.exp2(((s - wide(m, 4)) * EXP_SCALE).astype(BF16))
            m_ref[group, at, :] = m
        return factors

    def gather_values(group, weights, values, factors):
        update = dot(weights[...], values)
        if not factors:
            acc_ref[group] = update
            return
        for piece, factor in enumerate(factors):
            at = slice(piece * 128, (piece + 1) * 128)
            acc_ref[group, at, :] = acc_ref[group, at, :] * wide(factor, 2) + update[at, :]

    def own_chip():
        keys, values = kt_ref[t], values_of(t)
        s_a = dot(qa[0], keys)
        s_b = dot(qa[1], keys)
        soften(0, s_a, pa_ref, True)
        gather_values(0, pa_ref, values, None)
        soften(1, s_b, pb_ref, True)
        gather_values(1, pb_ref, values, None)

    def attend_chip(tt, upper):
        values = values_of(tt)
        s_b = dot(qa[1], kt_ref[tt])
        factors_a = soften(0, s_ref, pa_ref, False)
        gather_values(0, pa_ref, values, factors_a)
        s_ref[...] = dot(qa[0], kt_ref[jnp.minimum(tt + 1, upper)])
        factors_b = soften(1, s_b, pb_ref, False)
        gather_values(1, pb_ref, values, factors_b)

    chips = jnp.minimum(t, REACH)

    def attend(quarter):
        def chip(tt, carry):
            attend_chip(tt, jnp.maximum(t - 1, 0))
            return carry

        low = t - chips + lax.div(chips * quarter, 4)
        high = t - chips + lax.div(chips * (quarter + 1), 4)
        lax.fori_loop(low, high, chip, 0)

    def finish():
        for h in range(8):
            acc = acc_ref[h // 4, pl.ds((h % 4) * T, T), :]
            out = (acc[:, 0:HEAD] / acc[:, HEAD : 2 * HEAD]).astype(BF16)
            to_ref[128 : 128 + T, h * HEAD : (h + 1) * HEAD] = out
        last = Send(
            to_ref.at[pl.ds(128 + T - HALO, HALO)], to_ref.at[pl.ds(128 - HALO, HALO)],
            {"seq": lax.rem(i + 1, 32)},
        )
        first = Send(
            to_ref.at[pl.ds(128, HALO)], to_ref.at[pl.ds(128 + T, HALO)],
            {"seq": lax.rem(i + 31, 32)},
        )
        return [last, first]

    gather_kv.stage3()
    gather_w0.stage0()
    gather_w1.stage0()
    gather_kv.sibs[0].wait()
    build_keys(t)
    own_chip()
    gather_kv.stage4()

    def column(ref):
        return jnp.transpose(jnp.broadcast_to(ref[...].astype(F32), (128, T)))

    to_ref[0 : 128 - HALO, :] = jnp.zeros((128 - HALO, FEAT), BF16)
    to_ref[128 + T + HALO : 512, :] = jnp.zeros((128 - HALO, FEAT), BF16)
    span_start = column(start_ref)
    span_count = column(count_ref)
    inverse_count = 1.0 / span_count
    first_row = (i * T - 128).astype(F32)
    row_id = lax.broadcasted_iota(jnp.int32, (T, 512), 1).astype(F32) + first_row
    begin, end = wide(span_start, 4), wide(span_start + span_count, 4)
    select = jnp.where((row_id >= begin) & (row_id < end), 1.0, 0.0).astype(BF16)

    gather_kv.stage5(1)

    def keys_chip(tt, carry):
        build_keys(tt)
        return carry

    lax.fori_loop(t - chips, t, keys_chip, 0)

    @pl.when(chips > 0)
    def _():
        s_ref[...] = dot(qa[0], kt_ref[t - chips])

    attend(0)
    gather_w0.stage1()
    gather_w1.stage1()
    attend(1)
    gather_w0.stage2()
    gather_w1.stage2()
    attend(2)
    gather_w0.stage3()
    gather_w1.stage3()
    attend(3)
    halos = finish()
    gather_w0.stage4()
    gather_w1.stage4()
    gather_w0.stage5()
    gather_w1.stage5()

    def predict(piece, carry):
        cols = pl.ds(pl.multiple_of(piece * 256, 256), 256)
        total = jnp.zeros((T, 256), F32)
        for xx in range(4):
            total = total + dot(normed[:, xx * 896 : (xx + 1) * 896], wbuf[xx, :, :, :, cols].reshape(896, 256))
        p_ref[:, cols] = total
        return carry

    lax.fori_loop(0, 4, predict, 0)
    for s in halos:
        s.wait()

    inner = jnp.zeros((T, 128), F32)
    for piece in range(4):
        cols = slice(piece * 256, (piece + 1) * 256)
        target = dot(select, to_ref[:, cols]) * wide(inverse_count, 2)
        prediction = p_ref[:, cols]
        residual = (prediction - target).astype(BF16)
        r_ref[:, cols] = residual
        product = residual.astype(F32) * prediction
        inner = inner + product[:, 0:128] + product[:, 128:256]
    send_r = Send(r_ref, rsib, sib)
    inner = jnp.broadcast_to(jnp.sum(inner, axis=1, keepdims=True), (T, 128))
    in_own[...] = jnp.transpose(inner)[0:8, :]
    inners = [Send(in_own, in_all.at[d], {"tp": lax.rem(z + d, 8)}) for d in range(1, 8)]

    def normed_grad(d):
        zz = lax.rem(z + d, 8)
        w = wbuf[lax.div(zz, 2), pl.ds(lax.rem(zz, 2) * 2, 2)].reshape(448, FEAT)
        ngb[d] = dot_nt(w, r_ref[...]).astype(BF16)

    lo, hi = pl.ds(0, 224), pl.ds(224, 224)

    def z_send(step, sign, rows_):
        d = (4 - step if sign == 1 else 4 + step)
        box = zrp if sign == 1 else zrm
        return Send(ngb.at[d, rows_], box.at[step, rows_], dev_z[sign])

    def z_add(step, sign, rows_):
        d = (3 - step if sign == 1 else 5 + step)
        box = zrp if sign == 1 else zrm
        ngb[d, rows_] = (ngb[d, rows_].astype(F32) + box[step, rows_].astype(F32)).astype(BF16)

    normed_grad(4)
    z0p, z0m = z_send(0, 1, lo), z_send(0, -1, hi)

    send_nt.wait()
    send_r.wait()

    def grad_a(d):
        yy = mod4(y + d)
        left = nt_ref[:, yy, c].reshape(448, T)
        left_sib = nsib[:, yy].reshape(448, T)
        block = dot(left, r_ref[:, 0:512]) + dot(left_sib, rsib[:, 0:512])
        ga[d] = block.astype(BF16).reshape(4, 112, 512)

    def grad_b(d):
        xx = mod4(x + d)
        left = nt_ref[xx, :, c].reshape(448, T)
        left_sib = nsib[xx].reshape(448, T)
        block = dot(left, r_ref[:, 512:1024]) + dot(left_sib, rsib[:, 512:1024])
        gb[d] = block.astype(BF16).reshape(4, 112, 512)

    two, four = pl.ds(0, 2), pl.ds(2, 2)

    class Scatter:
        def __init__(self, g, r0p, r0m, r1p, r1m, h, s0p, s0m, s1p, s1m, dev_a, dev_b, b):
            self.g, self.r0, self.r1, self.h = g, {1: r0p, -1: r0m}, {1: r1p, -1: r1m}, h
            self.s0, self.s1 = {1: s0p, -1: s0m}, {1: s1p, -1: s1m}
            self.dev_a, self.dev_b, self.b = dev_a, dev_b, b
            self.part = {1: two, -1: four}
            self.cols = {1: pl.ds(0, 256), -1: pl.ds(256, 256)}

        def first(self):
            self.e0 = {s: Send(self.g.at[2, self.part[s]], self.r0[s], self.dev_a[s]) for s in (1, -1)}

        def second(self):
            self.e1 = {}
            for s, d in ((1, 1), (-1, 3)):
                part = self.part[-s]
                self.e1[s] = [Send(self.g.at[d, part], self.r1[s].at[part], self.dev_a[s])]

        def third(self):
            for s, d in ((1, 1), (-1, 3)):
                part = self.part[s]
                self.e0[s].wait()
                self.g[d, part] = (self.g[d, part].astype(F32) + self.r0[s][...].astype(F32)).astype(BF16)
                self.e1[s].append(Send(self.g.at[d, part], self.r1[s].at[part], self.dev_a[s]))

        def fourth(self):
            for s in (1, -1):
                for e in self.e1[s]:
                    e.wait()
            self.h[...] = (
                self.g[0].astype(F32) + self.r1[1][...].astype(F32) + self.r1[-1][...].astype(F32)
            ).astype(BF16)
            far = mod4(self.b + 2)
            self.f0, self.f1 = {}, {}
            for s in (1, -1):
                self.f0[s] = Send(self.h.at[far, :, self.cols[s]], self.s0[s], self.dev_b[s])
            for s in (1, -1):
                cols = self.cols[-s]
                self.f1[s] = [Send(self.h.at[mod4(self.b + s), :, cols], self.s1[s].at[:, cols], self.dev_b[s])]

        def fifth(self):
            for s in (1, -1):
                cols, near = self.cols[s], mod4(self.b + s)
                self.f0[s].wait()
                self.h[near, :, cols] = (
                    self.h[near, :, cols].astype(F32) + self.s0[s][...].astype(F32)
                ).astype(BF16)
                self.f1[s].append(Send(self.h.at[near, :, cols], self.s1[s].at[:, cols], self.dev_b[s]))

        def result(self):
            for s in (1, -1):
                for e in self.f1[s]:
                    e.wait()
            return self.h[self.b].astype(F32) + self.s1[1][...].astype(F32) + self.s1[-1][...].astype(F32)

    scatter_a = Scatter(ga, ra0p, ra0m, ra1p, ra1m, ha, sa0p, sa0m, sa1p, sa1m, dev_y, dev_x, x)
    scatter_b = Scatter(gb, rb0p, rb0m, rb1p, rb1m, hb, sb0p, sb0m, sb1p, sb1m, dev_x, dev_y, y)

    grad_a(2)
    grad_b(2)
    scatter_a.first()
    scatter_b.first()
    grad_a(1)
    grad_a(3)
    scatter_a.second()
    grad_b(1)
    grad_b(3)
    scatter_b.second()
    normed_grad(3)
    z1p = [z_send(1, 1, hi)]
    normed_grad(5)
    z1m = [z_send(1, -1, lo)]
    z0p.wait()
    z_add(0, 1, lo)
    z1p.append(z_send(1, 1, lo))
    z0m.wait()
    z_add(0, -1, hi)
    z1m.append(z_send(1, -1, hi))
    normed_grad(2)
    normed_grad(6)
    scatter_a.third()
    scatter_b.third()

    def z_pass(step, plus, minus):
        out_p, out_m = [], []
        for n in range(2):
            rows_p, rows_m = (hi, lo)[n], (lo, hi)[n]
            plus[n].wait()
            z_add(step, 1, rows_p)
            out_p.append(z_send(step + 1, 1, rows_p))
            minus[n].wait()
            z_add(step, -1, rows_m)
            out_m.append(z_send(step + 1, -1, rows_m))
        return out_p, out_m

    z2p, z2m = z_pass(1, z1p, z1m)
    normed_grad(1)
    normed_grad(7)
    normed_grad(0)
    grad_a(0)
    grad_b(0)
    z3p, z3m = z_pass(2, z2p, z2m)
    scatter_a.fourth()
    scatter_b.fourth()
    scatter_a.fifth()
    scatter_b.fifth()

    total_inner = in_own[0:1, :]
    for d, e in enumerate(inners):
        e.wait()
        total_inner = total_inner + in_all[d + 1, 0:1, :]
    scale_row = sct_ref[0:1, :]
    factor = total_inner * scale_row * scale_row * (1.0 / WIDE)
    for e in z3p + z3m:
        e.wait()
    mine = pl.ds(lax.rem(z, 2) * 448, 448)
    ng = ngb[0].astype(F32) + zrp[3].astype(F32) + zrm[3].astype(F32)
    u = ng * wide(gt_ref[mine, :], 2)
    gh_ref[...] = u * scale_row - ht_ref[mine, :].astype(F32) * factor

    gp_ref[:, 0:512] = scatter_a.result()
    gp_ref[:, 512:1024] = scatter_b.result()
    drain()


def deliver(gp_in, gh_in, gp_out, gh_out, gp, gh, sems):
    into = [pltpu.make_async_copy(gp_in, gp, sems.at[0]), pltpu.make_async_copy(gh_in, gh, sems.at[1])]
    out = [pltpu.make_async_copy(gp, gp_out, sems.at[2]), pltpu.make_async_copy(gh, gh_out, sems.at[3])]
    for copy in into:
        copy.start()
    for first, second in zip(into, out):
        first.wait()
        second.start()
    for copy in out:
        copy.wait()


def vm(shape, dtype=BF16):
    return pltpu.VMEM(shape, dtype)


def body(teacher_query, teacher_key, teacher_value, t_segment, s_hidden, norm_gain, proj_weight, span_start, span_count):
    spec = pl.BlockSpec(memory_space=pltpu.VMEM)
    scratch = [
        vm((2, 4, 4, T + 16, 2 * HEAD)),
        vm((16, 2 * HEAD, 2 * T)),
        vm((4, 4, 2, 112, FEAT)),
        vm((2, 4 * T, 2 * HEAD)),
        vm((2, 4 * T, 128), F32),
        vm((2, 4 * T, 2 * HEAD), F32),
        vm((4 * T, 2 * T), F32),
        vm((4 * T, 2 * T)),
        vm((4 * T, 2 * T)),
        vm((512, FEAT)),
        vm((T, WIDE)),
        vm((4, 4, 2, 112, T)),
        vm((4, 4, 112, T)),
        vm((896, T)),
        vm((896, 128), F32),
        vm((T, 128), F32),
        vm((8, T), F32),
        vm((T, FEAT), F32),
        vm((T, FEAT)),
        vm((T, FEAT)),
        vm((8, T), F32),
        vm((8, 8, T), F32),
        vm((8, 448, T)),
        vm((4, 448, T)),
        vm((4, 448, T)),
        vm((4, 4, 112, 512)),
        vm((4, 4, 112, 512)),
    ]
    scratch += [vm((2, 112, 512)), vm((2, 112, 512)), vm((4, 112, 512)), vm((4, 112, 512))] * 2
    scratch += [vm((4, 112, 512))] * 2
    scratch += [vm((112, 256)), vm((112, 256)), vm((112, 512)), vm((112, 512))] * 2
    scratch += [pltpu.SemaphoreType.DMA((EVENTS,)), pltpu.SemaphoreType.DMA((EVENTS,))]
    grad_proj, grad_hidden = pl.pallas_call(
        kernel,
        out_shape=(jax.ShapeDtypeStruct((112, FEAT), F32), jax.ShapeDtypeStruct((448, T), F32)),
        in_specs=[spec] * 9,
        out_specs=(spec, spec),
        scratch_shapes=scratch,
        compiler_params=pltpu.CompilerParams(
            collective_id=0, has_side_effects=True, vmem_limit_bytes=60 * 2**20
        ),
    )(
        teacher_query, teacher_key, teacher_value, t_segment.reshape(1, T), s_hidden,
        norm_gain.reshape(28, 128), proj_weight, span_start.reshape(1, T), span_count.reshape(1, T),
    )
    anywhere = pl.BlockSpec(memory_space=pl.ANY)
    grad_proj, grad_hidden = pl.pallas_call(
        deliver,
        out_shape=(jax.ShapeDtypeStruct((112, FEAT), F32), jax.ShapeDtypeStruct((448, T), F32)),
        in_specs=[anywhere] * 2,
        out_specs=(anywhere, anywhere),
        scratch_shapes=[vm((112, FEAT), F32), vm((448, T), F32), pltpu.SemaphoreType.DMA((4,))],
        compiler_params=pltpu.CompilerParams(vmem_limit_bytes=60 * 2**20),
    )(grad_proj, grad_hidden)
    return grad_proj, grad_hidden.T


def solution(mesh):
    return jax.shard_map(
        body,
        mesh=mesh,
        in_specs=(
            P("seq", "tp"),
            P("seq", "tp"),
            P("seq", "tp"),
            P("seq"),
            P("seq", None),
            P(),
            P("seq", "tp"),
            P("seq"),
            P("seq"),
        ),
        out_specs=(P("seq", "tp"), P("seq", "tp")),
        check_vma=False,
    )
```

```python
import math

import jax
import jax.numpy as jnp
from jax import lax
from jax.experimental import pallas as pl
from jax.experimental.pallas import tpu as pltpu
from jax.sharding import PartitionSpec as P

MESH = pl.DeviceIdType.MESH
F32, BF16 = jnp.float32, jnp.bfloat16
HEAD = 128
T = 256
WIDE = 3584
FEAT = 1024
BIG = float(2**20)
EXP_SCALE = math.log2(math.e) / math.sqrt(HEAD)
REACH = 12
HALO = 80
EVENTS = 176

NT = (((1,), (1,)), ((), ()))


def dot(a, b):
    return jnp.dot(a, b, preferred_element_type=F32)


def dot_nt(a, b):
    return lax.dot_general(a, b, NT, preferred_element_type=F32)


def kernel(
    q_hbm, k_ref, v_ref, seg_ref, sh_hbm, gain_ref, w_hbm, start_ref, count_ref,
    gp_ref, gh_ref,
    q_ref, sh_ref, kvbuf, wbuf, qa, m_ref, acc_ref, pa_ref, pb_ref, to_ref,
    normed, nt_ref, nsib, ht_ref, gt_ref, sc_ref, sct_ref, p_ref, r_ref, rsib,
    in_own, in_all, ngb, zrp, zrm,
    ga, gb, ra0p, ra0m, ra1p, ra1m, rb0p, rb0m, rb1p, rb1m,
    ha, hb, sa0p, sa0m, sa1p, sa1m, sb0p, sb0m, sb1p, sb1m,
    send_sems, recv_sems, load_sems,
):
    i = lax.axis_index("seq")
    z = lax.axis_index("tp")
    c = lax.rem(i, 2)
    t = lax.div(i, 2)
    y = lax.rem(t, 4)
    x = lax.div(t, 4)
    oc = 1 - c

    def mod4(v):
        return lax.rem(v + 8, 4)

    def seq_dev(xx, yy, cc):
        return {"seq": (xx * 4 + yy) * 2 + cc}

    dev_x = {1: seq_dev(mod4(x + 1), y, c), -1: seq_dev(mod4(x - 1), y, c)}
    dev_y = {1: seq_dev(x, mod4(y + 1), c), -1: seq_dev(x, mod4(y - 1), c)}
    dev_z = {d: {"tp": lax.rem(z + d + 8, 8)} for d in (1, -1)}
    sib = seq_dev(x, y, oc)

    barrier = pltpu.get_barrier_semaphore()
    partners = [dev_x[1], dev_x[-1], dev_y[1], dev_y[-1], sib, {"seq": lax.rem(i + 2 * c + 31, 32)}]
    partners += [{"tp": lax.rem(z + d, 8)} for d in range(1, 8)]
    for device in partners:
        pl.semaphore_signal(barrier, inc=1, device_id=device, device_id_type=MESH)

    loads = [
        pltpu.make_async_copy(sh_hbm, sh_ref, load_sems.at[0]),
        pltpu.make_async_copy(w_hbm, wbuf.at[x, y, c], load_sems.at[1]),
        pltpu.make_async_copy(q_hbm, q_ref, load_sems.at[2]),
    ]
    for load in loads:
        load.start()

    counter = [0]
    sent = []

    class Send:
        def __init__(self, src, dst, device, arrive=None):
            n = counter[0]
            counter[0] += 1
            self.parts = (n, device)
            self.copy = self.make(src, dst)
            self.copy.start()
            sent.append(self.copy)
            self.arrive = dst if arrive is None else arrive

        def make(self, src, dst):
            n, device = self.parts
            return pltpu.make_async_remote_copy(
                src_ref=src, dst_ref=dst, send_sem=send_sems.at[n], recv_sem=recv_sems.at[n],
                device_id=device, device_id_type=MESH,
            )

        def wait(self):
            self.make(self.arrive, self.arrive).wait_recv()

    def drain(count):
        for copy in sent[:count]:
            copy.wait_send()
        del sent[:count]

    class Gather:
        def __init__(self, view, column, a, b, sib_b, dev_a, dev_b):
            self.view, self.column = view, column
            self.a, self.b, self.sib_b, self.dev_a, self.dev_b = a, b, sib_b, dev_a, dev_b
            self.p2, self.f2, self.sibs = {}, {}, []

        def at(self, da, db, part=None):
            return self.view(mod4(self.a + da), mod4(self.b + db), part)

        def to_a(self, sign, da, part=None):
            ref = self.at(da, 0, part)
            return Send(ref, ref, self.dev_a[sign], self.at(da - sign, 0, part))

        def to_b(self, sign, da, db, part=None):
            ref = self.at(da, db, part)
            return Send(ref, ref, self.dev_b[sign], self.at(da, db - sign, part))

        def to_sib(self, db):
            ref = self.column(mod4(self.b + db), c)
            self.sibs.append(Send(ref, ref, sib, self.column(mod4(self.sib_b + db), oc)))

        def stage0(self):
            self.p1 = {s: self.to_a(s, 0) for s in (1, -1)}
            for s in (1, -1):
                self.p2[s, 0] = self.to_b(s, 0, 0)

        def stage1(self):
            self.f1 = {}
            for s, part in ((1, 0), (-1, 1)):
                self.p1[s].wait()
                self.f1[s] = self.to_a(s, -s, part)
                for sb in (1, -1):
                    self.p2[sb, -s] = self.to_b(sb, -s, 0)
            self.forward(0)

        def forward(self, da):
            for s, part in ((1, 0), (-1, 1)):
                self.p2[s, da].wait()
                self.f2[s, da] = self.to_b(s, da, -s, part)

        def stage2(self):
            for s in (1, -1):
                self.f1[s].wait()
            for sb in (1, -1):
                self.p2[sb, 2] = self.to_b(sb, 2, 0)
            self.forward(-1)
            self.forward(1)
            self.to_sib(0)

        def stage3(self):
            self.forward(2)
            self.to_sib(-1)
            self.to_sib(1)

        def stage4(self):
            for key in self.f2:
                self.f2[key].wait()
            self.to_sib(2)

        def stage5(self, first=0):
            for s in self.sibs[first:]:
                s.wait()

    def kv_view(aa, bb, part):
        if part is None:
            return kvbuf.at[c, aa, bb]
        return kvbuf.at[c, aa, bb, pl.ds((0, 128)[part], (128, 144)[part])]

    def w_view(first, x_first):
        def view(aa, bb, part):
            xx, yy = (aa, bb) if x_first else (bb, aa)
            if part is None:
                return wbuf.at[xx, yy, c, :, pl.ds(first, 512)]
            return wbuf.at[xx, yy, c, :, pl.ds(first + 256 * part, 256)]

        return view

    kv_a, kv_b = oc * x + c * y, oc * y + c * x
    step_a = {d: seq_dev(mod4(x + d * oc), mod4(y + d * c), c) for d in (1, -1)}
    step_b = {d: seq_dev(mod4(x + d * c), mod4(y + d * oc), c) for d in (1, -1)}
    gather_kv = Gather(kv_view, lambda bb, cc: kvbuf.at[cc, :, bb], kv_a, kv_b, kv_a, step_a, step_b)
    gather_w0 = Gather(w_view(0, True), lambda bb, cc: wbuf.at[:, bb, cc, :, pl.ds(0, 512)], x, y, y, dev_x, dev_y)
    gather_w1 = Gather(w_view(512, False), lambda bb, cc: wbuf.at[bb, :, cc, :, pl.ds(512, 512)], y, x, x, dev_y, dev_x)

    seg = seg_ref[...]
    below1 = jnp.sum((seg < 1).astype(F32), axis=1, keepdims=True)
    below2 = jnp.sum((seg < 2).astype(F32), axis=1, keepdims=True)
    strip_row = lax.broadcasted_iota(jnp.int32, (16, 128), 0)
    kvbuf[c, kv_a, kv_b, 0:T, 0:HEAD] = k_ref[...]
    kvbuf[c, kv_a, kv_b, 0:T, HEAD : 2 * HEAD] = v_ref[...]
    strip = jnp.where(strip_row < 8, below1, below2).astype(BF16)
    kvbuf[c, kv_a, kv_b, T : T + 16, :] = jnp.concatenate([strip, strip], axis=1)

    pl.semaphore_wait(barrier, len(partners))

    gather_kv.stage0()

    loads[0].wait()
    squares = jnp.zeros((T, 128), F32)
    for piece in range(WIDE // 128):
        h = sh_ref[:, piece * 128 : (piece + 1) * 128].astype(F32)
        squares = squares + h * h
    mean = jnp.sum(squares, axis=1, keepdims=True) * (1.0 / WIDE)
    scale = lax.rsqrt(mean + 1e-6)
    scale_wide = jnp.broadcast_to(scale, (T, 128))
    sc_ref[...] = scale_wide
    sct_ref[...] = jnp.transpose(scale_wide)[0:8, :]

    def norm_piece(piece, carry):
        cols = pl.ds(pl.multiple_of(piece * 896, 128), 896)
        h = sh_ref[:, cols]
        gain = jnp.concatenate([gain_ref[pl.ds(piece * 7 + n, 1), :] for n in range(7)], axis=1)
        value = (h.astype(F32) * sc_ref[:, 0:1] * gain).astype(BF16)
        normed[:, cols] = value
        nt_ref[piece] = jnp.transpose(value).reshape(4, 2, 112, T)

        @pl.when(piece == lax.div(z, 2))
        def _():
            ht_ref[...] = jnp.transpose(h)
            gt_ref[...] = jnp.transpose(jnp.broadcast_to(gain, (128, 896)))

        return carry

    lax.fori_loop(0, 1, norm_piece, 0)
    gather_kv.stage1()
    lax.fori_loop(1, 3, norm_piece, 0)
    gather_kv.stage2()
    loads[1].wait()
    gather_w0.stage0()
    gather_w1.stage0()
    lax.fori_loop(3, 4, norm_piece, 0)
    send_nt = Send(nt_ref.at[:, :, oc], nsib, sib)
    loads[2].wait()

    rows = lax.broadcasted_iota(jnp.int32, (T, 128), 0).astype(F32)
    lanes = lax.broadcasted_iota(jnp.int32, (T, 128), 1).astype(F32)

    def doc_of(n1, n2):
        return jnp.where(rows >= n1, 1.0, 0.0) + jnp.where(rows >= n2, 1.0, 0.0)

    one_hot = jnp.where(doc_of(below1, below2) == lanes, 1.0, 0.0).astype(BF16)
    for h in range(8):
        at = pl.ds((h % 4) * T, T)
        qa[h // 4, at, 0:HEAD] = q_ref[:, h * HEAD : (h + 1) * HEAD]
        qa[h // 4, at, HEAD : 2 * HEAD] = one_hot

    doc_id = lax.broadcasted_iota(jnp.int32, (16, T), 0).astype(F32)
    key_id = lax.broadcasted_iota(jnp.int32, (16, T), 1).astype(F32)

    def blocks(tt):
        xx, yy = lax.div(tt, 4), lax.rem(tt, 4)
        return kvbuf.at[0, xx, yy], kvbuf.at[1, yy, xx]

    def keys_of(tt):
        sides = []
        for block in blocks(tt):
            strip = block[T : T + 16, 0:HEAD].astype(F32)
            doc = jnp.where(key_id >= strip[0:1, 0:1], 1.0, 0.0) + jnp.where(key_id >= strip[8:9, 0:1], 1.0, 0.0)
            bias = jnp.where(doc == doc_id, 0.0, -BIG).astype(BF16)
            rest = jnp.zeros((HEAD - 16, T), BF16)
            sides.append(jnp.concatenate([jnp.transpose(block[0:T, 0:HEAD]), bias, rest], axis=0))
        return jnp.concatenate(sides, axis=1)

    ones = jnp.ones((2 * T, HEAD), BF16)

    def wide(v, n):
        return jnp.concatenate([v] * n, axis=1)

    def values_of(tt):
        v = jnp.concatenate([block[0:T, HEAD : 2 * HEAD] for block in blocks(tt)], axis=0)
        return jnp.concatenate([v, ones], axis=1)

    def soften(group, scores, weights, own):
        factors = []
        for piece in range(8):
            at = slice(piece * 128, (piece + 1) * 128)
            s = scores[at, :]
            if own:
                row = lax.broadcasted_iota(jnp.int32, (128, 2 * T), 0) + (piece % 2) * 128
                col = lax.broadcasted_iota(jnp.int32, (128, 2 * T), 1)
                s = jnp.where(col <= row + c * T, s, -2.0 * BIG)
                m = jnp.broadcast_to(jnp.max(s, axis=1, keepdims=True), (128, 128))
            else:
                m_old = m_ref[group, at, :]
                m = jnp.maximum(m_old, jnp.max(s, axis=1, keepdims=True))
                factors.append(jnp.exp2((m_old - m) * EXP_SCALE))
            weights[at, :] = jnp.exp2(((s - wide(m, 4)) * EXP_SCALE).astype(BF16))
            m_ref[group, at, :] = m
        return factors

    def gather_values(group, weights, values, factors):
        update = dot(weights[...], values)
        if not factors:
            acc_ref[group] = update
            return
        for piece, factor in enumerate(factors):
            at = slice(piece * 128, (piece + 1) * 128)
            acc_ref[group, at, :] = acc_ref[group, at, :] * wide(factor, 2) + update[at, :]

    def attend_chip(tt, own):
        keys, values = keys_of(tt), values_of(tt)
        s_a = dot(qa[0], keys)
        s_b = dot(qa[1], keys)
        factors_a = soften(0, s_a, pa_ref, own)
        gather_values(0, pa_ref, values, factors_a)
        factors_b = soften(1, s_b, pb_ref, own)
        gather_values(1, pb_ref, values, factors_b)

    def near(n):
        n = n + jnp.where(n >= 4, 1, 0)
        return lax.div(n, 3) - 1, lax.rem(n, 3) - 1

    def far(n):
        return jnp.where(n < 4, 2, n - 5), jnp.where(n < 4, n, 2)

    def attend(place, low, high):
        def step(n, carry):
            dx, dy = place(n)
            tt = mod4(x + dx) * 4 + mod4(y + dy)

            @pl.when((tt < t) & (tt >= t - REACH))
            def _():
                attend_chip(tt, False)

            return carry

        lax.fori_loop(low, high, step, 0)

    def finish():
        for h in range(8):
            acc = acc_ref[h // 4, pl.ds((h % 4) * T, T), :]
            out = (acc[:, 0:HEAD] / acc[:, HEAD : 2 * HEAD]).astype(BF16)
            to_ref[128 : 128 + T, h * HEAD : (h + 1) * HEAD] = out
        last = Send(
            to_ref.at[pl.ds(128 + T - HALO, HALO)], to_ref.at[pl.ds(128 - HALO, HALO)],
            {"seq": lax.rem(i + 1, 32)},
        )
        first = Send(
            to_ref.at[pl.ds(128, HALO)], to_ref.at[pl.ds(128 + T, HALO)],
            {"seq": lax.rem(i + 31, 32)},
        )
        return [last, first]

    def column(ref):
        return jnp.transpose(jnp.broadcast_to(ref[...].astype(F32), (128, T)))

    to_ref[0 : 128 - HALO, :] = jnp.zeros((128 - HALO, FEAT), BF16)
    to_ref[128 + T + HALO : 512, :] = jnp.zeros((128 - HALO, FEAT), BF16)
    span_start = column(start_ref)
    span_count = column(count_ref)
    inverse_count = 1.0 / span_count
    first_row = (i * T - 128).astype(F32)
    row_id = lax.broadcasted_iota(jnp.int32, (T, 512), 1).astype(F32) + first_row
    begin, end = wide(span_start, 4), wide(span_start + span_count, 4)
    select = jnp.where((row_id >= begin) & (row_id < end), 1.0, 0.0).astype(BF16)

    gather_kv.stage3()
    gather_kv.sibs[0].wait()
    attend_chip(t, True)
    gather_kv.stage4()
    gather_kv.sibs[1].wait()
    gather_kv.sibs[2].wait()
    gather_w0.stage1()
    gather_w1.stage1()
    attend(near, 0, 4)
    gather_w0.stage2()
    gather_w1.stage2()
    attend(near, 4, 8)
    gather_kv.sibs[3].wait()
    gather_w0.stage3()
    gather_w1.stage3()
    attend(far, 0, 4)
    gather_w0.stage4()
    gather_w1.stage4()
    attend(far, 4, 7)
    gathered = len(sent)
    halos = finish()
    gather_w0.stage5()
    gather_w1.stage5()

    def predict(piece, carry):
        cols = pl.ds(pl.multiple_of(piece * 256, 256), 256)
        total = jnp.zeros((T, 256), F32)
        for xx in range(4):
            total = total + dot(normed[:, xx * 896 : (xx + 1) * 896], wbuf[xx, :, :, :, cols].reshape(896, 256))
        p_ref[:, cols] = total
        return carry

    lax.fori_loop(0, 4, predict, 0)
    for s in halos:
        s.wait()

    inner = jnp.zeros((T, 128), F32)
    send_r = []
    for piece in range(4):
        cols = slice(piece * 256, (piece + 1) * 256)
        target = dot(select, to_ref[:, cols]) * wide(inverse_count, 2)
        prediction = p_ref[:, cols]
        residual = (prediction - target).astype(BF16)
        r_ref[:, cols] = residual
        product = residual.astype(F32) * prediction
        inner = inner + product[:, 0:128] + product[:, 128:256]
        if piece % 2 == 1:
            half = pl.ds((piece - 1) * 256, 512)
            send_r.append(Send(r_ref.at[:, half], rsib.at[:, half], sib))
    inner = jnp.broadcast_to(jnp.sum(inner, axis=1, keepdims=True), (T, 128))
    in_own[...] = jnp.transpose(inner)[0:8, :]
    inners = [Send(in_own, in_all.at[d], {"tp": lax.rem(z + d, 8)}) for d in range(1, 8)]

    def normed_grad(d):
        zz = lax.rem(z + d, 8)
        w = wbuf[lax.div(zz, 2), pl.ds(lax.rem(zz, 2) * 2, 2)].reshape(448, FEAT)
        ngb[d] = dot_nt(w, r_ref[...]).astype(BF16)

    lo, hi = pl.ds(0, 224), pl.ds(224, 224)

    def z_send(step, sign, rows_):
        d = (4 - step if sign == 1 else 4 + step)
        box = zrp if sign == 1 else zrm
        return Send(ngb.at[d, rows_], box.at[step, rows_], dev_z[sign])

    def z_add(step, sign, rows_):
        d = (3 - step if sign == 1 else 5 + step)
        box = zrp if sign == 1 else zrm
        ngb[d, rows_] = (ngb[d, rows_].astype(F32) + box[step, rows_].astype(F32)).astype(BF16)

    normed_grad(4)
    z0p, z0m = z_send(0, 1, lo), z_send(0, -1, hi)

    send_nt.wait()
    send_r[0].wait()

    def grad_a(d):
        yy = mod4(y + d)
        left = nt_ref[:, yy, c].reshape(448, T)
        left_sib = nsib[:, yy].reshape(448, T)
        block = dot(left, r_ref[:, 0:512]) + dot(left_sib, rsib[:, 0:512])
        ga[d] = block.astype(BF16).reshape(4, 112, 512)

    def grad_b(d):
        xx = mod4(x + d)
        left = nt_ref[xx, :, c].reshape(448, T)
        left_sib = nsib[xx].reshape(448, T)
        block = dot(left, r_ref[:, 512:1024]) + dot(left_sib, rsib[:, 512:1024])
        gb[d] = block.astype(BF16).reshape(4, 112, 512)

    two, four = pl.ds(0, 2), pl.ds(2, 2)

    class Scatter:
        def __init__(self, g, r0p, r0m, r1p, r1m, h, s0p, s0m, s1p, s1m, dev_a, dev_b, b):
            self.g, self.r0, self.r1, self.h = g, {1: r0p, -1: r0m}, {1: r1p, -1: r1m}, h
            self.s0, self.s1 = {1: s0p, -1: s0m}, {1: s1p, -1: s1m}
            self.dev_a, self.dev_b, self.b = dev_a, dev_b, b
            self.part = {1: two, -1: four}
            self.cols = {1: pl.ds(0, 256), -1: pl.ds(256, 256)}

        def first(self):
            self.e0 = {s: Send(self.g.at[2, self.part[s]], self.r0[s], self.dev_a[s]) for s in (1, -1)}

        def second(self):
            self.e1 = {}
            for s, d in ((1, 1), (-1, 3)):
                part = self.part[-s]
                self.e1[s] = [Send(self.g.at[d, part], self.r1[s].at[part], self.dev_a[s])]

        def third(self):
            for s, d in ((1, 1), (-1, 3)):
                part = self.part[s]
                self.e0[s].wait()
                self.g[d, part] = (self.g[d, part].astype(F32) + self.r0[s][...].astype(F32)).astype(BF16)
                self.e1[s].append(Send(self.g.at[d, part], self.r1[s].at[part], self.dev_a[s]))

        def fourth(self):
            for s in (1, -1):
                for e in self.e1[s]:
                    e.wait()
            self.h[...] = (
                self.g[0].astype(F32) + self.r1[1][...].astype(F32) + self.r1[-1][...].astype(F32)
            ).astype(BF16)
            far = mod4(self.b + 2)
            self.f0, self.f1 = {}, {}
            for s in (1, -1):
                self.f0[s] = Send(self.h.at[far, :, self.cols[s]], self.s0[s], self.dev_b[s])
            for s in (1, -1):
                cols = self.cols[-s]
                self.f1[s] = [Send(self.h.at[mod4(self.b + s), :, cols], self.s1[s].at[:, cols], self.dev_b[s])]

        def fifth(self):
            for s in (1, -1):
                cols, near = self.cols[s], mod4(self.b + s)
                self.f0[s].wait()
                self.h[near, :, cols] = (
                    self.h[near, :, cols].astype(F32) + self.s0[s][...].astype(F32)
                ).astype(BF16)
                self.f1[s].append(Send(self.h.at[near, :, cols], self.s1[s].at[:, cols], self.dev_b[s]))

        def result(self):
            for s in (1, -1):
                for e in self.f1[s]:
                    e.wait()
            return self.h[self.b].astype(F32) + self.s1[1][...].astype(F32) + self.s1[-1][...].astype(F32)

    scatter_a = Scatter(ga, ra0p, ra0m, ra1p, ra1m, ha, sa0p, sa0m, sa1p, sa1m, dev_y, dev_x, x)
    scatter_b = Scatter(gb, rb0p, rb0m, rb1p, rb1m, hb, sb0p, sb0m, sb1p, sb1m, dev_x, dev_y, y)

    grad_a(2)
    scatter_a.first()
    send_r[1].wait()
    grad_b(2)
    scatter_b.first()
    grad_a(1)
    grad_a(3)
    scatter_a.second()
    grad_b(1)
    grad_b(3)
    scatter_b.second()
    normed_grad(3)
    z1p = [z_send(1, 1, hi)]
    normed_grad(5)
    z1m = [z_send(1, -1, lo)]
    z0p.wait()
    z_add(0, 1, lo)
    z1p.append(z_send(1, 1, lo))
    z0m.wait()
    z_add(0, -1, hi)
    z1m.append(z_send(1, -1, hi))
    normed_grad(2)
    normed_grad(6)
    drain(gathered)
    scatter_a.third()
    scatter_b.third()

    def z_pass(step, plus, minus):
        out_p, out_m = [], []
        for n in range(2):
            rows_p, rows_m = (hi, lo)[n], (lo, hi)[n]
            plus[n].wait()
            z_add(step, 1, rows_p)
            out_p.append(z_send(step + 1, 1, rows_p))
            minus[n].wait()
            z_add(step, -1, rows_m)
            out_m.append(z_send(step + 1, -1, rows_m))
        return out_p, out_m

    z2p, z2m = z_pass(1, z1p, z1m)
    normed_grad(1)
    normed_grad(7)
    normed_grad(0)
    grad_a(0)
    grad_b(0)
    z3p, z3m = z_pass(2, z2p, z2m)
    drain(len(sent) - 8)
    scatter_a.fourth()
    scatter_b.fourth()
    scatter_a.fifth()
    scatter_b.fifth()

    total_inner = in_own[0:1, :]
    for d, e in enumerate(inners):
        e.wait()
        total_inner = total_inner + in_all[d + 1, 0:1, :]
    scale_row = sct_ref[0:1, :]
    factor = total_inner * scale_row * scale_row * (1.0 / WIDE)
    for e in z3p + z3m:
        e.wait()
    mine = pl.ds(lax.rem(z, 2) * 448, 448)
    ng = ngb[0].astype(F32) + zrp[3].astype(F32) + zrm[3].astype(F32)
    u = ng * wide(gt_ref[mine, :], 2)
    gh_ref[...] = u * scale_row - ht_ref[mine, :].astype(F32) * factor

    gp_ref[:, 0:512] = scatter_a.result()
    gp_ref[:, 512:1024] = scatter_b.result()
    drain(len(sent))


def deliver(gp_in, gh_in, gp_out, gh_out, gp, gh, sems):
    into = [pltpu.make_async_copy(gp_in, gp, sems.at[0]), pltpu.make_async_copy(gh_in, gh, sems.at[1])]
    out = [pltpu.make_async_copy(gp, gp_out, sems.at[2]), pltpu.make_async_copy(gh, gh_out, sems.at[3])]
    for copy in into:
        copy.start()
    for first, second in zip(into, out):
        first.wait()
        second.start()
    for copy in out:
        copy.wait()


def vm(shape, dtype=BF16):
    return pltpu.VMEM(shape, dtype)


def body(teacher_query, teacher_key, teacher_value, t_segment, s_hidden, norm_gain, proj_weight, span_start, span_count):
    spec = pl.BlockSpec(memory_space=pltpu.VMEM)
    scratch = [
        vm((T, FEAT)),
        vm((T, WIDE)),
        vm((2, 4, 4, T + 16, 2 * HEAD)),
        vm((4, 4, 2, 112, FEAT)),
        vm((2, 4 * T, 2 * HEAD)),
        vm((2, 4 * T, 128), F32),
        vm((2, 4 * T, 2 * HEAD), F32),
        vm((4 * T, 2 * T)),
        vm((4 * T, 2 * T)),
        vm((512, FEAT)),
        vm((T, WIDE)),
        vm((4, 4, 2, 112, T)),
        vm((4, 4, 112, T)),
        vm((896, T)),
        vm((896, 128), F32),
        vm((T, 128), F32),
        vm((8, T), F32),
        vm((T, FEAT), F32),
        vm((T, FEAT)),
        vm((T, FEAT)),
        vm((8, T), F32),
        vm((8, 8, T), F32),
        vm((8, 448, T)),
        vm((4, 448, T)),
        vm((4, 448, T)),
        vm((4, 4, 112, 512)),
        vm((4, 4, 112, 512)),
    ]
    scratch += [vm((2, 112, 512)), vm((2, 112, 512)), vm((4, 112, 512)), vm((4, 112, 512))] * 2
    scratch += [vm((4, 112, 512))] * 2
    scratch += [vm((112, 256)), vm((112, 256)), vm((112, 512)), vm((112, 512))] * 2
    scratch += [pltpu.SemaphoreType.DMA((EVENTS,)), pltpu.SemaphoreType.DMA((EVENTS,)), pltpu.SemaphoreType.DMA((3,))]
    anywhere = pl.BlockSpec(memory_space=pl.ANY)
    grad_proj, grad_hidden = pl.pallas_call(
        kernel,
        out_shape=(jax.ShapeDtypeStruct((112, FEAT), F32), jax.ShapeDtypeStruct((448, T), F32)),
        in_specs=[anywhere, spec, spec, spec, anywhere, spec, anywhere, spec, spec],
        out_specs=(spec, spec),
        scratch_shapes=scratch,
        compiler_params=pltpu.CompilerParams(
            collective_id=0, has_side_effects=True, vmem_limit_bytes=60 * 2**20
        ),
    )(
        teacher_query, teacher_key, teacher_value, t_segment.reshape(1, T), s_hidden,
        norm_gain.reshape(28, 128), proj_weight, span_start.reshape(1, T), span_count.reshape(1, T),
    )
    grad_proj, grad_hidden = pl.pallas_call(
        deliver,
        out_shape=(jax.ShapeDtypeStruct((112, FEAT), F32), jax.ShapeDtypeStruct((448, T), F32)),
        in_specs=[anywhere] * 2,
        out_specs=(anywhere, anywhere),
        scratch_shapes=[vm((112, FEAT), F32), vm((448, T), F32), pltpu.SemaphoreType.DMA((4,))],
        compiler_params=pltpu.CompilerParams(vmem_limit_bytes=60 * 2**20),
    )(grad_proj, grad_hidden)
    return grad_proj, grad_hidden.T


def solution(mesh):
    return jax.shard_map(
        body,
        mesh=mesh,
        in_specs=(
            P("seq", "tp"),
            P("seq", "tp"),
            P("seq", "tp"),
            P("seq"),
            P("seq", None),
            P(),
            P("seq", "tp"),
            P("seq"),
            P("seq"),
        ),
        out_specs=(P("seq", "tp"), P("seq", "tp")),
        check_vma=False,
    )
```

```python
import math

import jax
import jax.numpy as jnp
from jax import lax
from jax.experimental import pallas as pl
from jax.experimental.pallas import tpu as pltpu
from jax.sharding import PartitionSpec as P

MESH = pl.DeviceIdType.MESH
F32, BF16 = jnp.float32, jnp.bfloat16
HEAD = 128
T = 256
WIDE = 3584
FEAT = 1024
BIG = float(2**20)
EXP_SCALE = math.log2(math.e) / math.sqrt(HEAD)
REACH = 12
HALO = 80
EVENTS = 224

NT = (((1,), (1,)), ((), ()))


def dot(a, b):
    return jnp.dot(a, b, preferred_element_type=F32)


def dot_nt(a, b):
    return lax.dot_general(a, b, NT, preferred_element_type=F32)


def kernel(
    q_hbm, k_ref, v_ref, seg_ref, sh_hbm, gain_ref, w_hbm, start_ref, count_ref,
    gp_ref, gh_ref,
    q_ref, sh_ref, kvbuf, wbuf, qa, m_ref, acc_ref, pa_ref, pb_ref, to_ref,
    normed, nt_ref, nsib, ht_ref, gt_ref, sc_ref, sct_ref, p_ref, r_ref, rsib,
    in_own, in_all, ngb, zrp, zrm,
    g_ref, r0_ref, r1_ref, h_ref, s0_ref, s1_ref,
    send_sems, recv_sems, load_sems,
):
    i = lax.axis_index("seq")
    z = lax.axis_index("tp")
    c = lax.rem(i, 2)
    t = lax.div(i, 2)
    y = lax.rem(t, 4)
    x = lax.div(t, 4)
    oc = 1 - c

    def mod4(v):
        return lax.rem(v + 8, 4)

    def seq_dev(xx, yy, cc):
        return {"seq": (xx * 4 + yy) * 2 + cc}

    dev_x = {1: seq_dev(mod4(x + 1), y, c), -1: seq_dev(mod4(x - 1), y, c)}
    dev_y = {1: seq_dev(x, mod4(y + 1), c), -1: seq_dev(x, mod4(y - 1), c)}
    dev_z = {d: {"tp": lax.rem(z + d + 8, 8)} for d in (1, -1)}
    sib = seq_dev(x, y, oc)

    barrier = pltpu.get_barrier_semaphore()
    partners = [dev_x[1], dev_x[-1], dev_y[1], dev_y[-1], sib, {"seq": lax.rem(i + 2 * c + 31, 32)}]
    partners += [{"tp": lax.rem(z + d, 8)} for d in range(1, 8)]
    for device in partners:
        pl.semaphore_signal(barrier, inc=1, device_id=device, device_id_type=MESH)

    loads = [
        pltpu.make_async_copy(sh_hbm, sh_ref, load_sems.at[0]),
        pltpu.make_async_copy(w_hbm, wbuf.at[x, y, c], load_sems.at[1]),
        pltpu.make_async_copy(q_hbm, q_ref, load_sems.at[2]),
    ]
    for load in loads:
        load.start()

    counter = [0]
    sent = []

    class Send:
        def __init__(self, src, dst, device, arrive=None):
            n = counter[0]
            counter[0] += 1
            self.parts = (n, device)
            self.copy = self.make(src, dst)
            self.copy.start()
            sent.append(self.copy)
            self.arrive = dst if arrive is None else arrive

        def make(self, src, dst):
            n, device = self.parts
            return pltpu.make_async_remote_copy(
                src_ref=src, dst_ref=dst, send_sem=send_sems.at[n], recv_sem=recv_sems.at[n],
                device_id=device, device_id_type=MESH,
            )

        def wait(self):
            self.make(self.arrive, self.arrive).wait_recv()

    def drain(count):
        for copy in sent[:count]:
            copy.wait_send()
        del sent[:count]

    class Gather:
        def __init__(self, view, column, a, b, sib_b, dev_a, dev_b):
            self.view, self.column = view, column
            self.a, self.b, self.sib_b, self.dev_a, self.dev_b = a, b, sib_b, dev_a, dev_b
            self.p2, self.f2, self.sibs = {}, {}, []

        def at(self, da, db, part=None):
            return self.view(mod4(self.a + da), mod4(self.b + db), part)

        def to_a(self, sign, da, part=None):
            ref = self.at(da, 0, part)
            return Send(ref, ref, self.dev_a[sign], self.at(da - sign, 0, part))

        def to_b(self, sign, da, db, part=None):
            ref = self.at(da, db, part)
            return Send(ref, ref, self.dev_b[sign], self.at(da, db - sign, part))

        def to_sib(self, db):
            ref = self.column(mod4(self.b + db), c)
            self.sibs.append(Send(ref, ref, sib, self.column(mod4(self.sib_b + db), oc)))

        def stage0(self):
            self.p1 = {s: self.to_a(s, 0) for s in (1, -1)}
            for s in (1, -1):
                self.p2[s, 0] = self.to_b(s, 0, 0)

        def stage1(self):
            self.f1 = {}
            for s, part in ((1, 0), (-1, 1)):
                self.p1[s].wait()
                self.f1[s] = self.to_a(s, -s, part)
                for sb in (1, -1):
                    self.p2[sb, -s] = self.to_b(sb, -s, 0)
            self.forward(0)

        def forward(self, da):
            for s, part in ((1, 0), (-1, 1)):
                self.p2[s, da].wait()
                self.f2[s, da] = self.to_b(s, da, -s, part)

        def stage2(self):
            for s in (1, -1):
                self.f1[s].wait()
            for sb in (1, -1):
                self.p2[sb, 2] = self.to_b(sb, 2, 0)

        def stage2b(self):
            self.forward(-1)
            self.forward(1)

        def stage3(self):
            self.forward(2)

        def stage4(self):
            for key in self.f2:
                self.f2[key].wait()
            self.to_sib(2)

        def stage5(self):
            for s in self.sibs:
                s.wait()

    def kv_view(aa, bb, part):
        if part is None:
            return kvbuf.at[c, aa, bb]
        return kvbuf.at[c, aa, bb, pl.ds((0, 128)[part], (128, 144)[part])]

    def w_view(first, x_first):
        def view(aa, bb, part):
            xx, yy = (aa, bb) if x_first else (bb, aa)
            if part is None:
                return wbuf.at[xx, yy, c, :, pl.ds(first, 512)]
            return wbuf.at[xx, yy, c, :, pl.ds(first + 256 * part, 256)]

        return view

    kv_a, kv_b = oc * x + c * y, oc * y + c * x
    step_a = {d: seq_dev(mod4(x + d * oc), mod4(y + d * c), c) for d in (1, -1)}
    step_b = {d: seq_dev(mod4(x + d * c), mod4(y + d * oc), c) for d in (1, -1)}
    gather_kv = Gather(kv_view, lambda bb, cc: kvbuf.at[cc, :, bb], kv_a, kv_b, kv_a, step_a, step_b)
    def share(da, db):
        ref = gather_kv.at(da, db)
        return Send(ref, ref, sib, kvbuf.at[oc, mod4(kv_b + da), mod4(kv_a + db)])

    gather_w0 = Gather(w_view(0, True), lambda bb, cc: wbuf.at[:, bb, cc, :, pl.ds(0, 512)], x, y, y, dev_x, dev_y)
    gather_w1 = Gather(w_view(512, False), lambda bb, cc: wbuf.at[bb, :, cc, :, pl.ds(512, 512)], y, x, x, dev_y, dev_x)

    seg = seg_ref[...]
    below1 = jnp.sum((seg < 1).astype(F32), axis=1, keepdims=True)
    below2 = jnp.sum((seg < 2).astype(F32), axis=1, keepdims=True)
    strip_row = lax.broadcasted_iota(jnp.int32, (16, 128), 0)
    kvbuf[c, kv_a, kv_b, 0:T, 0:HEAD] = k_ref[...]
    kvbuf[c, kv_a, kv_b, 0:T, HEAD : 2 * HEAD] = v_ref[...]
    strip = jnp.where(strip_row < 8, below1, below2).astype(BF16)
    kvbuf[c, kv_a, kv_b, T : T + 16, :] = jnp.concatenate([strip, strip], axis=1)

    pl.semaphore_wait(barrier, len(partners))

    gather_kv.stage0()
    shared = [share(0, 0)]

    loads[0].wait()
    squares = jnp.zeros((T, 128), F32)
    for piece in range(WIDE // 128):
        h = sh_ref[:, piece * 128 : (piece + 1) * 128].astype(F32)
        squares = squares + h * h
    mean = jnp.sum(squares, axis=1, keepdims=True) * (1.0 / WIDE)
    scale = lax.rsqrt(mean + 1e-6)
    scale_wide = jnp.broadcast_to(scale, (T, 128))
    sc_ref[...] = scale_wide
    sct_ref[...] = jnp.transpose(scale_wide)[0:8, :]

    def norm_piece(piece, carry):
        cols = pl.ds(pl.multiple_of(piece * 896, 128), 896)
        h = sh_ref[:, cols]
        gain = jnp.concatenate([gain_ref[pl.ds(piece * 7 + n, 1), :] for n in range(7)], axis=1)
        value = (h.astype(F32) * sc_ref[:, 0:1] * gain).astype(BF16)
        normed[:, cols] = value
        nt_ref[piece] = jnp.transpose(value).reshape(4, 2, 112, T)

        @pl.when(piece == lax.div(z, 2))
        def _():
            ht_ref[...] = jnp.transpose(h)
            gt_ref[...] = jnp.transpose(jnp.broadcast_to(gain, (128, 896)))

        return carry

    lax.fori_loop(0, 1, norm_piece, 0)
    gather_kv.stage1()
    near_shared = [share(1, 0), share(-1, 0), share(0, 1), share(0, -1)]
    loads[2].wait()

    rows = lax.broadcasted_iota(jnp.int32, (T, 128), 0).astype(F32)
    lanes = lax.broadcasted_iota(jnp.int32, (T, 128), 1).astype(F32)

    def doc_of(n1, n2):
        return jnp.where(rows >= n1, 1.0, 0.0) + jnp.where(rows >= n2, 1.0, 0.0)

    one_hot = jnp.where(doc_of(below1, below2) == lanes, 1.0, 0.0).astype(BF16)
    for h in range(8):
        at = pl.ds((h % 4) * T, T)
        qa[h // 4, at, 0:HEAD] = q_ref[:, h * HEAD : (h + 1) * HEAD]
        qa[h // 4, at, HEAD : 2 * HEAD] = one_hot

    doc_id = lax.broadcasted_iota(jnp.int32, (16, T), 0).astype(F32)
    key_id = lax.broadcasted_iota(jnp.int32, (16, T), 1).astype(F32)

    def blocks(tt):
        xx, yy = lax.div(tt, 4), lax.rem(tt, 4)
        return kvbuf.at[0, xx, yy], kvbuf.at[1, yy, xx]

    def keys_of(tt):
        sides = []
        for block in blocks(tt):
            strip = block[T : T + 16, 0:HEAD].astype(F32)
            doc = jnp.where(key_id >= strip[0:1, 0:1], 1.0, 0.0) + jnp.where(key_id >= strip[8:9, 0:1], 1.0, 0.0)
            bias = jnp.where(doc == doc_id, 0.0, -BIG).astype(BF16)
            rest = jnp.zeros((HEAD - 16, T), BF16)
            sides.append(jnp.concatenate([jnp.transpose(block[0:T, 0:HEAD]), bias, rest], axis=0))
        return jnp.concatenate(sides, axis=1)

    ones = jnp.ones((2 * T, HEAD), BF16)

    def wide(v, n):
        return jnp.concatenate([v] * n, axis=1)

    def values_of(tt):
        v = jnp.concatenate([block[0:T, HEAD : 2 * HEAD] for block in blocks(tt)], axis=0)
        return jnp.concatenate([v, ones], axis=1)

    def soften(group, scores, weights, own):
        factors = []
        for piece in range(8):
            at = slice(piece * 128, (piece + 1) * 128)
            s = scores[at, :]
            if own:
                row = lax.broadcasted_iota(jnp.int32, (128, 2 * T), 0) + (piece % 2) * 128
                col = lax.broadcasted_iota(jnp.int32, (128, 2 * T), 1)
                s = jnp.where(col <= row + c * T, s, -2.0 * BIG)
                m = jnp.broadcast_to(jnp.max(s, axis=1, keepdims=True), (128, 128))
            else:
                m_old = m_ref[group, at, :]
                m = jnp.maximum(m_old, jnp.max(s, axis=1, keepdims=True))
                factors.append(jnp.exp2((m_old - m) * EXP_SCALE))
            weights[at, :] = jnp.exp2(((s - wide(m, 4)) * EXP_SCALE).astype(BF16))
            m_ref[group, at, :] = m
        return factors

    def gather_values(group, weights, values, factors):
        update = dot(weights[...], values)
        if not factors:
            acc_ref[group] = update
            return
        for piece, factor in enumerate(factors):
            at = slice(piece * 128, (piece + 1) * 128)
            acc_ref[group, at, :] = acc_ref[group, at, :] * wide(factor, 2) + update[at, :]

    def attend_chip(tt, own):
        keys, values = keys_of(tt), values_of(tt)
        s_a = dot(qa[0], keys)
        s_b = dot(qa[1], keys)
        factors_a = soften(0, s_a, pa_ref, own)
        gather_values(0, pa_ref, values, factors_a)
        factors_b = soften(1, s_b, pb_ref, own)
        gather_values(1, pb_ref, values, factors_b)

    def near(n):
        n = n + jnp.where(n >= 4, 1, 0)
        return lax.div(n, 3) - 1, lax.rem(n, 3) - 1

    def far(n):
        return jnp.where(n < 4, 2, n - 5), jnp.where(n < 4, n, 2)

    def attend(place, low, high):
        def step(n, carry):
            dx, dy = place(n)
            tt = mod4(x + dx) * 4 + mod4(y + dy)

            @pl.when((tt < t) & (tt >= t - REACH))
            def _():
                attend_chip(tt, False)

            return carry

        lax.fori_loop(low, high, step, 0)

    def finish():
        for h in range(8):
            acc = acc_ref[h // 4, pl.ds((h % 4) * T, T), :]
            out = (acc[:, 0:HEAD] / acc[:, HEAD : 2 * HEAD]).astype(BF16)
            to_ref[128 : 128 + T, h * HEAD : (h + 1) * HEAD] = out
        last = Send(
            to_ref.at[pl.ds(128 + T - HALO, HALO)], to_ref.at[pl.ds(128 - HALO, HALO)],
            {"seq": lax.rem(i + 1, 32)},
        )
        first = Send(
            to_ref.at[pl.ds(128, HALO)], to_ref.at[pl.ds(128 + T, HALO)],
            {"seq": lax.rem(i + 31, 32)},
        )
        return [last, first]

    def column(ref):
        return jnp.transpose(jnp.broadcast_to(ref[...].astype(F32), (128, T)))

    to_ref[0 : 128 - HALO, :] = jnp.zeros((128 - HALO, FEAT), BF16)
    to_ref[128 + T + HALO : 512, :] = jnp.zeros((128 - HALO, FEAT), BF16)
    span_start = column(start_ref)
    span_count = column(count_ref)
    inverse_count = 1.0 / span_count
    first_row = (i * T - 128).astype(F32)
    row_id = lax.broadcasted_iota(jnp.int32, (T, 512), 1).astype(F32) + first_row
    begin, end = wide(span_start, 4), wide(span_start + span_count, 4)
    select = jnp.where((row_id >= begin) & (row_id < end), 1.0, 0.0).astype(BF16)

    gather_kv.stage2()
    far_shared = [share(2, 0)]
    loads[1].wait()
    gather_w0.stage0()
    gather_w1.stage0()
    shared[0].wait()
    attend_chip(t, True)
    gather_kv.stage2b()
    near_shared += [share(da, db) for da in (1, -1) for db in (1, -1)]
    lax.fori_loop(1, 4, norm_piece, 0)
    send_nt = Send(nt_ref.at[:, :, oc], nsib, sib)
    gather_kv.stage3()
    far_shared += [share(2, 1), share(2, -1)]
    for s in near_shared:
        s.wait()
    attend(near, 0, 3)
    gather_w0.stage1()
    gather_w1.stage1()
    attend(near, 3, 6)
    gather_kv.stage4()
    gather_w0.stage2()
    gather_w1.stage2()
    gather_w0.to_sib(0)
    gather_w1.to_sib(0)
    attend(near, 6, 8)
    for s in far_shared:
        s.wait()
    gather_kv.stage5()
    gather_w0.stage2b()
    gather_w1.stage2b()
    attend(far, 0, 3)
    for gather in (gather_w0, gather_w1):
        gather.stage3()
        gather.to_sib(-1)
        gather.to_sib(1)
    attend(far, 3, 5)
    gather_w0.stage4()
    gather_w1.stage4()
    attend(far, 5, 7)
    gathered = len(sent)
    halos = finish()
    gather_w0.stage5()
    gather_w1.stage5()

    def predict(piece, carry):
        cols = pl.ds(pl.multiple_of(piece * 256, 256), 256)
        total = jnp.zeros((T, 256), F32)
        for xx in range(4):
            total = total + dot(normed[:, xx * 896 : (xx + 1) * 896], wbuf[xx, :, :, :, cols].reshape(896, 256))
        p_ref[:, cols] = total
        return carry

    lax.fori_loop(0, 4, predict, 0)
    for s in halos:
        s.wait()

    inner = jnp.zeros((T, 128), F32)
    send_r = []
    for piece in range(4):
        cols = slice(piece * 256, (piece + 1) * 256)
        target = dot(select, to_ref[:, cols]) * wide(inverse_count, 2)
        prediction = p_ref[:, cols]
        residual = (prediction - target).astype(BF16)
        r_ref[:, cols] = residual
        product = residual.astype(F32) * prediction
        inner = inner + product[:, 0:128] + product[:, 128:256]
        if piece % 2 == 1:
            half = pl.ds((piece - 1) * 256, 512)
            send_r.append(Send(r_ref.at[:, half], rsib.at[:, half], sib))
    inner = jnp.broadcast_to(jnp.sum(inner, axis=1, keepdims=True), (T, 128))
    in_own[...] = jnp.transpose(inner)[0:8, :]
    inners = [Send(in_own, in_all.at[d], {"tp": lax.rem(z + d, 8)}) for d in range(1, 8)]

    def normed_grad(d):
        zz = lax.rem(z + d, 8)
        w = wbuf[lax.div(zz, 2), pl.ds(lax.rem(zz, 2) * 2, 2)].reshape(448, FEAT)
        ngb[d] = dot_nt(w, r_ref[...]).astype(BF16)

    lo, hi = pl.ds(0, 224), pl.ds(224, 224)

    def z_send(step, sign, rows_):
        d = (4 - step if sign == 1 else 4 + step)
        box = zrp if sign == 1 else zrm
        return Send(ngb.at[d, rows_], box.at[step, rows_], dev_z[sign])

    def z_add(step, sign, rows_):
        d = (3 - step if sign == 1 else 5 + step)
        box = zrp if sign == 1 else zrm
        ngb[d, rows_] = (ngb[d, rows_].astype(F32) + box[step, rows_].astype(F32)).astype(BF16)

    normed_grad(4)
    z0p, z0m = z_send(0, 1, lo), z_send(0, -1, hi)

    send_nt.wait()
    send_r[0].wait()

    def grad_a(d):
        yy = mod4(y + d)
        left = nt_ref[:, yy, c].reshape(448, T)
        left_sib = nsib[:, yy].reshape(448, T)
        block = dot(left, r_ref[:, 0:512]) + dot(left_sib, rsib[:, 0:512])
        block = block.astype(BF16)
        g_ref[0, d] = block[:, 0:256].reshape(4, 112, 256)
        g_ref[1, d] = block[:, 256:512].reshape(4, 112, 256)

    def grad_b(d):
        xx = mod4(x + d)
        left = nt_ref[xx, :, c].reshape(448, T)
        left_sib = nsib[xx].reshape(448, T)
        block = dot(left, r_ref[:, 512:1024]) + dot(left_sib, rsib[:, 512:1024])
        block = block.astype(BF16)
        g_ref[2, d] = block[:, 0:256].reshape(4, 112, 256)
        g_ref[3, d] = block[:, 256:512].reshape(4, 112, 256)

    two, four = pl.ds(0, 2), pl.ds(2, 2)

    class Scatter:
        def __init__(self, n, dev_a, dev_b, b):
            self.g, self.h = g_ref.at[n], h_ref.at[n]
            self.r0 = {1: r0_ref.at[n, 0], -1: r0_ref.at[n, 1]}
            self.r1 = {1: r1_ref.at[n, 0], -1: r1_ref.at[n, 1]}
            self.s0 = {1: s0_ref.at[n, 0], -1: s0_ref.at[n, 1]}
            self.s1 = {1: s1_ref.at[n, 0], -1: s1_ref.at[n, 1]}
            self.dev_a, self.dev_b, self.b = dev_a, dev_b, b
            self.part = {1: two, -1: four}
            self.cols = {1: pl.ds(0, 128), -1: pl.ds(128, 128)}

        def first(self):
            self.e0 = {s: Send(self.g.at[2, self.part[s]], self.r0[s], self.dev_a[s]) for s in (1, -1)}

        def second(self):
            self.e1 = {}
            for s, d in ((1, 1), (-1, 3)):
                part = self.part[-s]
                self.e1[s] = [Send(self.g.at[d, part], self.r1[s].at[part], self.dev_a[s])]

        def third(self):
            for s, d in ((1, 1), (-1, 3)):
                part = self.part[s]
                self.e0[s].wait()
                self.g[d, part] = (self.g[d, part].astype(F32) + self.r0[s][...].astype(F32)).astype(BF16)
                self.e1[s].append(Send(self.g.at[d, part], self.r1[s].at[part], self.dev_a[s]))

        def fourth(self):
            for s in (1, -1):
                for e in self.e1[s]:
                    e.wait()
            self.h[...] = (
                self.g[0].astype(F32) + self.r1[1][...].astype(F32) + self.r1[-1][...].astype(F32)
            ).astype(BF16)
            far = mod4(self.b + 2)
            self.f0, self.f1 = {}, {}
            for s in (1, -1):
                self.f0[s] = Send(self.h.at[far, :, self.cols[s]], self.s0[s], self.dev_b[s])
            for s in (1, -1):
                cols = self.cols[-s]
                self.f1[s] = [Send(self.h.at[mod4(self.b + s), :, cols], self.s1[s].at[:, cols], self.dev_b[s])]

        def fifth(self):
            for s in (1, -1):
                cols, near = self.cols[s], mod4(self.b + s)
                self.f0[s].wait()
                self.h[near, :, cols] = (
                    self.h[near, :, cols].astype(F32) + self.s0[s][...].astype(F32)
                ).astype(BF16)
                self.f1[s].append(Send(self.h.at[near, :, cols], self.s1[s].at[:, cols], self.dev_b[s]))

        def result(self):
            for s in (1, -1):
                for e in self.f1[s]:
                    e.wait()
            return self.h[self.b].astype(F32) + self.s1[1][...].astype(F32) + self.s1[-1][...].astype(F32)

    a0, a1 = Scatter(0, dev_y, dev_x, x), Scatter(1, dev_y, dev_x, x)
    b0, b1 = Scatter(2, dev_x, dev_y, y), Scatter(3, dev_x, dev_y, y)

    grad_a(2)
    a0.first()
    send_r[1].wait()
    grad_b(2)
    b0.first()
    a1.first()
    b1.first()
    grad_a(1)
    grad_a(3)
    a0.second()
    grad_b(1)
    grad_b(3)
    b0.second()
    normed_grad(3)
    z1p = [z_send(1, 1, hi)]
    normed_grad(5)
    z1m = [z_send(1, -1, lo)]
    z0p.wait()
    z_add(0, 1, lo)
    z1p.append(z_send(1, 1, lo))
    z0m.wait()
    z_add(0, -1, hi)
    z1m.append(z_send(1, -1, hi))
    a0.third()
    b0.third()
    a1.second()
    b1.second()
    normed_grad(2)
    normed_grad(6)
    a1.third()
    b1.third()
    drain(gathered)

    def z_pass(step, plus, minus):
        out_p, out_m = [], []
        for n in range(2):
            rows_p, rows_m = (hi, lo)[n], (lo, hi)[n]
            plus[n].wait()
            z_add(step, 1, rows_p)
            out_p.append(z_send(step + 1, 1, rows_p))
            minus[n].wait()
            z_add(step, -1, rows_m)
            out_m.append(z_send(step + 1, -1, rows_m))
        return out_p, out_m

    z2p, z2m = z_pass(1, z1p, z1m)
    normed_grad(1)
    normed_grad(7)
    normed_grad(0)
    grad_a(0)
    grad_b(0)
    z3p, z3m = z_pass(2, z2p, z2m)
    a0.fourth()
    b0.fourth()
    a0.fifth()
    b0.fifth()
    a1.fourth()
    b1.fourth()
    a1.fifth()
    b1.fifth()
    drain(len(sent) - 32)

    total_inner = in_own[0:1, :]
    for d, e in enumerate(inners):
        e.wait()
        total_inner = total_inner + in_all[d + 1, 0:1, :]
    scale_row = sct_ref[0:1, :]
    factor = total_inner * scale_row * scale_row * (1.0 / WIDE)
    for e in z3p + z3m:
        e.wait()
    mine = pl.ds(lax.rem(z, 2) * 448, 448)
    ng = ngb[0].astype(F32) + zrp[3].astype(F32) + zrm[3].astype(F32)
    u = ng * wide(gt_ref[mine, :], 2)
    gh_ref[...] = u * scale_row - ht_ref[mine, :].astype(F32) * factor

    for n, part in enumerate((a0, a1, b0, b1)):
        gp_ref[:, n * 256 : (n + 1) * 256] = part.result()
    drain(len(sent))
    assert counter[0] <= EVENTS


def deliver(gp_in, gh_in, gp_out, gh_out, gp, gh, sems):
    into = [pltpu.make_async_copy(gp_in, gp, sems.at[0]), pltpu.make_async_copy(gh_in, gh, sems.at[1])]
    out = [pltpu.make_async_copy(gp, gp_out, sems.at[2]), pltpu.make_async_copy(gh, gh_out, sems.at[3])]
    for copy in into:
        copy.start()
    for first, second in zip(into, out):
        first.wait()
        second.start()
    for copy in out:
        copy.wait()


def vm(shape, dtype=BF16):
    return pltpu.VMEM(shape, dtype)


def body(teacher_query, teacher_key, teacher_value, t_segment, s_hidden, norm_gain, proj_weight, span_start, span_count):
    spec = pl.BlockSpec(memory_space=pltpu.VMEM)
    scratch = [
        vm((T, FEAT)),
        vm((T, WIDE)),
        vm((2, 4, 4, T + 16, 2 * HEAD)),
        vm((4, 4, 2, 112, FEAT)),
        vm((2, 4 * T, 2 * HEAD)),
        vm((2, 4 * T, 128), F32),
        vm((2, 4 * T, 2 * HEAD), F32),
        vm((4 * T, 2 * T)),
        vm((4 * T, 2 * T)),
        vm((512, FEAT)),
        vm((T, WIDE)),
        vm((4, 4, 2, 112, T)),
        vm((4, 4, 112, T)),
        vm((896, T)),
        vm((896, 128), F32),
        vm((T, 128), F32),
        vm((8, T), F32),
        vm((T, FEAT), F32),
        vm((T, FEAT)),
        vm((T, FEAT)),
        vm((8, T), F32),
        vm((8, 8, T), F32),
        vm((8, 448, T)),
        vm((4, 448, T)),
        vm((4, 448, T)),
        vm((4, 4, 4, 112, 256)),
        vm((4, 2, 2, 112, 256)),
        vm((4, 2, 4, 112, 256)),
        vm((4, 4, 112, 256)),
        vm((4, 2, 112, 128)),
        vm((4, 2, 112, 256)),
    ]
    scratch += [pltpu.SemaphoreType.DMA((EVENTS,)), pltpu.SemaphoreType.DMA((EVENTS,)), pltpu.SemaphoreType.DMA((3,))]
    anywhere = pl.BlockSpec(memory_space=pl.ANY)
    grad_proj, grad_hidden = pl.pallas_call(
        kernel,
        out_shape=(jax.ShapeDtypeStruct((112, FEAT), F32), jax.ShapeDtypeStruct((448, T), F32)),
        in_specs=[anywhere, spec, spec, spec, anywhere, spec, anywhere, spec, spec],
        out_specs=(spec, spec),
        scratch_shapes=scratch,
        compiler_params=pltpu.CompilerParams(
            collective_id=0, has_side_effects=True, vmem_limit_bytes=60 * 2**20
        ),
    )(
        teacher_query, teacher_key, teacher_value, t_segment.reshape(1, T), s_hidden,
        norm_gain.reshape(28, 128), proj_weight, span_start.reshape(1, T), span_count.reshape(1, T),
    )
    grad_proj, grad_hidden = pl.pallas_call(
        deliver,
        out_shape=(jax.ShapeDtypeStruct((112, FEAT), F32), jax.ShapeDtypeStruct((448, T), F32)),
        in_specs=[anywhere] * 2,
        out_specs=(anywhere, anywhere),
        scratch_shapes=[vm((112, FEAT), F32), vm((448, T), F32), pltpu.SemaphoreType.DMA((4,))],
        compiler_params=pltpu.CompilerParams(vmem_limit_bytes=60 * 2**20),
    )(grad_proj, grad_hidden)
    return grad_proj, grad_hidden.T


def solution(mesh):
    return jax.shard_map(
        body,
        mesh=mesh,
        in_specs=(
            P("seq", "tp"),
            P("seq", "tp"),
            P("seq", "tp"),
            P("seq"),
            P("seq", None),
            P(),
            P("seq", "tp"),
            P("seq"),
            P("seq"),
        ),
        out_specs=(P("seq", "tp"), P("seq", "tp")),
        check_vma=False,
    )
```

```python
import math

import jax
import jax.numpy as jnp
from jax import lax
from jax.experimental import pallas as pl
from jax.experimental.pallas import tpu as pltpu
from jax.sharding import PartitionSpec as P

MESH = pl.DeviceIdType.MESH
F32, BF16 = jnp.float32, jnp.bfloat16
HEAD = 128
T = 256
WIDE = 3584
FEAT = 1024
BIG = float(2**20)
EXP_SCALE = math.log2(math.e) / math.sqrt(HEAD)
REACH = 12
HALO = 80
EVENTS = 224

NT = (((1,), (1,)), ((), ()))


def dot(a, b):
    return jnp.dot(a, b, preferred_element_type=F32)


def dot_nt(a, b):
    return lax.dot_general(a, b, NT, preferred_element_type=F32)


def kernel(
    q_hbm, k_ref, v_ref, seg_ref, sh_hbm, gain_ref, w_hbm, start_ref, count_ref,
    gp_ref, gh_ref,
    q_ref, sh_ref, kvbuf, wbuf, qa, m_ref, acc_ref, pa_ref, pb_ref, to_ref,
    normed, nt_ref, nsib, ht_ref, gt_ref, sc_ref, sct_ref, p_ref, r_ref, rsib,
    in_own, in_all, ngb, zrp, zrm,
    g_ref, r0_ref, r1_ref, h_ref, s0_ref, s1_ref,
    send_sems, recv_sems, load_sems,
):
    i = lax.axis_index("seq")
    z = lax.axis_index("tp")
    c = lax.rem(i, 2)
    t = lax.div(i, 2)
    y = lax.rem(t, 4)
    x = lax.div(t, 4)
    oc = 1 - c

    def mod4(v):
        return lax.rem(v + 8, 4)

    def seq_dev(xx, yy, cc):
        return {"seq": (xx * 4 + yy) * 2 + cc}

    dev_x = {1: seq_dev(mod4(x + 1), y, c), -1: seq_dev(mod4(x - 1), y, c)}
    dev_y = {1: seq_dev(x, mod4(y + 1), c), -1: seq_dev(x, mod4(y - 1), c)}
    dev_z = {d: {"tp": lax.rem(z + d + 8, 8)} for d in (1, -1)}
    sib = seq_dev(x, y, oc)

    barrier = pltpu.get_barrier_semaphore()
    partners = [dev_x[1], dev_x[-1], dev_y[1], dev_y[-1], sib, {"seq": lax.rem(i + 2 * c + 31, 32)}]
    partners += [{"tp": lax.rem(z + d, 8)} for d in range(1, 8)]
    for device in partners:
        pl.semaphore_signal(barrier, inc=1, device_id=device, device_id_type=MESH)

    loads = [
        pltpu.make_async_copy(sh_hbm, sh_ref, load_sems.at[0]),
        pltpu.make_async_copy(w_hbm, wbuf.at[x, y, c], load_sems.at[1]),
        pltpu.make_async_copy(q_hbm, q_ref, load_sems.at[2]),
    ]
    for load in loads:
        load.start()

    counter = [0]
    sent = []

    class Send:
        def __init__(self, src, dst, device, arrive=None):
            n = counter[0]
            counter[0] += 1
            self.parts = (n, device)
            self.copy = self.make(src, dst)
            self.copy.start()
            sent.append(self.copy)
            self.arrive = dst if arrive is None else arrive

        def make(self, src, dst):
            n, device = self.parts
            return pltpu.make_async_remote_copy(
                src_ref=src, dst_ref=dst, send_sem=send_sems.at[n], recv_sem=recv_sems.at[n],
                device_id=device, device_id_type=MESH,
            )

        def wait(self):
            self.make(self.arrive, self.arrive).wait_recv()

    def drain(count):
        for copy in sent[:count]:
            copy.wait_send()
        del sent[:count]

    class Gather:
        def __init__(self, view, column, a, b, sib_b, dev_a, dev_b):
            self.view, self.column = view, column
            self.a, self.b, self.sib_b, self.dev_a, self.dev_b = a, b, sib_b, dev_a, dev_b
            self.p2, self.f2, self.sibs = {}, {}, []

        def at(self, da, db, part=None):
            return self.view(mod4(self.a + da), mod4(self.b + db), part)

        def to_a(self, sign, da, part=None):
            ref = self.at(da, 0, part)
            return Send(ref, ref, self.dev_a[sign], self.at(da - sign, 0, part))

        def to_b(self, sign, da, db, part=None):
            ref = self.at(da, db, part)
            return Send(ref, ref, self.dev_b[sign], self.at(da, db - sign, part))

        def to_sib(self, db):
            ref = self.column(mod4(self.b + db), c)
            self.sibs.append(Send(ref, ref, sib, self.column(mod4(self.sib_b + db), oc)))

        def stage0(self):
            self.p1 = {s: self.to_a(s, 0) for s in (1, -1)}
            for s in (1, -1):
                self.p2[s, 0] = self.to_b(s, 0, 0)

        def stage1(self):
            self.f1 = {}
            for s, part in ((1, 0), (-1, 1)):
                self.p1[s].wait()
                self.f1[s] = self.to_a(s, -s, part)
                for sb in (1, -1):
                    self.p2[sb, -s] = self.to_b(sb, -s, 0)
            self.forward(0)

        def forward(self, da):
            for s, part in ((1, 0), (-1, 1)):
                self.p2[s, da].wait()
                self.f2[s, da] = self.to_b(s, da, -s, part)

        def stage2(self):
            for s in (1, -1):
                self.f1[s].wait()
            for sb in (1, -1):
                self.p2[sb, 2] = self.to_b(sb, 2, 0)

        def stage2b(self):
            self.forward(-1)
            self.forward(1)

        def stage3(self):
            self.forward(2)

        def stage4(self):
            for key in self.f2:
                self.f2[key].wait()
            self.to_sib(2)

        def stage5(self):
            for s in self.sibs:
                s.wait()

    def kv_view(aa, bb, part):
        if part is None:
            return kvbuf.at[c, aa, bb]
        return kvbuf.at[c, aa, bb, pl.ds((0, 128)[part], (128, 144)[part])]

    def w_view(first, x_first):
        def view(aa, bb, part):
            xx, yy = (aa, bb) if x_first else (bb, aa)
            if part is None:
                return wbuf.at[xx, yy, c, :, pl.ds(first, 512)]
            return wbuf.at[xx, yy, c, :, pl.ds(first + 256 * part, 256)]

        return view

    kv_a, kv_b = oc * x + c * y, oc * y + c * x
    step_a = {d: seq_dev(mod4(x + d * oc), mod4(y + d * c), c) for d in (1, -1)}
    step_b = {d: seq_dev(mod4(x + d * c), mod4(y + d * oc), c) for d in (1, -1)}
    gather_kv = Gather(kv_view, lambda bb, cc: kvbuf.at[cc, :, bb], kv_a, kv_b, kv_a, step_a, step_b)
    def share(da, db):
        ref = gather_kv.at(da, db)
        return Send(ref, ref, sib, kvbuf.at[oc, mod4(kv_b + da), mod4(kv_a + db)])

    gather_w0 = Gather(w_view(0, True), lambda bb, cc: wbuf.at[:, bb, cc, :, pl.ds(0, 512)], x, y, y, dev_x, dev_y)
    gather_w1 = Gather(w_view(512, False), lambda bb, cc: wbuf.at[bb, :, cc, :, pl.ds(512, 512)], y, x, x, dev_y, dev_x)

    seg = seg_ref[...]
    below1 = jnp.sum((seg < 1).astype(F32), axis=1, keepdims=True)
    below2 = jnp.sum((seg < 2).astype(F32), axis=1, keepdims=True)
    strip_row = lax.broadcasted_iota(jnp.int32, (16, 128), 0)
    kvbuf[c, kv_a, kv_b, 0:T, 0:HEAD] = k_ref[...]
    kvbuf[c, kv_a, kv_b, 0:T, HEAD : 2 * HEAD] = v_ref[...]
    strip = jnp.where(strip_row < 8, below1, below2).astype(BF16)
    kvbuf[c, kv_a, kv_b, T : T + 16, :] = jnp.concatenate([strip, strip], axis=1)

    pl.semaphore_wait(barrier, len(partners))

    gather_kv.stage0()
    shared = [share(0, 0)]

    loads[0].wait()
    squares = jnp.zeros((T, 128), F32)
    for piece in range(WIDE // 128):
        h = sh_ref[:, piece * 128 : (piece + 1) * 128].astype(F32)
        squares = squares + h * h
    mean = jnp.sum(squares, axis=1, keepdims=True) * (1.0 / WIDE)
    scale = lax.rsqrt(mean + 1e-6)
    scale_wide = jnp.broadcast_to(scale, (T, 128))
    sc_ref[...] = scale_wide
    sct_ref[...] = jnp.transpose(scale_wide)[0:8, :]

    def norm_piece(piece, carry):
        cols = pl.ds(pl.multiple_of(piece * 896, 128), 896)
        h = sh_ref[:, cols]
        gain = jnp.concatenate([gain_ref[pl.ds(piece * 7 + n, 1), :] for n in range(7)], axis=1)
        value = (h.astype(F32) * sc_ref[:, 0:1] * gain).astype(BF16)
        normed[:, cols] = value
        nt_ref[piece] = jnp.transpose(value).reshape(4, 2, 112, T)

        @pl.when(piece == lax.div(z, 2))
        def _():
            ht_ref[...] = jnp.transpose(h)
            gt_ref[...] = jnp.transpose(jnp.broadcast_to(gain, (128, 896)))

        return carry

    lax.fori_loop(0, 1, norm_piece, 0)
    gather_kv.stage1()
    near_shared = [share(1, 0), share(-1, 0), share(0, 1), share(0, -1)]
    loads[1].wait()
    gather_w0.stage0()
    gather_w1.stage0()
    loads[2].wait()

    doc_row = lax.broadcasted_iota(jnp.int32, (HEAD, T), 0).astype(F32)
    token = lax.broadcasted_iota(jnp.int32, (HEAD, T), 1).astype(F32)
    own_doc = jnp.where(token >= below1, 1.0, 0.0) + jnp.where(token >= below2, 1.0, 0.0)
    one_hot = jnp.where(own_doc == doc_row, 1.0, 0.0).astype(BF16)
    for h in range(8):
        at = pl.ds((h % 4) * T, T)
        qa[h // 4, 0:HEAD, at] = jnp.transpose(q_ref[:, h * HEAD : (h + 1) * HEAD])
        qa[h // 4, HEAD : 2 * HEAD, at] = one_hot

    key_row = lax.broadcasted_iota(jnp.int32, (T, HEAD), 0).astype(F32)
    doc_lane = lax.broadcasted_iota(jnp.int32, (T, HEAD), 1).astype(F32)

    def blocks(tt):
        xx, yy = lax.div(tt, 4), lax.rem(tt, 4)
        return kvbuf.at[0, xx, yy], kvbuf.at[1, yy, xx]

    def keys_of(tt):
        sides = []
        for block in blocks(tt):
            strip = block[T : T + 16, 0:HEAD].astype(F32)
            doc = jnp.where(key_row >= strip[0:1, :], 1.0, 0.0) + jnp.where(key_row >= strip[8:9, :], 1.0, 0.0)
            bias = jnp.where(doc == doc_lane, 0.0, -BIG).astype(BF16)
            sides.append(jnp.concatenate([block[0:T, 0:HEAD], bias], axis=1))
        return jnp.concatenate(sides, axis=0)

    ones = jnp.ones((16, 2 * T), BF16)

    def wide(v, n):
        return jnp.concatenate([v] * n, axis=1)

    def values_of(tt):
        v = jnp.concatenate([jnp.transpose(block[0:T, HEAD : 2 * HEAD]) for block in blocks(tt)], axis=1)
        return jnp.concatenate([v, ones], axis=0)

    def soften(group, scores, weights, own):
        factors = []
        for piece in range(8):
            at = slice(piece * 128, (piece + 1) * 128)
            s = scores[:, at]
            if own:
                row = lax.broadcasted_iota(jnp.int32, (2 * T, 128), 0)
                col = lax.broadcasted_iota(jnp.int32, (2 * T, 128), 1) + (piece % 2) * 128
                s = jnp.where(row <= col + c * T, s, -2.0 * BIG)
                m = jnp.max(s, axis=0, keepdims=True)
            else:
                m_old = m_ref[group, 0:1, at]
                m = jnp.maximum(m_old, jnp.max(s, axis=0, keepdims=True))
                factors.append(jnp.exp2((m_old - m) * EXP_SCALE))
            weights[:, at] = jnp.exp2(((s - m) * EXP_SCALE).astype(BF16))
            m_ref[group, 0:1, at] = m
        return factors

    def gather_values(group, weights, values, factors):
        update = dot(values, weights[...])
        if not factors:
            acc_ref[group] = update
            return
        for piece, factor in enumerate(factors):
            at = slice(piece * 128, (piece + 1) * 128)
            acc_ref[group, :, at] = acc_ref[group, :, at] * factor + update[:, at]

    def attend_chip(tt, own):
        keys, values = keys_of(tt), values_of(tt)
        s_a = dot(keys, qa[0])
        s_b = dot(keys, qa[1])
        factors_a = soften(0, s_a, pa_ref, own)
        gather_values(0, pa_ref, values, factors_a)
        factors_b = soften(1, s_b, pb_ref, own)
        gather_values(1, pb_ref, values, factors_b)

    def near(n):
        n = n + jnp.where(n >= 4, 1, 0)
        return lax.div(n, 3) - 1, lax.rem(n, 3) - 1

    def far(n):
        return jnp.where(n < 4, 2, n - 5), jnp.where(n < 4, n, 2)

    def attend(place, low, high):
        def step(n, carry):
            dx, dy = place(n)
            tt = mod4(x + dx) * 4 + mod4(y + dy)

            @pl.when((tt < t) & (tt >= t - REACH))
            def _():
                attend_chip(tt, False)

            return carry

        lax.fori_loop(low, high, step, 0)

    def finish():
        for h in range(8):
            at = pl.ds((h % 4) * T, T)
            out = acc_ref[h // 4, 0:HEAD, at] / acc_ref[h // 4, HEAD : HEAD + 1, at]
            to_ref[128 : 128 + T, h * HEAD : (h + 1) * HEAD] = jnp.transpose(out.astype(BF16))
        last = Send(
            to_ref.at[pl.ds(128 + T - HALO, HALO)], to_ref.at[pl.ds(128 - HALO, HALO)],
            {"seq": lax.rem(i + 1, 32)},
        )
        first = Send(
            to_ref.at[pl.ds(128, HALO)], to_ref.at[pl.ds(128 + T, HALO)],
            {"seq": lax.rem(i + 31, 32)},
        )
        return [last, first]

    def column(ref):
        return jnp.transpose(jnp.broadcast_to(ref[...].astype(F32), (128, T)))

    to_ref[0 : 128 - HALO, :] = jnp.zeros((128 - HALO, FEAT), BF16)
    to_ref[128 + T + HALO : 512, :] = jnp.zeros((128 - HALO, FEAT), BF16)
    span_start = column(start_ref)
    span_count = column(count_ref)
    inverse_count = 1.0 / span_count
    first_row = (i * T - 128).astype(F32)
    row_id = lax.broadcasted_iota(jnp.int32, (T, 512), 1).astype(F32) + first_row
    begin, end = wide(span_start, 4), wide(span_start + span_count, 4)
    select = jnp.where((row_id >= begin) & (row_id < end), 1.0, 0.0).astype(BF16)

    gather_kv.stage2()
    far_shared = [share(2, 0)]
    shared[0].wait()
    attend_chip(t, True)
    gather_kv.stage2b()
    near_shared += [share(da, db) for da in (1, -1) for db in (1, -1)]
    lax.fori_loop(1, 4, norm_piece, 0)
    send_nt = Send(nt_ref.at[:, :, oc], nsib, sib)
    for s in near_shared:
        s.wait()
    gather_w0.stage1()
    gather_w1.stage1()
    attend(near, 0, 2)
    gather_kv.stage3()
    far_shared += [share(2, 1), share(2, -1)]
    attend(near, 2, 4)
    for gather in (gather_w0, gather_w1):
        gather.stage2()
        gather.to_sib(0)
    attend(near, 4, 6)
    gather_kv.stage4()
    gather_w0.stage2b()
    gather_w1.stage2b()
    attend(near, 6, 8)
    for s in far_shared:
        s.wait()
    gather_kv.stage5()
    for gather in (gather_w0, gather_w1):
        gather.stage3()
        gather.to_sib(-1)
        gather.to_sib(1)
    attend(far, 0, 3)
    gather_w0.stage4()
    gather_w1.stage4()
    attend(far, 3, 7)
    gathered = len(sent)
    halos = finish()
    gather_w0.stage5()
    gather_w1.stage5()

    def predict(piece, carry):
        cols = pl.ds(pl.multiple_of(piece * 256, 256), 256)
        total = jnp.zeros((T, 256), F32)
        for xx in range(4):
            total = total + dot(normed[:, xx * 896 : (xx + 1) * 896], wbuf[xx, :, :, :, cols].reshape(896, 256))
        p_ref[:, cols] = total
        return carry

    lax.fori_loop(0, 4, predict, 0)
    for s in halos:
        s.wait()

    inner = jnp.zeros((T, 128), F32)
    send_r = []
    for piece in range(4):
        cols = slice(piece * 256, (piece + 1) * 256)
        target = dot(select, to_ref[:, cols]) * wide(inverse_count, 2)
        prediction = p_ref[:, cols]
        residual = (prediction - target).astype(BF16)
        r_ref[:, cols] = residual
        product = residual.astype(F32) * prediction
        inner = inner + product[:, 0:128] + product[:, 128:256]
        if piece % 2 == 1:
            half = pl.ds((piece - 1) * 256, 512)
            send_r.append(Send(r_ref.at[:, half], rsib.at[:, half], sib))
    inner = jnp.broadcast_to(jnp.sum(inner, axis=1, keepdims=True), (T, 128))
    in_own[...] = jnp.transpose(inner)[0:8, :]
    inners = [Send(in_own, in_all.at[d], {"tp": lax.rem(z + d, 8)}) for d in range(1, 8)]

    def normed_grad(d):
        zz = lax.rem(z + d, 8)
        w = wbuf[lax.div(zz, 2), pl.ds(lax.rem(zz, 2) * 2, 2)].reshape(448, FEAT)
        ngb[d] = dot_nt(w, r_ref[...]).astype(BF16)

    lo, hi = pl.ds(0, 224), pl.ds(224, 224)

    def z_send(step, sign, rows_):
        d = (4 - step if sign == 1 else 4 + step)
        box = zrp if sign == 1 else zrm
        return Send(ngb.at[d, rows_], box.at[step, rows_], dev_z[sign])

    def z_add(step, sign, rows_):
        d = (3 - step if sign == 1 else 5 + step)
        box = zrp if sign == 1 else zrm
        ngb[d, rows_] = (ngb[d, rows_].astype(F32) + box[step, rows_].astype(F32)).astype(BF16)

    normed_grad(4)
    z0p, z0m = z_send(0, 1, lo), z_send(0, -1, hi)

    send_nt.wait()
    send_r[0].wait()

    def grad_a(d):
        yy = mod4(y + d)
        left = nt_ref[:, yy, c].reshape(448, T)
        left_sib = nsib[:, yy].reshape(448, T)
        block = dot(left, r_ref[:, 0:512]) + dot(left_sib, rsib[:, 0:512])
        block = block.astype(BF16)
        g_ref[0, d] = block[:, 0:256].reshape(4, 112, 256)
        g_ref[1, d] = block[:, 256:512].reshape(4, 112, 256)

    def grad_b(d):
        xx = mod4(x + d)
        left = nt_ref[xx, :, c].reshape(448, T)
        left_sib = nsib[xx].reshape(448, T)
        block = dot(left, r_ref[:, 512:1024]) + dot(left_sib, rsib[:, 512:1024])
        block = block.astype(BF16)
        g_ref[2, d] = block[:, 0:256].reshape(4, 112, 256)
        g_ref[3, d] = block[:, 256:512].reshape(4, 112, 256)

    two, four = pl.ds(0, 2), pl.ds(2, 2)

    class Scatter:
        def __init__(self, n, dev_a, dev_b, b):
            self.g, self.h = g_ref.at[n], h_ref.at[n]
            self.r0 = {1: r0_ref.at[n, 0], -1: r0_ref.at[n, 1]}
            self.r1 = {1: r1_ref.at[n, 0], -1: r1_ref.at[n, 1]}
            self.s0 = {1: s0_ref.at[n, 0], -1: s0_ref.at[n, 1]}
            self.s1 = {1: s1_ref.at[n, 0], -1: s1_ref.at[n, 1]}
            self.dev_a, self.dev_b, self.b = dev_a, dev_b, b
            self.part = {1: two, -1: four}
            self.cols = {1: pl.ds(0, 128), -1: pl.ds(128, 128)}

        def first(self):
            self.e0 = {s: Send(self.g.at[2, self.part[s]], self.r0[s], self.dev_a[s]) for s in (1, -1)}

        def second(self):
            self.e1 = {}
            for s, d in ((1, 1), (-1, 3)):
                part = self.part[-s]
                self.e1[s] = [Send(self.g.at[d, part], self.r1[s].at[part], self.dev_a[s])]

        def third(self):
            for s, d in ((1, 1), (-1, 3)):
                part = self.part[s]
                self.e0[s].wait()
                self.g[d, part] = (self.g[d, part].astype(F32) + self.r0[s][...].astype(F32)).astype(BF16)
                self.e1[s].append(Send(self.g.at[d, part], self.r1[s].at[part], self.dev_a[s]))

        def fourth(self):
            for s in (1, -1):
                for e in self.e1[s]:
                    e.wait()
            self.h[...] = (
                self.g[0].astype(F32) + self.r1[1][...].astype(F32) + self.r1[-1][...].astype(F32)
            ).astype(BF16)
            far = mod4(self.b + 2)
            self.f0, self.f1 = {}, {}
            for s in (1, -1):
                self.f0[s] = Send(self.h.at[far, :, self.cols[s]], self.s0[s], self.dev_b[s])
            for s in (1, -1):
                cols = self.cols[-s]
                self.f1[s] = [Send(self.h.at[mod4(self.b + s), :, cols], self.s1[s].at[:, cols], self.dev_b[s])]

        def fifth(self):
            for s in (1, -1):
                cols, near = self.cols[s], mod4(self.b + s)
                self.f0[s].wait()
                self.h[near, :, cols] = (
                    self.h[near, :, cols].astype(F32) + self.s0[s][...].astype(F32)
                ).astype(BF16)
                self.f1[s].append(Send(self.h.at[near, :, cols], self.s1[s].at[:, cols], self.dev_b[s]))

        def result(self):
            for s in (1, -1):
                for e in self.f1[s]:
                    e.wait()
            return self.h[self.b].astype(F32) + self.s1[1][...].astype(F32) + self.s1[-1][...].astype(F32)

    a0, a1 = Scatter(0, dev_y, dev_x, x), Scatter(1, dev_y, dev_x, x)
    b0, b1 = Scatter(2, dev_x, dev_y, y), Scatter(3, dev_x, dev_y, y)

    def z_half(step, n, plus, minus):
        rows_p, rows_m = (hi, lo)[n], (lo, hi)[n]
        plus[n].wait()
        z_add(step, 1, rows_p)
        out_p = z_send(step + 1, 1, rows_p)
        minus[n].wait()
        z_add(step, -1, rows_m)
        return out_p, z_send(step + 1, -1, rows_m)

    grad_a(2)
    a0.first()
    send_r[1].wait()
    grad_b(2)
    b0.first()
    a1.first()
    b1.first()
    normed_grad(3)
    z1p = [z_send(1, 1, hi)]
    normed_grad(5)
    z1m = [z_send(1, -1, lo)]
    grad_a(1)
    grad_a(3)
    a0.second()
    z0p.wait()
    z_add(0, 1, lo)
    z1p.append(z_send(1, 1, lo))
    z0m.wait()
    z_add(0, -1, hi)
    z1m.append(z_send(1, -1, hi))
    grad_b(1)
    grad_b(3)
    b0.second()
    normed_grad(2)
    normed_grad(6)
    a0.third()
    b0.third()
    a1.second()
    b1.second()
    z2 = [z_half(1, 0, z1p, z1m)]
    a1.third()
    b1.third()
    z2.append(z_half(1, 1, z1p, z1m))
    z2p, z2m = zip(*z2)
    normed_grad(1)
    normed_grad(7)
    grad_a(0)
    grad_b(0)
    normed_grad(0)
    drain(gathered)
    z3 = [z_half(2, 0, z2p, z2m)]
    a0.fourth()
    b0.fourth()
    z3.append(z_half(2, 1, z2p, z2m))
    a0.fifth()
    b0.fifth()
    a1.fourth()
    b1.fourth()
    a1.fifth()
    b1.fifth()
    drain(len(sent) - 32)

    total_inner = in_own[0:1, :]
    for d, e in enumerate(inners):
        e.wait()
        total_inner = total_inner + in_all[d + 1, 0:1, :]
    scale_row = sct_ref[0:1, :]
    factor = total_inner * scale_row * scale_row * (1.0 / WIDE)
    for pair in z3:
        for e in pair:
            e.wait()
    mine = pl.ds(lax.rem(z, 2) * 448, 448)
    ng = ngb[0].astype(F32) + zrp[3].astype(F32) + zrm[3].astype(F32)
    u = ng * wide(gt_ref[mine, :], 2)
    gh_ref[...] = u * scale_row - ht_ref[mine, :].astype(F32) * factor

    for n, part in enumerate((a0, a1, b0, b1)):
        gp_ref[:, n * 256 : (n + 1) * 256] = part.result()
    drain(len(sent))
    assert counter[0] <= EVENTS


def deliver(gp_in, gh_in, gp_out, gh_out, gp, gh, sems):
    into = [pltpu.make_async_copy(gp_in, gp, sems.at[0]), pltpu.make_async_copy(gh_in, gh, sems.at[1])]
    out = [pltpu.make_async_copy(gp, gp_out, sems.at[2]), pltpu.make_async_copy(gh, gh_out, sems.at[3])]
    for copy in into:
        copy.start()
    for first, second in zip(into, out):
        first.wait()
        second.start()
    for copy in out:
        copy.wait()


def vm(shape, dtype=BF16):
    return pltpu.VMEM(shape, dtype)


def body(teacher_query, teacher_key, teacher_value, t_segment, s_hidden, norm_gain, proj_weight, span_start, span_count):
    spec = pl.BlockSpec(memory_space=pltpu.VMEM)
    scratch = [
        vm((T, FEAT)),
        vm((T, WIDE)),
        vm((2, 4, 4, T + 16, 2 * HEAD)),
        vm((4, 4, 2, 112, FEAT)),
        vm((2, 2 * HEAD, 4 * T)),
        vm((2, 8, 4 * T), F32),
        vm((2, HEAD + 16, 4 * T), F32),
        vm((2 * T, 4 * T)),
        vm((2 * T, 4 * T)),
        vm((512, FEAT)),
        vm((T, WIDE)),
        vm((4, 4, 2, 112, T)),
        vm((4, 4, 112, T)),
        vm((896, T)),
        vm((896, 128), F32),
        vm((T, 128), F32),
        vm((8, T), F32),
        vm((T, FEAT), F32),
        vm((T, FEAT)),
        vm((T, FEAT)),
        vm((8, T), F32),
        vm((8, 8, T), F32),
        vm((8, 448, T)),
        vm((4, 448, T)),
        vm((4, 448, T)),
        vm((4, 4, 4, 112, 256)),
        vm((4, 2, 2, 112, 256)),
        vm((4, 2, 4, 112, 256)),
        vm((4, 4, 112, 256)),
        vm((4, 2, 112, 128)),
        vm((4, 2, 112, 256)),
    ]
    scratch += [pltpu.SemaphoreType.DMA((EVENTS,)), pltpu.SemaphoreType.DMA((EVENTS,)), pltpu.SemaphoreType.DMA((3,))]
    anywhere = pl.BlockSpec(memory_space=pl.ANY)
    grad_proj, grad_hidden = pl.pallas_call(
        kernel,
        out_shape=(jax.ShapeDtypeStruct((112, FEAT), F32), jax.ShapeDtypeStruct((448, T), F32)),
        in_specs=[anywhere, spec, spec, spec, anywhere, spec, anywhere, spec, spec],
        out_specs=(spec, spec),
        scratch_shapes=scratch,
        compiler_params=pltpu.CompilerParams(
            collective_id=0, has_side_effects=True, vmem_limit_bytes=60 * 2**20
        ),
    )(
        teacher_query, teacher_key, teacher_value, t_segment.reshape(1, T), s_hidden,
        norm_gain.reshape(28, 128), proj_weight, span_start.reshape(1, T), span_count.reshape(1, T),
    )
    grad_proj, grad_hidden = pl.pallas_call(
        deliver,
        out_shape=(jax.ShapeDtypeStruct((112, FEAT), F32), jax.ShapeDtypeStruct((448, T), F32)),
        in_specs=[anywhere] * 2,
        out_specs=(anywhere, anywhere),
        scratch_shapes=[vm((112, FEAT), F32), vm((448, T), F32), pltpu.SemaphoreType.DMA((4,))],
        compiler_params=pltpu.CompilerParams(vmem_limit_bytes=60 * 2**20),
    )(grad_proj, grad_hidden)
    return grad_proj, grad_hidden.T


def solution(mesh):
    return jax.shard_map(
        body,
        mesh=mesh,
        in_specs=(
            P("seq", "tp"),
            P("seq", "tp"),
            P("seq", "tp"),
            P("seq"),
            P("seq", None),
            P(),
            P("seq", "tp"),
            P("seq"),
            P("seq"),
        ),
        out_specs=(P("seq", "tp"), P("seq", "tp")),
        check_vma=False,
    )
```

```python
import math

import jax
import jax.numpy as jnp
from jax import lax
from jax.experimental import pallas as pl
from jax.experimental.pallas import tpu as pltpu
from jax.sharding import PartitionSpec as P

MESH = pl.DeviceIdType.MESH
F32, BF16 = jnp.float32, jnp.bfloat16
HEAD = 128
T = 256
WIDE = 3584
FEAT = 1024
BIG = float(2**20)
EXP_SCALE = math.log2(math.e) / math.sqrt(HEAD)
REACH = 12
HALO = 80
EVENTS = 224

NT = (((1,), (1,)), ((), ()))


def dot(a, b):
    return jnp.dot(a, b, preferred_element_type=F32)


def dot_nt(a, b):
    return lax.dot_general(a, b, NT, preferred_element_type=F32)


def kernel(
    q_hbm, k_ref, v_ref, seg_ref, sh_hbm, gain_ref, w_hbm, start_ref, count_ref,
    gp_ref, gh_ref,
    q_ref, sh_ref, kvbuf, wbuf, qa, m_ref, acc_ref, pa_ref, pb_ref, to_ref,
    normed, nt_ref, nsib, ht_ref, gt_ref, sc_ref, sct_ref, p_ref, r_ref, rsib,
    in_own, in_all, ngb, zrp, zrm,
    g_ref, r0_ref, r1_ref, h_ref, s0_ref, s1_ref,
    send_sems, recv_sems, load_sems,
):
    i = lax.axis_index("seq")
    z = lax.axis_index("tp")
    c = lax.rem(i, 2)
    t = lax.div(i, 2)
    y = lax.rem(t, 4)
    x = lax.div(t, 4)
    oc = 1 - c

    def mod4(v):
        return lax.rem(v + 8, 4)

    def seq_dev(xx, yy, cc):
        return {"seq": (xx * 4 + yy) * 2 + cc}

    dev_x = {1: seq_dev(mod4(x + 1), y, c), -1: seq_dev(mod4(x - 1), y, c)}
    dev_y = {1: seq_dev(x, mod4(y + 1), c), -1: seq_dev(x, mod4(y - 1), c)}
    dev_z = {d: {"tp": lax.rem(z + d + 8, 8)} for d in (1, -1)}
    sib = seq_dev(x, y, oc)

    barrier = pltpu.get_barrier_semaphore()
    partners = [dev_x[1], dev_x[-1], dev_y[1], dev_y[-1], sib, {"seq": lax.rem(i + 2 * c + 31, 32)}]
    partners += [{"tp": lax.rem(z + d, 8)} for d in range(1, 8)]
    for device in partners:
        pl.semaphore_signal(barrier, inc=1, device_id=device, device_id_type=MESH)

    loads = [
        pltpu.make_async_copy(sh_hbm, sh_ref, load_sems.at[0]),
        pltpu.make_async_copy(w_hbm, wbuf.at[x, y, c], load_sems.at[1]),
        pltpu.make_async_copy(q_hbm, q_ref, load_sems.at[2]),
    ]
    for load in loads:
        load.start()

    counter = [0]
    sent = []

    class Send:
        def __init__(self, src, dst, device, arrive=None):
            n = counter[0]
            counter[0] += 1
            self.parts = (n, device)
            self.copy = self.make(src, dst)
            self.copy.start()
            sent.append(self.copy)
            self.arrive = dst if arrive is None else arrive

        def make(self, src, dst):
            n, device = self.parts
            return pltpu.make_async_remote_copy(
                src_ref=src, dst_ref=dst, send_sem=send_sems.at[n], recv_sem=recv_sems.at[n],
                device_id=device, device_id_type=MESH,
            )

        def wait(self):
            self.make(self.arrive, self.arrive).wait_recv()

    def drain(count):
        for copy in sent[:count]:
            copy.wait_send()
        del sent[:count]

    class Gather:
        def __init__(self, view, column, a, b, sib_b, dev_a, dev_b):
            self.view, self.column = view, column
            self.a, self.b, self.sib_b, self.dev_a, self.dev_b = a, b, sib_b, dev_a, dev_b
            self.p2, self.f2, self.sibs = {}, {}, []

        def at(self, da, db, part=None):
            return self.view(mod4(self.a + da), mod4(self.b + db), part)

        def to_a(self, sign, da, part=None):
            ref = self.at(da, 0, part)
            return Send(ref, ref, self.dev_a[sign], self.at(da - sign, 0, part))

        def to_b(self, sign, da, db, part=None):
            ref = self.at(da, db, part)
            return Send(ref, ref, self.dev_b[sign], self.at(da, db - sign, part))

        def to_sib(self, db):
            ref = self.column(mod4(self.b + db), c)
            self.sibs.append(Send(ref, ref, sib, self.column(mod4(self.sib_b + db), oc)))

        def stage0(self):
            self.p1 = {s: self.to_a(s, 0) for s in (1, -1)}
            for s in (1, -1):
                self.p2[s, 0] = self.to_b(s, 0, 0)

        def stage1(self):
            self.f1 = {}
            for s, part in ((1, 0), (-1, 1)):
                self.p1[s].wait()
                self.f1[s] = self.to_a(s, -s, part)
                for sb in (1, -1):
                    self.p2[sb, -s] = self.to_b(sb, -s, 0)
            self.forward(0)

        def forward(self, da):
            for s, part in ((1, 0), (-1, 1)):
                self.p2[s, da].wait()
                self.f2[s, da] = self.to_b(s, da, -s, part)

        def stage2(self):
            for s in (1, -1):
                self.f1[s].wait()
            for sb in (1, -1):
                self.p2[sb, 2] = self.to_b(sb, 2, 0)

        def stage2b(self):
            self.forward(-1)
            self.forward(1)

        def stage3(self):
            self.forward(2)

        def stage4(self):
            for key in self.f2:
                self.f2[key].wait()
            self.to_sib(2)

        def stage4_by_shard(self):
            for da in (0, -1, 1, 2):
                for sign in (1, -1):
                    self.f2[sign, da].wait()
                at = mod4(self.a + da), mod4(self.b + 2)
                ref = self.view(*at, None)
                self.sibs.append(Send(ref, ref, sib, self.view(*at, None, oc)))

        def stage5(self):
            for s in self.sibs:
                s.wait()

    def kv_view(aa, bb, part):
        if part is None:
            return kvbuf.at[c, aa, bb]
        return kvbuf.at[c, aa, bb, pl.ds((0, 128)[part], (128, 144)[part])]

    def w_view(first, x_first):
        def view(aa, bb, part, core=c):
            xx, yy = (aa, bb) if x_first else (bb, aa)
            if part is None:
                return wbuf.at[xx, yy, core, :, pl.ds(first, 512)]
            return wbuf.at[xx, yy, core, :, pl.ds(first + 256 * part, 256)]

        return view

    kv_a, kv_b = oc * x + c * y, oc * y + c * x
    step_a = {d: seq_dev(mod4(x + d * oc), mod4(y + d * c), c) for d in (1, -1)}
    step_b = {d: seq_dev(mod4(x + d * c), mod4(y + d * oc), c) for d in (1, -1)}
    gather_kv = Gather(kv_view, lambda bb, cc: kvbuf.at[cc, :, bb], kv_a, kv_b, kv_a, step_a, step_b)
    def share(da, db):
        ref = gather_kv.at(da, db)
        return Send(ref, ref, sib, kvbuf.at[oc, mod4(kv_b + da), mod4(kv_a + db)])

    gather_w0 = Gather(w_view(0, True), lambda bb, cc: wbuf.at[:, bb, cc, :, pl.ds(0, 512)], x, y, y, dev_x, dev_y)
    gather_w1 = Gather(w_view(512, False), lambda bb, cc: wbuf.at[bb, :, cc, :, pl.ds(512, 512)], y, x, x, dev_y, dev_x)

    seg = seg_ref[...]
    below1 = jnp.sum((seg < 1).astype(F32), axis=1, keepdims=True)
    below2 = jnp.sum((seg < 2).astype(F32), axis=1, keepdims=True)
    strip_row = lax.broadcasted_iota(jnp.int32, (16, 128), 0)
    kvbuf[c, kv_a, kv_b, 0:T, 0:HEAD] = k_ref[...]
    kvbuf[c, kv_a, kv_b, 0:T, HEAD : 2 * HEAD] = v_ref[...]
    strip = jnp.where(strip_row < 8, below1, below2).astype(BF16)
    kvbuf[c, kv_a, kv_b, T : T + 16, :] = jnp.concatenate([strip, strip], axis=1)

    pl.semaphore_wait(barrier, len(partners))

    gather_kv.stage0()
    shared = [share(0, 0)]

    loads[0].wait()
    squares = jnp.zeros((T, 128), F32)
    for piece in range(WIDE // 128):
        h = sh_ref[:, piece * 128 : (piece + 1) * 128].astype(F32)
        squares = squares + h * h
    mean = jnp.sum(squares, axis=1, keepdims=True) * (1.0 / WIDE)
    scale = lax.rsqrt(mean + 1e-6)
    scale_wide = jnp.broadcast_to(scale, (T, 128))
    sc_ref[...] = scale_wide
    sct_ref[...] = jnp.transpose(scale_wide)[0:8, :]

    def norm_piece(piece, carry):
        cols = pl.ds(pl.multiple_of(piece * 896, 128), 896)
        h = sh_ref[:, cols]
        gain = jnp.concatenate([gain_ref[pl.ds(piece * 7 + n, 1), :] for n in range(7)], axis=1)
        value = (h.astype(F32) * sc_ref[:, 0:1] * gain).astype(BF16)
        normed[:, cols] = value
        nt_ref[piece] = jnp.transpose(value).reshape(4, 2, 112, T)

        @pl.when(piece == lax.div(z, 2))
        def _():
            ht_ref[...] = jnp.transpose(h)
            gt_ref[...] = jnp.transpose(jnp.broadcast_to(gain, (128, 896)))

        return carry

    lax.fori_loop(0, 1, norm_piece, 0)
    gather_kv.stage1()
    near_shared = [share(1, 0), share(-1, 0), share(0, 1), share(0, -1)]
    loads[1].wait()
    gather_w0.stage0()
    gather_w1.stage0()
    loads[2].wait()

    rows = lax.broadcasted_iota(jnp.int32, (T, 128), 0).astype(F32)
    lanes = lax.broadcasted_iota(jnp.int32, (T, 128), 1).astype(F32)

    def doc_of(n1, n2):
        return jnp.where(rows >= n1, 1.0, 0.0) + jnp.where(rows >= n2, 1.0, 0.0)

    one_hot = jnp.where(doc_of(below1, below2) == lanes, 1.0, 0.0).astype(BF16)
    for h in range(8):
        at = pl.ds((h % 4) * T, T)
        qa[h // 4, at, 0:HEAD] = q_ref[:, h * HEAD : (h + 1) * HEAD]
        qa[h // 4, at, HEAD : 2 * HEAD] = one_hot

    doc_id = lax.broadcasted_iota(jnp.int32, (16, T), 0).astype(F32)
    key_id = lax.broadcasted_iota(jnp.int32, (16, T), 1).astype(F32)

    def blocks(tt):
        xx, yy = lax.div(tt, 4), lax.rem(tt, 4)
        return kvbuf.at[0, xx, yy], kvbuf.at[1, yy, xx]

    def keys_of(tt):
        sides = []
        for block in blocks(tt):
            strip = block[T : T + 16, 0:HEAD].astype(F32)
            doc = jnp.where(key_id >= strip[0:1, 0:1], 1.0, 0.0) + jnp.where(key_id >= strip[8:9, 0:1], 1.0, 0.0)
            bias = jnp.where(doc == doc_id, 0.0, -BIG).astype(BF16)
            rest = jnp.zeros((HEAD - 16, T), BF16)
            sides.append(jnp.concatenate([jnp.transpose(block[0:T, 0:HEAD]), bias, rest], axis=0))
        return jnp.concatenate(sides, axis=1)

    ones = jnp.ones((2 * T, HEAD), BF16)

    def wide(v, n):
        return jnp.concatenate([v] * n, axis=1)

    def values_of(tt):
        v = jnp.concatenate([block[0:T, HEAD : 2 * HEAD] for block in blocks(tt)], axis=0)
        return jnp.concatenate([v, ones], axis=1)

    def soften(group, scores, weights, own):
        factors = []
        for piece in range(8):
            at = slice(piece * 128, (piece + 1) * 128)
            s = scores[at, :]
            if own:
                row = lax.broadcasted_iota(jnp.int32, (128, 2 * T), 0) + (piece % 2) * 128
                col = lax.broadcasted_iota(jnp.int32, (128, 2 * T), 1)
                s = jnp.where(col <= row + c * T, s, -2.0 * BIG)
                m = jnp.broadcast_to(jnp.max(s, axis=1, keepdims=True), (128, 128))
            else:
                m_old = m_ref[group, at, :]
                m = jnp.maximum(m_old, jnp.max(s, axis=1, keepdims=True))
                factors.append(jnp.exp2((m_old - m) * EXP_SCALE))
            weights[at, :] = jnp.exp2(((s - wide(m, 4)) * EXP_SCALE).astype(BF16))
            m_ref[group, at, :] = m
        return factors

    def gather_values(group, weights, values, factors):
        update = dot(weights[...], values)
        if not factors:
            acc_ref[group] = update
            return
        for piece, factor in enumerate(factors):
            at = slice(piece * 128, (piece + 1) * 128)
            acc_ref[group, at, :] = acc_ref[group, at, :] * wide(factor, 2) + update[at, :]

    def attend_chip(tt, own):
        keys, values = keys_of(tt), values_of(tt)
        s_a = dot(qa[0], keys)
        s_b = dot(qa[1], keys)
        factors_a = soften(0, s_a, pa_ref, own)
        gather_values(0, pa_ref, values, factors_a)
        factors_b = soften(1, s_b, pb_ref, own)
        gather_values(1, pb_ref, values, factors_b)

    def near(n):
        n = n + jnp.where(n >= 4, 1, 0)
        return lax.div(n, 3) - 1, lax.rem(n, 3) - 1

    def far(n):
        return jnp.where(n < 4, 2, n - 5), jnp.where(n < 4, n, 2)

    def attend(place, low, high):
        def step(n, carry):
            dx, dy = place(n)
            tt = mod4(x + dx) * 4 + mod4(y + dy)

            @pl.when((tt < t) & (tt >= t - REACH))
            def _():
                attend_chip(tt, False)

            return carry

        lax.fori_loop(low, high, step, 0)

    def finish():
        for h in range(8):
            acc = acc_ref[h // 4, pl.ds((h % 4) * T, T), :]
            out = (acc[:, 0:HEAD] / acc[:, HEAD : 2 * HEAD]).astype(BF16)
            to_ref[128 : 128 + T, h * HEAD : (h + 1) * HEAD] = out
        last = Send(
            to_ref.at[pl.ds(128 + T - HALO, HALO)], to_ref.at[pl.ds(128 - HALO, HALO)],
            {"seq": lax.rem(i + 1, 32)},
        )
        first = Send(
            to_ref.at[pl.ds(128, HALO)], to_ref.at[pl.ds(128 + T, HALO)],
            {"seq": lax.rem(i + 31, 32)},
        )
        return [last, first]

    def column(ref):
        return jnp.transpose(jnp.broadcast_to(ref[...].astype(F32), (128, T)))

    to_ref[0 : 128 - HALO, :] = jnp.zeros((128 - HALO, FEAT), BF16)
    to_ref[128 + T + HALO : 512, :] = jnp.zeros((128 - HALO, FEAT), BF16)
    span_start = column(start_ref)
    span_count = column(count_ref)
    inverse_count = 1.0 / span_count
    first_row = (i * T - 128).astype(F32)
    row_id = lax.broadcasted_iota(jnp.int32, (T, 512), 1).astype(F32) + first_row
    begin, end = wide(span_start, 4), wide(span_start + span_count, 4)
    select = jnp.where((row_id >= begin) & (row_id < end), 1.0, 0.0).astype(BF16)

    gather_kv.stage2()
    far_shared = [share(2, 0)]
    shared[0].wait()
    attend_chip(t, True)
    gather_kv.stage2b()
    near_shared += [share(da, db) for da in (1, -1) for db in (1, -1)]
    lax.fori_loop(1, 4, norm_piece, 0)
    send_nt = Send(nt_ref.at[:, :, oc], nsib, sib)
    for s in near_shared:
        s.wait()
    gather_w0.stage1()
    gather_w1.stage1()
    attend(near, 0, 2)
    gather_kv.stage3()
    far_shared += [share(2, 1), share(2, -1)]
    attend(near, 2, 4)
    for gather in (gather_w0, gather_w1):
        gather.stage2()
        gather.to_sib(0)
    attend(near, 4, 6)
    gather_kv.stage4()
    gather_w0.stage2b()
    gather_w1.stage2b()
    attend(near, 6, 8)
    for s in far_shared:
        s.wait()
    gather_kv.stage5()
    for gather in (gather_w0, gather_w1):
        gather.stage3()
        gather.to_sib(-1)
        gather.to_sib(1)
    attend(far, 0, 3)
    attend(far, 3, 5)
    gather_w0.stage4_by_shard()
    gather_w1.stage4_by_shard()
    attend(far, 5, 7)
    gathered = len(sent)
    halos = finish()

    def predict_rows(xx, cols):
        rows = pl.ds(pl.multiple_of(xx * 896, 128), 896)
        return dot(normed[:, rows], wbuf[xx, :, :, :, cols].reshape(896, 256))

    def predict_second(rows, fresh):
        def step(piece, carry):
            cols = pl.ds(pl.multiple_of(512 + piece * 256, 256), 256)
            total = jnp.zeros((T, 256), F32) if fresh else p_ref[:, cols]
            for d in rows:
                total = total + predict_rows(mod4(x + d), cols)
            p_ref[:, cols] = total
            return carry

        lax.fori_loop(0, 2, step, 0)

    def predict_first(piece, carry):
        cols = pl.ds(pl.multiple_of(piece * 256, 256), 256)
        total = jnp.zeros((T, 256), F32)
        for xx in range(4):
            total = total + predict_rows(xx, cols)
        p_ref[:, cols] = total
        return carry

    inner = [jnp.zeros((T, 128), F32)]
    send_r = []

    def residual(half):
        for piece in (2 * half, 2 * half + 1):
            cols = slice(piece * 256, (piece + 1) * 256)
            target = dot(select, to_ref[:, cols]) * wide(inverse_count, 2)
            prediction = p_ref[:, cols]
            value = (prediction - target).astype(BF16)
            r_ref[:, cols] = value
            product = value.astype(F32) * prediction
            inner[0] = inner[0] + product[:, 0:128] + product[:, 128:256]
        cols = pl.ds(half * 512, 512)
        send_r.append(Send(r_ref.at[:, cols], rsib.at[:, cols], sib))

    for s in gather_w1.sibs[:3]:
        s.wait()
    predict_second((0, 1, -1), True)
    for s in gather_w0.sibs + gather_w1.sibs[3:]:
        s.wait()
    lax.fori_loop(0, 2, predict_first, 0)
    for s in halos:
        s.wait()
    residual(0)
    predict_second((2,), False)
    residual(1)
    inner = inner[0]
    inner = jnp.broadcast_to(jnp.sum(inner, axis=1, keepdims=True), (T, 128))
    in_own[...] = jnp.transpose(inner)[0:8, :]
    inners = [Send(in_own, in_all.at[d], {"tp": lax.rem(z + d, 8)}) for d in range(1, 8)]

    def normed_grad(d):
        zz = lax.rem(z + d, 8)
        w = wbuf[lax.div(zz, 2), pl.ds(lax.rem(zz, 2) * 2, 2)].reshape(448, FEAT)
        ngb[d] = dot_nt(w, r_ref[...]).astype(BF16)

    lo, hi = pl.ds(0, 224), pl.ds(224, 224)

    def z_send(step, sign, rows_):
        d = (4 - step if sign == 1 else 4 + step)
        box = zrp if sign == 1 else zrm
        return Send(ngb.at[d, rows_], box.at[step, rows_], dev_z[sign])

    def z_add(step, sign, rows_):
        d = (3 - step if sign == 1 else 5 + step)
        box = zrp if sign == 1 else zrm
        ngb[d, rows_] = (ngb[d, rows_].astype(F32) + box[step, rows_].astype(F32)).astype(BF16)

    normed_grad(4)
    z0p, z0m = z_send(0, 1, lo), z_send(0, -1, hi)

    send_nt.wait()
    send_r[0].wait()

    def grad_a(d):
        yy = mod4(y + d)
        left = nt_ref[:, yy, c].reshape(448, T)
        left_sib = nsib[:, yy].reshape(448, T)
        block = dot(left, r_ref[:, 0:512]) + dot(left_sib, rsib[:, 0:512])
        block = block.astype(BF16)
        g_ref[0, d] = block[:, 0:256].reshape(4, 112, 256)
        g_ref[1, d] = block[:, 256:512].reshape(4, 112, 256)

    def grad_b(d):
        xx = mod4(x + d)
        left = nt_ref[xx, :, c].reshape(448, T)
        left_sib = nsib[xx].reshape(448, T)
        block = dot(left, r_ref[:, 512:1024]) + dot(left_sib, rsib[:, 512:1024])
        block = block.astype(BF16)
        g_ref[2, d] = block[:, 0:256].reshape(4, 112, 256)
        g_ref[3, d] = block[:, 256:512].reshape(4, 112, 256)

    two, four = pl.ds(0, 2), pl.ds(2, 2)

    class Scatter:
        def __init__(self, n, dev_a, dev_b, b):
            self.g, self.h = g_ref.at[n], h_ref.at[n]
            self.r0 = {1: r0_ref.at[n, 0], -1: r0_ref.at[n, 1]}
            self.r1 = {1: r1_ref.at[n, 0], -1: r1_ref.at[n, 1]}
            self.s0 = {1: s0_ref.at[n, 0], -1: s0_ref.at[n, 1]}
            self.s1 = {1: s1_ref.at[n, 0], -1: s1_ref.at[n, 1]}
            self.dev_a, self.dev_b, self.b = dev_a, dev_b, b
            self.part = {1: two, -1: four}
            self.cols = {1: pl.ds(0, 128), -1: pl.ds(128, 128)}

        def first(self):
            self.e0 = {s: Send(self.g.at[2, self.part[s]], self.r0[s], self.dev_a[s]) for s in (1, -1)}

        def second(self):
            self.e1 = {}
            for s, d in ((1, 1), (-1, 3)):
                part = self.part[-s]
                self.e1[s] = [Send(self.g.at[d, part], self.r1[s].at[part], self.dev_a[s])]

        def third(self):
            for s, d in ((1, 1), (-1, 3)):
                part = self.part[s]
                self.e0[s].wait()
                self.g[d, part] = (self.g[d, part].astype(F32) + self.r0[s][...].astype(F32)).astype(BF16)
                self.e1[s].append(Send(self.g.at[d, part], self.r1[s].at[part], self.dev_a[s]))

        def fourth(self):
            for s in (1, -1):
                for e in self.e1[s]:
                    e.wait()
            self.h[...] = (
                self.g[0].astype(F32) + self.r1[1][...].astype(F32) + self.r1[-1][...].astype(F32)
            ).astype(BF16)
            far = mod4(self.b + 2)
            self.f0, self.f1 = {}, {}
            for s in (1, -1):
                self.f0[s] = Send(self.h.at[far, :, self.cols[s]], self.s0[s], self.dev_b[s])
            for s in (1, -1):
                cols = self.cols[-s]
                self.f1[s] = [Send(self.h.at[mod4(self.b + s), :, cols], self.s1[s].at[:, cols], self.dev_b[s])]

        def fifth(self):
            for s in (1, -1):
                cols, near = self.cols[s], mod4(self.b + s)
                self.f0[s].wait()
                self.h[near, :, cols] = (
                    self.h[near, :, cols].astype(F32) + self.s0[s][...].astype(F32)
                ).astype(BF16)
                self.f1[s].append(Send(self.h.at[near, :, cols], self.s1[s].at[:, cols], self.dev_b[s]))

        def result(self):
            for s in (1, -1):
                for e in self.f1[s]:
                    e.wait()
            return self.h[self.b].astype(F32) + self.s1[1][...].astype(F32) + self.s1[-1][...].astype(F32)

    a0, a1 = Scatter(0, dev_y, dev_x, x), Scatter(1, dev_y, dev_x, x)
    b0, b1 = Scatter(2, dev_x, dev_y, y), Scatter(3, dev_x, dev_y, y)

    def z_half(step, n, plus, minus):
        rows_p, rows_m = (hi, lo)[n], (lo, hi)[n]
        plus[n].wait()
        z_add(step, 1, rows_p)
        out_p = z_send(step + 1, 1, rows_p)
        minus[n].wait()
        z_add(step, -1, rows_m)
        return out_p, z_send(step + 1, -1, rows_m)

    grad_a(2)
    a0.first()
    send_r[1].wait()
    grad_b(2)
    b0.first()
    a1.first()
    b1.first()
    normed_grad(3)
    z1p = [z_send(1, 1, hi)]
    normed_grad(5)
    z1m = [z_send(1, -1, lo)]
    grad_a(1)
    grad_a(3)
    a0.second()
    z0p.wait()
    z_add(0, 1, lo)
    z1p.append(z_send(1, 1, lo))
    z0m.wait()
    z_add(0, -1, hi)
    z1m.append(z_send(1, -1, hi))
    grad_b(1)
    grad_b(3)
    b0.second()
    normed_grad(2)
    normed_grad(6)
    a0.third()
    b0.third()
    a1.second()
    b1.second()
    z2 = [z_half(1, 0, z1p, z1m)]
    a1.third()
    b1.third()
    z2.append(z_half(1, 1, z1p, z1m))
    z2p, z2m = zip(*z2)
    normed_grad(1)
    normed_grad(7)
    grad_a(0)
    grad_b(0)
    normed_grad(0)
    drain(gathered)
    z3 = [z_half(2, 0, z2p, z2m)]
    a0.fourth()
    b0.fourth()
    z3.append(z_half(2, 1, z2p, z2m))
    a0.fifth()
    b0.fifth()
    a1.fourth()
    b1.fourth()
    a1.fifth()
    b1.fifth()
    drain(len(sent) - 32)

    total_inner = in_own[0:1, :]
    for d, e in enumerate(inners):
        e.wait()
        total_inner = total_inner + in_all[d + 1, 0:1, :]
    scale_row = sct_ref[0:1, :]
    factor = total_inner * scale_row * scale_row * (1.0 / WIDE)
    for pair in z3:
        for e in pair:
            e.wait()
    mine = pl.ds(lax.rem(z, 2) * 448, 448)
    ng = ngb[0].astype(F32) + zrp[3].astype(F32) + zrm[3].astype(F32)
    u = ng * wide(gt_ref[mine, :], 2)
    gh_ref[...] = u * scale_row - ht_ref[mine, :].astype(F32) * factor

    for n, part in enumerate((a0, a1, b0, b1)):
        gp_ref[:, n * 256 : (n + 1) * 256] = part.result()
    drain(len(sent))
    assert counter[0] <= EVENTS


def deliver(gp_in, gh_in, gp_out, gh_out, gp, gh, sems):
    into = [pltpu.make_async_copy(gp_in, gp, sems.at[0]), pltpu.make_async_copy(gh_in, gh, sems.at[1])]
    out = [pltpu.make_async_copy(gp, gp_out, sems.at[2]), pltpu.make_async_copy(gh, gh_out, sems.at[3])]
    for copy in into:
        copy.start()
    for first, second in zip(into, out):
        first.wait()
        second.start()
    for copy in out:
        copy.wait()


def vm(shape, dtype=BF16):
    return pltpu.VMEM(shape, dtype)


def body(teacher_query, teacher_key, teacher_value, t_segment, s_hidden, norm_gain, proj_weight, span_start, span_count):
    spec = pl.BlockSpec(memory_space=pltpu.VMEM)
    scratch = [
        vm((T, FEAT)),
        vm((T, WIDE)),
        vm((2, 4, 4, T + 16, 2 * HEAD)),
        vm((4, 4, 2, 112, FEAT)),
        vm((2, 4 * T, 2 * HEAD)),
        vm((2, 4 * T, 128), F32),
        vm((2, 4 * T, 2 * HEAD), F32),
        vm((4 * T, 2 * T)),
        vm((4 * T, 2 * T)),
        vm((512, FEAT)),
        vm((T, WIDE)),
        vm((4, 4, 2, 112, T)),
        vm((4, 4, 112, T)),
        vm((896, T)),
        vm((896, 128), F32),
        vm((T, 128), F32),
        vm((8, T), F32),
        vm((T, FEAT), F32),
        vm((T, FEAT)),
        vm((T, FEAT)),
        vm((8, T), F32),
        vm((8, 8, T), F32),
        vm((8, 448, T)),
        vm((4, 448, T)),
        vm((4, 448, T)),
        vm((4, 4, 4, 112, 256)),
        vm((4, 2, 2, 112, 256)),
        vm((4, 2, 4, 112, 256)),
        vm((4, 4, 112, 256)),
        vm((4, 2, 112, 128)),
        vm((4, 2, 112, 256)),
    ]
    scratch += [pltpu.SemaphoreType.DMA((EVENTS,)), pltpu.SemaphoreType.DMA((EVENTS,)), pltpu.SemaphoreType.DMA((3,))]
    anywhere = pl.BlockSpec(memory_space=pl.ANY)
    grad_proj, grad_hidden = pl.pallas_call(
        kernel,
        out_shape=(jax.ShapeDtypeStruct((112, FEAT), F32), jax.ShapeDtypeStruct((448, T), F32)),
        in_specs=[anywhere, spec, spec, spec, anywhere, spec, anywhere, spec, spec],
        out_specs=(spec, spec),
        scratch_shapes=scratch,
        compiler_params=pltpu.CompilerParams(
            collective_id=0, has_side_effects=True, vmem_limit_bytes=60 * 2**20
        ),
    )(
        teacher_query, teacher_key, teacher_value, t_segment.reshape(1, T), s_hidden,
        norm_gain.reshape(28, 128), proj_weight, span_start.reshape(1, T), span_count.reshape(1, T),
    )
    grad_proj, grad_hidden = pl.pallas_call(
        deliver,
        out_shape=(jax.ShapeDtypeStruct((112, FEAT), F32), jax.ShapeDtypeStruct((448, T), F32)),
        in_specs=[anywhere] * 2,
        out_specs=(anywhere, anywhere),
        scratch_shapes=[vm((112, FEAT), F32), vm((448, T), F32), pltpu.SemaphoreType.DMA((4,))],
        compiler_params=pltpu.CompilerParams(vmem_limit_bytes=60 * 2**20),
    )(grad_proj, grad_hidden)
    return grad_proj, grad_hidden.T


def solution(mesh):
    return jax.shard_map(
        body,
        mesh=mesh,
        in_specs=(
            P("seq", "tp"),
            P("seq", "tp"),
            P("seq", "tp"),
            P("seq"),
            P("seq", None),
            P(),
            P("seq", "tp"),
            P("seq"),
            P("seq"),
        ),
        out_specs=(P("seq", "tp"), P("seq", "tp")),
        check_vma=False,
    )
```

```python
import math

import jax
import jax.numpy as jnp
from jax import lax
from jax.experimental import pallas as pl
from jax.experimental.pallas import tpu as pltpu
from jax.sharding import PartitionSpec as P

MESH = pl.DeviceIdType.MESH
F32, BF16 = jnp.float32, jnp.bfloat16
HEAD = 128
T = 256
WIDE = 3584
FEAT = 1024
BIG = float(2**20)
EXP_SCALE = math.log2(math.e) / math.sqrt(HEAD)
REACH = 12
HALO = 80
EVENTS = 224

NT = (((1,), (1,)), ((), ()))


def dot(a, b):
    return jnp.dot(a, b, preferred_element_type=F32)


def dot_nt(a, b):
    return lax.dot_general(a, b, NT, preferred_element_type=F32)


def kernel(
    q_hbm, k_ref, v_ref, seg_ref, sh_hbm, gain_ref, w_hbm, start_ref, count_ref,
    gp_ref, gh_ref,
    q_ref, sh_ref, kvbuf, wbuf, qa, m_ref, acc_ref, pa_ref, pb_ref, to_ref,
    normed, nt_ref, nsib, ht_ref, gt_ref, sc_ref, sct_ref, p_ref, r_ref, rsib,
    in_own, in_all, ngb, zrp, zrm,
    g_ref, r0_ref, r1_ref, h_ref, s0_ref, s1_ref,
    send_sems, recv_sems, load_sems,
):
    i = lax.axis_index("seq")
    z = lax.axis_index("tp")
    c = lax.rem(i, 2)
    t = lax.div(i, 2)
    y = lax.rem(t, 4)
    x = lax.div(t, 4)
    oc = 1 - c

    def mod4(v):
        return lax.rem(v + 8, 4)

    def seq_dev(xx, yy, cc):
        return {"seq": (xx * 4 + yy) * 2 + cc}

    dev_x = {1: seq_dev(mod4(x + 1), y, c), -1: seq_dev(mod4(x - 1), y, c)}
    dev_y = {1: seq_dev(x, mod4(y + 1), c), -1: seq_dev(x, mod4(y - 1), c)}
    dev_z = {d: {"tp": lax.rem(z + d + 8, 8)} for d in (1, -1)}
    sib = seq_dev(x, y, oc)

    barrier = pltpu.get_barrier_semaphore()
    partners = [dev_x[1], dev_x[-1], dev_y[1], dev_y[-1], sib, {"seq": lax.rem(i + 2 * c + 31, 32)}]
    partners += [{"tp": lax.rem(z + d, 8)} for d in range(1, 8)]
    for device in partners:
        pl.semaphore_signal(barrier, inc=1, device_id=device, device_id_type=MESH)

    loads = [
        pltpu.make_async_copy(sh_hbm, sh_ref, load_sems.at[0]),
        pltpu.make_async_copy(w_hbm, wbuf.at[x, y, c], load_sems.at[1]),
        pltpu.make_async_copy(q_hbm, q_ref, load_sems.at[2]),
    ]
    for load in loads:
        load.start()

    counter = [0]
    sent = []

    class Send:
        def __init__(self, src, dst, device, arrive=None):
            n = counter[0]
            counter[0] += 1
            self.parts = (n, device)
            self.copy = self.make(src, dst)
            self.copy.start()
            sent.append(self.copy)
            self.arrive = dst if arrive is None else arrive

        def make(self, src, dst):
            n, device = self.parts
            return pltpu.make_async_remote_copy(
                src_ref=src, dst_ref=dst, send_sem=send_sems.at[n], recv_sem=recv_sems.at[n],
                device_id=device, device_id_type=MESH,
            )

        def wait(self):
            self.make(self.arrive, self.arrive).wait_recv()

    def drain(count):
        for copy in sent[:count]:
            copy.wait_send()
        del sent[:count]

    class Gather:
        def __init__(self, view, column, a, b, sib_b, dev_a, dev_b):
            self.view, self.column = view, column
            self.a, self.b, self.sib_b, self.dev_a, self.dev_b = a, b, sib_b, dev_a, dev_b
            self.p2, self.f2, self.sibs = {}, {}, []

        def at(self, da, db, part=None):
            return self.view(mod4(self.a + da), mod4(self.b + db), part)

        def to_a(self, sign, da, part=None):
            ref = self.at(da, 0, part)
            return Send(ref, ref, self.dev_a[sign], self.at(da - sign, 0, part))

        def to_b(self, sign, da, db, part=None):
            ref = self.at(da, db, part)
            return Send(ref, ref, self.dev_b[sign], self.at(da, db - sign, part))

        def to_sib(self, db):
            ref = self.column(mod4(self.b + db), c)
            self.sibs.append(Send(ref, ref, sib, self.column(mod4(self.sib_b + db), oc)))

        def stage0(self):
            self.p1 = {s: self.to_a(s, 0) for s in (1, -1)}
            for s in (1, -1):
                self.p2[s, 0] = self.to_b(s, 0, 0)

        def stage1(self):
            self.f1 = {}
            for s, part in ((1, 0), (-1, 1)):
                self.p1[s].wait()
                self.f1[s] = self.to_a(s, -s, part)
                for sb in (1, -1):
                    self.p2[sb, -s] = self.to_b(sb, -s, 0)
            self.forward(0)

        def forward(self, da):
            for s, part in ((1, 0), (-1, 1)):
                self.p2[s, da].wait()
                self.f2[s, da] = self.to_b(s, da, -s, part)

        def stage2(self):
            for s in (1, -1):
                self.f1[s].wait()
            for sb in (1, -1):
                self.p2[sb, 2] = self.to_b(sb, 2, 0)

        def stage2b(self):
            self.forward(-1)
            self.forward(1)

        def stage3(self):
            self.forward(2)

        def stage4(self):
            for key in self.f2:
                self.f2[key].wait()
            self.to_sib(2)

        def stage4_by_shard(self):
            for da in (0, -1, 1, 2):
                for sign in (1, -1):
                    self.f2[sign, da].wait()
                at = mod4(self.a + da), mod4(self.b + 2)
                ref = self.view(*at, None)
                self.sibs.append(Send(ref, ref, sib, self.view(*at, None, oc)))

        def stage5(self):
            for s in self.sibs:
                s.wait()

    def kv_view(aa, bb, part):
        if part is None:
            return kvbuf.at[c, aa, bb]
        return kvbuf.at[c, aa, bb, pl.ds((0, 128)[part], (128, 144)[part])]

    def w_view(first, x_first):
        def view(aa, bb, part, core=c):
            xx, yy = (aa, bb) if x_first else (bb, aa)
            if part is None:
                return wbuf.at[xx, yy, core, :, pl.ds(first, 512)]
            return wbuf.at[xx, yy, core, :, pl.ds(first + 256 * part, 256)]

        return view

    kv_a, kv_b = oc * x + c * y, oc * y + c * x
    step_a = {d: seq_dev(mod4(x + d * oc), mod4(y + d * c), c) for d in (1, -1)}
    step_b = {d: seq_dev(mod4(x + d * c), mod4(y + d * oc), c) for d in (1, -1)}
    gather_kv = Gather(kv_view, lambda bb, cc: kvbuf.at[cc, :, bb], kv_a, kv_b, kv_a, step_a, step_b)
    def share(da, db):
        ref = gather_kv.at(da, db)
        return Send(ref, ref, sib, kvbuf.at[oc, mod4(kv_b + da), mod4(kv_a + db)])

    gather_w0 = Gather(w_view(0, True), lambda bb, cc: wbuf.at[:, bb, cc, :, pl.ds(0, 512)], x, y, y, dev_x, dev_y)
    gather_w1 = Gather(w_view(512, False), lambda bb, cc: wbuf.at[bb, :, cc, :, pl.ds(512, 512)], y, x, x, dev_y, dev_x)

    seg = seg_ref[...]
    below1 = jnp.sum((seg < 1).astype(F32), axis=1, keepdims=True)
    below2 = jnp.sum((seg < 2).astype(F32), axis=1, keepdims=True)
    strip_row = lax.broadcasted_iota(jnp.int32, (16, 128), 0)
    kvbuf[c, kv_a, kv_b, 0:T, 0:HEAD] = k_ref[...]
    kvbuf[c, kv_a, kv_b, 0:T, HEAD : 2 * HEAD] = v_ref[...]
    strip = jnp.where(strip_row < 8, below1, below2).astype(BF16)
    kvbuf[c, kv_a, kv_b, T : T + 16, :] = jnp.concatenate([strip, strip], axis=1)

    pl.semaphore_wait(barrier, len(partners))

    gather_kv.stage0()
    shared = [share(0, 0)]

    loads[0].wait()
    squares = jnp.zeros((T, 128), F32)
    for piece in range(WIDE // 128):
        h = sh_ref[:, piece * 128 : (piece + 1) * 128].astype(F32)
        squares = squares + h * h
    mean = jnp.sum(squares, axis=1, keepdims=True) * (1.0 / WIDE)
    scale = lax.rsqrt(mean + 1e-6)
    scale_wide = jnp.broadcast_to(scale, (T, 128))
    sc_ref[...] = scale_wide
    sct_ref[...] = jnp.transpose(scale_wide)[0:8, :]

    def norm_piece(piece, carry):
        cols = pl.ds(pl.multiple_of(piece * 896, 128), 896)
        h = sh_ref[:, cols]
        gain = jnp.concatenate([gain_ref[pl.ds(piece * 7 + n, 1), :] for n in range(7)], axis=1)
        value = (h.astype(F32) * sc_ref[:, 0:1] * gain).astype(BF16)
        normed[:, cols] = value
        nt_ref[piece] = jnp.transpose(value).reshape(4, 2, 112, T)

        @pl.when(piece == lax.div(z, 2))
        def _():
            ht_ref[...] = jnp.transpose(h)
            gt_ref[...] = jnp.transpose(jnp.broadcast_to(gain, (128, 896)))

        return carry

    lax.fori_loop(0, 1, norm_piece, 0)
    loads[2].wait()

    rows = lax.broadcasted_iota(jnp.int32, (T, 128), 0).astype(F32)
    lanes = lax.broadcasted_iota(jnp.int32, (T, 128), 1).astype(F32)

    def doc_of(n1, n2):
        return jnp.where(rows >= n1, 1.0, 0.0) + jnp.where(rows >= n2, 1.0, 0.0)

    one_hot = jnp.where(doc_of(below1, below2) == lanes, 1.0, 0.0).astype(BF16)
    for h in range(8):
        at = pl.ds((h % 4) * T, T)
        qa[h // 4, at, 0:HEAD] = q_ref[:, h * HEAD : (h + 1) * HEAD]
        qa[h // 4, at, HEAD : 2 * HEAD] = one_hot

    doc_id = lax.broadcasted_iota(jnp.int32, (16, T), 0).astype(F32)
    key_id = lax.broadcasted_iota(jnp.int32, (16, T), 1).astype(F32)

    def blocks(tt):
        xx, yy = lax.div(tt, 4), lax.rem(tt, 4)
        return kvbuf.at[0, xx, yy], kvbuf.at[1, yy, xx]

    def keys_of(tt):
        sides = []
        for block in blocks(tt):
            strip = block[T : T + 16, 0:HEAD].astype(F32)
            doc = jnp.where(key_id >= strip[0:1, 0:1], 1.0, 0.0) + jnp.where(key_id >= strip[8:9, 0:1], 1.0, 0.0)
            bias = jnp.where(doc == doc_id, 0.0, -BIG).astype(BF16)
            rest = jnp.zeros((HEAD - 16, T), BF16)
            sides.append(jnp.concatenate([jnp.transpose(block[0:T, 0:HEAD]), bias, rest], axis=0))
        return jnp.concatenate(sides, axis=1)

    ones = jnp.ones((2 * T, HEAD), BF16)

    def wide(v, n):
        return jnp.concatenate([v] * n, axis=1)

    def values_of(tt):
        v = jnp.concatenate([block[0:T, HEAD : 2 * HEAD] for block in blocks(tt)], axis=0)
        return jnp.concatenate([v, ones], axis=1)

    def soften(group, scores, weights, own):
        factors = []
        for piece in range(8):
            at = slice(piece * 128, (piece + 1) * 128)
            s = scores[at, :]
            if own:
                row = lax.broadcasted_iota(jnp.int32, (128, 2 * T), 0) + (piece % 2) * 128
                col = lax.broadcasted_iota(jnp.int32, (128, 2 * T), 1)
                s = jnp.where(col <= row + c * T, s, -2.0 * BIG)
                m = jnp.broadcast_to(jnp.max(s, axis=1, keepdims=True), (128, 128))
            else:
                m_old = m_ref[group, at, :]
                m = jnp.maximum(m_old, jnp.max(s, axis=1, keepdims=True))
                factors.append(jnp.exp2((m_old - m) * EXP_SCALE))
            weights[at, :] = jnp.exp2(((s - wide(m, 4)) * EXP_SCALE).astype(BF16))
            m_ref[group, at, :] = m
        return factors

    def gather_values(group, weights, values, factors):
        update = dot(weights[...], values)
        if not factors:
            acc_ref[group] = update
            return
        for piece, factor in enumerate(factors):
            at = slice(piece * 128, (piece + 1) * 128)
            acc_ref[group, at, :] = acc_ref[group, at, :] * wide(factor, 2) + update[at, :]

    def attend_chip(tt, own):
        keys, values = keys_of(tt), values_of(tt)
        s_a = dot(qa[0], keys)
        s_b = dot(qa[1], keys)
        factors_a = soften(0, s_a, pa_ref, own)
        gather_values(0, pa_ref, values, factors_a)
        factors_b = soften(1, s_b, pb_ref, own)
        gather_values(1, pb_ref, values, factors_b)

    def near(n):
        n = n + jnp.where(n >= 4, 1, 0)
        return lax.div(n, 3) - 1, lax.rem(n, 3) - 1

    def far(n):
        return jnp.where(n < 4, 2, n - 5), jnp.where(n < 4, n, 2)

    def attend(place, low, high):
        def step(n, carry):
            dx, dy = place(n)
            tt = mod4(x + dx) * 4 + mod4(y + dy)

            @pl.when((tt < t) & (tt >= t - REACH))
            def _():
                attend_chip(tt, False)

            return carry

        lax.fori_loop(low, high, step, 0)

    def finish():
        for h in range(8):
            acc = acc_ref[h // 4, pl.ds((h % 4) * T, T), :]
            out = (acc[:, 0:HEAD] / acc[:, HEAD : 2 * HEAD]).astype(BF16)
            to_ref[128 : 128 + T, h * HEAD : (h + 1) * HEAD] = out
        last = Send(
            to_ref.at[pl.ds(128 + T - HALO, HALO)], to_ref.at[pl.ds(128 - HALO, HALO)],
            {"seq": lax.rem(i + 1, 32)},
        )
        first = Send(
            to_ref.at[pl.ds(128, HALO)], to_ref.at[pl.ds(128 + T, HALO)],
            {"seq": lax.rem(i + 31, 32)},
        )
        return [last, first]

    def column(ref):
        return jnp.transpose(jnp.broadcast_to(ref[...].astype(F32), (128, T)))

    to_ref[0 : 128 - HALO, :] = jnp.zeros((128 - HALO, FEAT), BF16)
    to_ref[128 + T + HALO : 512, :] = jnp.zeros((128 - HALO, FEAT), BF16)
    span_start = column(start_ref)
    span_count = column(count_ref)
    inverse_count = 1.0 / span_count
    first_row = (i * T - 128).astype(F32)
    row_id = lax.broadcasted_iota(jnp.int32, (T, 512), 1).astype(F32) + first_row
    begin, end = wide(span_start, 4), wide(span_start + span_count, 4)
    select = jnp.where((row_id >= begin) & (row_id < end), 1.0, 0.0).astype(BF16)

    gather_kv.stage1()
    near_shared = [share(1, 0), share(-1, 0), share(0, 1), share(0, -1)]
    shared[0].wait()
    attend_chip(t, True)
    gather_kv.stage2()
    far_shared = [share(2, 0)]
    loads[1].wait()
    gather_w0.stage0()
    gather_w1.stage0()
    gather_kv.stage2b()
    near_shared += [share(da, db) for da in (1, -1) for db in (1, -1)]
    lax.fori_loop(1, 4, norm_piece, 0)
    send_nt = Send(nt_ref.at[:, :, oc], nsib, sib)
    gather_kv.stage3()
    far_shared += [share(2, 1), share(2, -1)]
    for s in near_shared:
        s.wait()
    attend(near, 0, 2)
    gather_w0.stage1()
    gather_w1.stage1()
    attend(near, 2, 4)
    gather_kv.stage4()
    attend(near, 4, 7)
    for gather in (gather_w0, gather_w1):
        gather.stage2()
        gather.to_sib(0)
    attend(near, 7, 8)
    for s in far_shared:
        s.wait()
    gather_kv.stage5()
    gather_w0.stage2b()
    gather_w1.stage2b()
    attend(far, 0, 1)
    for gather in (gather_w0, gather_w1):
        gather.stage3()
        gather.to_sib(-1)
        gather.to_sib(1)
    attend(far, 1, 4)
    gather_w0.stage4_by_shard()
    gather_w1.stage4_by_shard()
    attend(far, 4, 7)
    gathered = len(sent)
    halos = finish()

    def predict_rows(xx, cols):
        rows = pl.ds(pl.multiple_of(xx * 896, 128), 896)
        return dot(normed[:, rows], wbuf[xx, :, :, :, cols].reshape(896, 256))

    def predict_second(rows, fresh):
        def step(piece, carry):
            cols = pl.ds(pl.multiple_of(512 + piece * 256, 256), 256)
            total = jnp.zeros((T, 256), F32) if fresh else p_ref[:, cols]
            for d in rows:
                total = total + predict_rows(mod4(x + d), cols)
            p_ref[:, cols] = total
            return carry

        lax.fori_loop(0, 2, step, 0)

    def predict_first(piece, carry):
        cols = pl.ds(pl.multiple_of(piece * 256, 256), 256)
        total = jnp.zeros((T, 256), F32)
        for xx in range(4):
            total = total + predict_rows(xx, cols)
        p_ref[:, cols] = total
        return carry

    inner = [jnp.zeros((T, 128), F32)]
    send_r = []

    def residual(half):
        for piece in (2 * half, 2 * half + 1):
            cols = slice(piece * 256, (piece + 1) * 256)
            target = dot(select, to_ref[:, cols]) * wide(inverse_count, 2)
            prediction = p_ref[:, cols]
            value = (prediction - target).astype(BF16)
            r_ref[:, cols] = value
            product = value.astype(F32) * prediction
            inner[0] = inner[0] + product[:, 0:128] + product[:, 128:256]
        cols = pl.ds(half * 512, 512)
        send_r.append(Send(r_ref.at[:, cols], rsib.at[:, cols], sib))

    for s in gather_w1.sibs[:3]:
        s.wait()
    predict_second((0, 1, -1), True)
    for s in gather_w0.sibs + gather_w1.sibs[3:]:
        s.wait()
    lax.fori_loop(0, 2, predict_first, 0)
    for s in halos:
        s.wait()
    residual(0)
    predict_second((2,), False)
    residual(1)
    inner = inner[0]
    inner = jnp.broadcast_to(jnp.sum(inner, axis=1, keepdims=True), (T, 128))
    in_own[...] = jnp.transpose(inner)[0:8, :]
    inners = [Send(in_own, in_all.at[d], {"tp": lax.rem(z + d, 8)}) for d in range(1, 8)]

    def normed_grad(d):
        zz = lax.rem(z + d, 8)
        w = wbuf[lax.div(zz, 2), pl.ds(lax.rem(zz, 2) * 2, 2)].reshape(448, FEAT)
        ngb[d] = dot_nt(w, r_ref[...]).astype(BF16)

    lo, hi = pl.ds(0, 224), pl.ds(224, 224)

    def z_send(step, sign, rows_):
        d = (4 - step if sign == 1 else 4 + step)
        box = zrp if sign == 1 else zrm
        return Send(ngb.at[d, rows_], box.at[step, rows_], dev_z[sign])

    def z_add(step, sign, rows_):
        d = (3 - step if sign == 1 else 5 + step)
        box = zrp if sign == 1 else zrm
        ngb[d, rows_] = (ngb[d, rows_].astype(F32) + box[step, rows_].astype(F32)).astype(BF16)

    normed_grad(4)
    z0p, z0m = z_send(0, 1, lo), z_send(0, -1, hi)

    send_nt.wait()
    send_r[0].wait()

    def grad_a(d):
        yy = mod4(y + d)
        left = nt_ref[:, yy, c].reshape(448, T)
        left_sib = nsib[:, yy].reshape(448, T)
        block = dot(left, r_ref[:, 0:512]) + dot(left_sib, rsib[:, 0:512])
        block = block.astype(BF16)
        g_ref[0, d] = block[:, 0:256].reshape(4, 112, 256)
        g_ref[1, d] = block[:, 256:512].reshape(4, 112, 256)

    def grad_b(d):
        xx = mod4(x + d)
        left = nt_ref[xx, :, c].reshape(448, T)
        left_sib = nsib[xx].reshape(448, T)
        block = dot(left, r_ref[:, 512:1024]) + dot(left_sib, rsib[:, 512:1024])
        block = block.astype(BF16)
        g_ref[2, d] = block[:, 0:256].reshape(4, 112, 256)
        g_ref[3, d] = block[:, 256:512].reshape(4, 112, 256)

    two, four = pl.ds(0, 2), pl.ds(2, 2)

    class Scatter:
        def __init__(self, n, dev_a, dev_b, b):
            self.g, self.h = g_ref.at[n], h_ref.at[n]
            self.r0 = {1: r0_ref.at[n, 0], -1: r0_ref.at[n, 1]}
            self.r1 = {1: r1_ref.at[n, 0], -1: r1_ref.at[n, 1]}
            self.s0 = {1: s0_ref.at[n, 0], -1: s0_ref.at[n, 1]}
            self.s1 = {1: s1_ref.at[n, 0], -1: s1_ref.at[n, 1]}
            self.dev_a, self.dev_b, self.b = dev_a, dev_b, b
            self.part = {1: two, -1: four}
            self.cols = {1: pl.ds(0, 128), -1: pl.ds(128, 128)}

        def first(self):
            self.e0 = {s: Send(self.g.at[2, self.part[s]], self.r0[s], self.dev_a[s]) for s in (1, -1)}

        def second(self):
            self.e1 = {}
            for s, d in ((1, 1), (-1, 3)):
                part = self.part[-s]
                self.e1[s] = [Send(self.g.at[d, part], self.r1[s].at[part], self.dev_a[s])]

        def third(self):
            for s, d in ((1, 1), (-1, 3)):
                part = self.part[s]
                self.e0[s].wait()
                self.g[d, part] = (self.g[d, part].astype(F32) + self.r0[s][...].astype(F32)).astype(BF16)
                self.e1[s].append(Send(self.g.at[d, part], self.r1[s].at[part], self.dev_a[s]))

        def fourth(self):
            for s in (1, -1):
                for e in self.e1[s]:
                    e.wait()
            self.h[...] = (
                self.g[0].astype(F32) + self.r1[1][...].astype(F32) + self.r1[-1][...].astype(F32)
            ).astype(BF16)
            far = mod4(self.b + 2)
            self.f0, self.f1 = {}, {}
            for s in (1, -1):
                self.f0[s] = Send(self.h.at[far, :, self.cols[s]], self.s0[s], self.dev_b[s])
            for s in (1, -1):
                cols = self.cols[-s]
                self.f1[s] = [Send(self.h.at[mod4(self.b + s), :, cols], self.s1[s].at[:, cols], self.dev_b[s])]

        def fifth(self):
            for s in (1, -1):
                cols, near = self.cols[s], mod4(self.b + s)
                self.f0[s].wait()
                self.h[near, :, cols] = (
                    self.h[near, :, cols].astype(F32) + self.s0[s][...].astype(F32)
                ).astype(BF16)
                self.f1[s].append(Send(self.h.at[near, :, cols], self.s1[s].at[:, cols], self.dev_b[s]))

        def result(self):
            for s in (1, -1):
                for e in self.f1[s]:
                    e.wait()
            return self.h[self.b].astype(F32) + self.s1[1][...].astype(F32) + self.s1[-1][...].astype(F32)

    a0, a1 = Scatter(0, dev_y, dev_x, x), Scatter(1, dev_y, dev_x, x)
    b0, b1 = Scatter(2, dev_x, dev_y, y), Scatter(3, dev_x, dev_y, y)

    def z_half(step, n, plus, minus):
        rows_p, rows_m = (hi, lo)[n], (lo, hi)[n]
        plus[n].wait()
        z_add(step, 1, rows_p)
        out_p = z_send(step + 1, 1, rows_p)
        minus[n].wait()
        z_add(step, -1, rows_m)
        return out_p, z_send(step + 1, -1, rows_m)

    grad_a(2)
    a0.first()
    send_r[1].wait()
    grad_b(2)
    b0.first()
    a1.first()
    b1.first()
    normed_grad(3)
    z1p = [z_send(1, 1, hi)]
    normed_grad(5)
    z1m = [z_send(1, -1, lo)]
    grad_a(1)
    grad_a(3)
    a0.second()
    z0p.wait()
    z_add(0, 1, lo)
    z1p.append(z_send(1, 1, lo))
    z0m.wait()
    z_add(0, -1, hi)
    z1m.append(z_send(1, -1, hi))
    grad_b(1)
    grad_b(3)
    b0.second()
    normed_grad(2)
    normed_grad(6)
    a0.third()
    b0.third()
    a1.second()
    b1.second()
    z2 = [z_half(1, 0, z1p, z1m)]
    a1.third()
    b1.third()
    z2.append(z_half(1, 1, z1p, z1m))
    z2p, z2m = zip(*z2)
    normed_grad(1)
    normed_grad(7)
    grad_a(0)
    grad_b(0)
    normed_grad(0)
    drain(gathered)
    z3 = [z_half(2, 0, z2p, z2m)]
    a0.fourth()
    b0.fourth()
    z3.append(z_half(2, 1, z2p, z2m))
    a0.fifth()
    b0.fifth()
    a1.fourth()
    b1.fourth()
    a1.fifth()
    b1.fifth()
    drain(len(sent) - 32)

    total_inner = in_own[0:1, :]
    for d, e in enumerate(inners):
        e.wait()
        total_inner = total_inner + in_all[d + 1, 0:1, :]
    scale_row = sct_ref[0:1, :]
    factor = total_inner * scale_row * scale_row * (1.0 / WIDE)
    for pair in z3:
        for e in pair:
            e.wait()
    mine = pl.ds(lax.rem(z, 2) * 448, 448)
    ng = ngb[0].astype(F32) + zrp[3].astype(F32) + zrm[3].astype(F32)
    u = ng * wide(gt_ref[mine, :], 2)
    gh_ref[...] = u * scale_row - ht_ref[mine, :].astype(F32) * factor

    for n, part in enumerate((a0, a1, b0, b1)):
        gp_ref[:, n * 256 : (n + 1) * 256] = part.result()
    drain(len(sent))
    assert counter[0] <= EVENTS


def deliver(gp_in, gh_in, gp_out, gh_out, gp, gh, sems):
    into = [pltpu.make_async_copy(gp_in, gp, sems.at[0]), pltpu.make_async_copy(gh_in, gh, sems.at[1])]
    out = [pltpu.make_async_copy(gp, gp_out, sems.at[2]), pltpu.make_async_copy(gh, gh_out, sems.at[3])]
    for copy in into:
        copy.start()
    for first, second in zip(into, out):
        first.wait()
        second.start()
    for copy in out:
        copy.wait()


def vm(shape, dtype=BF16):
    return pltpu.VMEM(shape, dtype)


def body(teacher_query, teacher_key, teacher_value, t_segment, s_hidden, norm_gain, proj_weight, span_start, span_count):
    spec = pl.BlockSpec(memory_space=pltpu.VMEM)
    scratch = [
        vm((T, FEAT)),
        vm((T, WIDE)),
        vm((2, 4, 4, T + 16, 2 * HEAD)),
        vm((4, 4, 2, 112, FEAT)),
        vm((2, 4 * T, 2 * HEAD)),
        vm((2, 4 * T, 128), F32),
        vm((2, 4 * T, 2 * HEAD), F32),
        vm((4 * T, 2 * T)),
        vm((4 * T, 2 * T)),
        vm((512, FEAT)),
        vm((T, WIDE)),
        vm((4, 4, 2, 112, T)),
        vm((4, 4, 112, T)),
        vm((896, T)),
        vm((896, 128), F32),
        vm((T, 128), F32),
        vm((8, T), F32),
        vm((T, FEAT), F32),
        vm((T, FEAT)),
        vm((T, FEAT)),
        vm((8, T), F32),
        vm((8, 8, T), F32),
        vm((8, 448, T)),
        vm((4, 448, T)),
        vm((4, 448, T)),
        vm((4, 4, 4, 112, 256)),
        vm((4, 2, 2, 112, 256)),
        vm((4, 2, 4, 112, 256)),
        vm((4, 4, 112, 256)),
        vm((4, 2, 112, 128)),
        vm((4, 2, 112, 256)),
    ]
    scratch += [pltpu.SemaphoreType.DMA((EVENTS,)), pltpu.SemaphoreType.DMA((EVENTS,)), pltpu.SemaphoreType.DMA((3,))]
    anywhere = pl.BlockSpec(memory_space=pl.ANY)
    grad_proj, grad_hidden = pl.pallas_call(
        kernel,
        out_shape=(jax.ShapeDtypeStruct((112, FEAT), F32), jax.ShapeDtypeStruct((448, T), F32)),
        in_specs=[anywhere, spec, spec, spec, anywhere, spec, anywhere, spec, spec],
        out_specs=(spec, spec),
        scratch_shapes=scratch,
        compiler_params=pltpu.CompilerParams(
            collective_id=0, has_side_effects=True, vmem_limit_bytes=60 * 2**20
        ),
    )(
        teacher_query, teacher_key, teacher_value, t_segment.reshape(1, T), s_hidden,
        norm_gain.reshape(28, 128), proj_weight, span_start.reshape(1, T), span_count.reshape(1, T),
    )
    grad_proj, grad_hidden = pl.pallas_call(
        deliver,
        out_shape=(jax.ShapeDtypeStruct((112, FEAT), F32), jax.ShapeDtypeStruct((448, T), F32)),
        in_specs=[anywhere] * 2,
        out_specs=(anywhere, anywhere),
        scratch_shapes=[vm((112, FEAT), F32), vm((448, T), F32), pltpu.SemaphoreType.DMA((4,))],
        compiler_params=pltpu.CompilerParams(vmem_limit_bytes=60 * 2**20),
    )(grad_proj, grad_hidden)
    return grad_proj, grad_hidden.T


def solution(mesh):
    return jax.shard_map(
        body,
        mesh=mesh,
        in_specs=(
            P("seq", "tp"),
            P("seq", "tp"),
            P("seq", "tp"),
            P("seq"),
            P("seq", None),
            P(),
            P("seq", "tp"),
            P("seq"),
            P("seq"),
        ),
        out_specs=(P("seq", "tp"), P("seq", "tp")),
        check_vma=False,
    )
```
